32 devices in a mesh: dp: 16 (over z, y, x), head: 2 (over core).
Axes of the slice: x: 2, y: 2, z: 4, core: 2. Of those that a mesh axis runs over, the one named last changes fastest.
Arguments:
- tokens: bfloat16 [288, 198, 384], P(('dp', 'head')), may hold values from -6 to 6
- cotangent: bfloat16 [288, 198, 384], P(('dp', 'head')), may hold values from -6 to 6
- keep_mask: int32 [288, 198], P(('dp', 'head')), may hold values from 0 to 1, as said below
- source: int32 [288], P(('dp', 'head')), may hold values from 0 to 95, as said below
- qkv_master: float32 [384, 1152], P('dp'), may hold values from -0.3125 to 0.3125
- proj_master: float32 [384, 384], P('dp'), may hold values from -1.25 to 1.25
- fc1_master: float32 [384, 1536], P('dp'), may hold values from -0.3125 to 0.3125
- fc2_master: float32 [1536, 384], P('dp'), may hold values from -0.15625 to 0.15625
- vec_master: float32 [12, 384], P(None, 'dp'), may hold values from -1.2 to 1.4, as said below
- qkv_first: float32 [384, 1152], P('dp'), may hold values from -160 to 160
- proj_first: float32 [384, 384], P('dp'), may hold values from -24 to 24
- fc1_first: float32 [384, 1536], P('dp'), may hold values from -40 to 40
- fc2_first: float32 [1536, 384], P('dp'), may hold values from -80 to 80
- vec_first: float32 [12, 384], P(None, 'dp'), may hold values from -160 to 160
- qkv_second: float32 [384, 1152], P('dp'), may hold values from 28.512 to 456.192
- proj_second: float32 [384, 384], P('dp'), may hold values from 0.6443712 to 10.26432
- fc1_second: float32 [384, 1536], P('dp'), may hold values from 1.7848512 to 28.512
- fc2_second: float32 [1536, 384], P('dp'), may hold values from 7.128 to 114.048
- vec_second: float32 [12, 384], P(None, 'dp'), may hold values from 28.512 to 456.192
Outputs:
- layer_out: bfloat16 [288, 198, 384], P(('dp', 'head'))
- input_grad: float32 [288, 198, 384], P(('dp', 'head'))
- qkv_first_new: float32 [384, 1152], P('dp')
- qkv_second_new: float32 [384, 1152], P('dp')
- qkv_new: float32 [384, 1152], P('dp')
- proj_first_new: float32 [384, 384], P('dp')
- proj_second_new: float32 [384, 384], P('dp')
- proj_new: float32 [384, 384], P('dp')
- fc1_first_new: float32 [384, 1536], P('dp')
- fc1_second_new: float32 [384, 1536], P('dp')
- fc1_new: float32 [384, 1536], P('dp')
- fc2_first_new: float32 [1536, 384], P('dp')
- fc2_second_new: float32 [1536, 384], P('dp')
- fc2_new: float32 [1536, 384], P('dp')
- vec_first_new: float32 [12, 384], P(None, 'dp')
- vec_second_new: float32 [12, 384], P(None, 'dp')
- vec_new: float32 [12, 384], P(None, 'dp')
The draws below stay inside these ranges and needn't reach their ends.
Inputs may be any that keep to these rules, and one draw needn't show every extreme that they name: `keep_mask`: 1 keeps a token; tokens 0 and 1 of every image (class and distillation tokens) are always kept. Every source number names exactly three images, and these stand on three different indices of dp. `vec_master`: rows 0 and 5 lie between 0.6 and 1.4.
All inputs are finite; a program needn't handle non-finite values.
Results may differ from the reference program's by a relative error of at most 0.012.
The reference program's roundings to bfloat16 on the way count: a program that leaves them out, or rounds other values in their place, can miss the bound.
Values may be sent and summed in bfloat16 or wider, within the bound.
A program may use at most 128 MiB of HBM per device.

```python
import math
import jax
import jax.numpy as jnp
from jax import lax

D = 384
HEADS = 6
HEAD_DIM = 64
FF = 1536
SEQ = 198
IMG_DEV = 18
STEP = 10
IMAGES = 288
SOURCES = 96


def draw_keep_mask(key, part):
    key = jax.random.fold_in(key, 11)
    level_key, roll_key = jax.random.split(key, 2)
    image_index = jnp.arange(IMAGES, dtype=jnp.int32)
    base_rate = 250 + 500 * image_index // max(IMAGES - 1, 1)
    level_pick = jax.random.randint(level_key, (IMAGES,), 0, 3)
    factor_table = jnp.array([2, 3, 4], dtype=jnp.int32)
    image_rate = base_rate * factor_table[level_pick] // 2
    place_index = jnp.arange(SEQ, dtype=jnp.int32)
    position_lift = 100 + 1100 * place_index // (SEQ - 1)
    threshold = jnp.minimum(image_rate[:, None] * position_lift[None, :] // 1000, 950)
    rolled = jax.random.randint(roll_key, (IMAGES, SEQ), 0, 1000)
    kept_flags = (rolled < threshold).astype(jnp.int32)
    return jnp.where(place_index[None, :] < 2, 1, kept_flags).astype(jnp.int32)


def draw_source(key, part):
    key = jax.random.fold_in(key, 12)
    perm_key, first_key, second_key = jax.random.split(key, 3)
    shuffled = jax.random.permutation(perm_key, SOURCES).astype(jnp.int32)
    slot_index = jnp.arange(IMAGES, dtype=jnp.int32)
    group_size = IMG_DEV // 3
    device_count = IMAGES // IMG_DEV
    device_index = slot_index // IMG_DEV
    local_index = slot_index % IMG_DEV
    copy_index = local_index % 3
    position = device_index * group_size + local_index // 3
    first_shift = jax.random.randint(first_key, (), 1, device_count).astype(jnp.int32)
    second_pick = jax.random.randint(second_key, (), 1, device_count - 1).astype(jnp.int32)
    second_shift = second_pick + (second_pick >= first_shift).astype(jnp.int32)
    shifts = jnp.stack([jnp.zeros((), jnp.int32), first_shift, second_shift]).astype(jnp.int32)
    offset = shifts[copy_index] * group_size
    return shuffled[(position + offset) % SOURCES].astype(jnp.int32)


def draw_vec_master(key, part):
    key = jax.random.fold_in(key, 13)
    gain_key, bias_key = jax.random.split(key, 2)
    gains = jax.random.uniform(gain_key, (12, D), jnp.float32, 0.6, 1.4)
    biases = jnp.clip(0.3 * jax.random.normal(bias_key, (12, D), jnp.float32), -1.2, 1.2)
    row_index = jnp.arange(12)[:, None]
    return jnp.where((row_index == 0) | (row_index == 5), gains, biases).astype(jnp.float32)


def block_levels(rng, extent, shards, low, high):
    loudness, own = 1.0, jax.random.fold_in(rng, 6)
    for dim, blocks in shards:
        heights = jnp.exp(jax.random.uniform(jax.random.fold_in(own, dim), (blocks,), jnp.float32, low / len(shards), high / len(shards)))
        loudness = loudness * jnp.repeat(heights, extent[dim] // blocks).reshape([-1 if axis == dim else 1 for axis in range(len(extent))])
    return loudness


def normal_values(key, shape, width, limit, cuts=(), kind=jnp.bfloat16):
    factor_of = block_levels(key, shape, cuts, -0.22, 0.18) if cuts else 1.0
    entries = jax.random.normal(key, shape, jnp.float32) * width * factor_of
    return jnp.minimum(jnp.maximum(entries, -limit), limit).astype(kind)


def setup_inputs(seed: int = 0) -> dict:
    arg_keys = jax.random.split(jax.random.key(seed), 20)
    return {
        "tokens": normal_values(arg_keys[0], (IMAGES, SEQ, D), 1.0, 6.0, ((0, 32),)),
        "cotangent": normal_values(arg_keys[1], (IMAGES, SEQ, D), 1.0, 6.0, ((0, 32),)),
        "keep_mask": draw_keep_mask(jax.random.fold_in(arg_keys[19], 71), 0),
        "source": draw_source(jax.random.fold_in(arg_keys[19], 71), 0),
        "qkv_master": normal_values(arg_keys[4], (D, 3 * D), D ** -0.5, 0.3125, ((0, 16),), jnp.float32),
        "proj_master": normal_values(arg_keys[5], (D, D), (D // 16) ** -0.5, 1.25, ((0, 16),), jnp.float32),
        "fc1_master": normal_values(arg_keys[6], (D, FF), D ** -0.5, 0.3125, ((0, 16),), jnp.float32),
        "fc2_master": normal_values(arg_keys[7], (FF, D), FF ** -0.5, 0.15625, ((0, 16),), jnp.float32),
        "vec_master": draw_vec_master(jax.random.fold_in(arg_keys[19], 71), 0),
        "qkv_first": normal_values(arg_keys[9], (D, 3 * D), (0.11 * (IMAGES * SEQ) ** 0.5), 160.0, ((0, 16),), jnp.float32),
        "proj_first": normal_values(arg_keys[10], (D, D), (0.0165 * (IMAGES * SEQ) ** 0.5), 24.0, ((0, 16),), jnp.float32),
        "fc1_first": normal_values(arg_keys[11], (D, FF), (0.0275 * (IMAGES * SEQ) ** 0.5), 40.0, ((0, 16),), jnp.float32),
        "fc2_first": normal_values(arg_keys[12], (FF, D), (0.055 * (IMAGES * SEQ) ** 0.5), 80.0, ((0, 16),), jnp.float32),
        "vec_first": normal_values(arg_keys[13], (12, D), (0.11 * (IMAGES * SEQ) ** 0.5), 160.0, ((1, 16),), jnp.float32),
        "qkv_second": jnp.clip(jnp.exp(math.log(456.192) - 2.7725887 * jax.random.uniform(arg_keys[14], (D, 3 * D), jnp.float32) ** block_levels(arg_keys[14], (D, 3 * D), ((0, 16),), -0.2, 0.2)), 28.512, 456.192),
        "proj_second": jnp.clip(jnp.exp(math.log(10.26432) - 2.7681541 * jax.random.uniform(arg_keys[15], (D, D), jnp.float32) ** block_levels(arg_keys[15], (D, D), ((0, 16),), -0.2, 0.2)), 0.6443712, 10.26432),
        "fc1_second": jnp.clip(jnp.exp(math.log(28.512) - 2.77099 * jax.random.uniform(arg_keys[16], (D, FF), jnp.float32) ** block_levels(arg_keys[16], (D, FF), ((0, 16),), -0.2, 0.2)), 1.7848512, 28.512),
        "fc2_second": jnp.clip(jnp.exp(math.log(114.048) - 2.7725887 * jax.random.uniform(arg_keys[17], (FF, D), jnp.float32) ** block_levels(arg_keys[17], (FF, D), ((0, 16),), -0.2, 0.2)), 7.128, 114.048),
        "vec_second": jnp.clip(jnp.exp(math.log(456.192) - 2.7725887 * jax.random.uniform(arg_keys[18], (12, D), jnp.float32) ** block_levels(arg_keys[18], (12, D), ((1, 16),), -0.2, 0.2)), 28.512, 456.192),
    }


@jax.custom_vjp
def low(v):
    return lax.optimization_barrier(v.astype(jnp.bfloat16)).astype(jnp.float32)

@jax.custom_vjp
def low_back(v):
    return v

def low_keep(v):
    return (low(v), None)

def low_pass(kept, grad):
    return (grad,)

def back_keep(v):
    return (v, None)

def back_low(kept, grad):
    return (low(grad),)
low.defvjp(low_keep, low_pass)
low_back.defvjp(back_keep, back_low)
norm_eps = 1e-06
step_rates = (0.1, 0.4, 0.1, 0.05, 0.5)
decays = (0.05, 0.05, 0.05, 0.05, 0.0)

def layer_norm(values, gain_row, shift_row):
    average = lax.optimization_barrier(jnp.mean(values, -1, keepdims=True))
    centred = values - average
    variance = lax.optimization_barrier(jnp.mean(centred * centred, -1, keepdims=True))
    return centred * lax.rsqrt(variance + norm_eps) * gain_row + shift_row

def matmul(left, right):
    return jnp.einsum('...k,kn->...n', left, right, precision=lax.Precision.HIGHEST)

def forward(params, inputs, live_mask):
    w_qkv, w_proj, w_fc1, w_fc2, vectors = [low(weight_item) for weight_item in params]
    images, length, features = inputs.shape
    normed = low(layer_norm(inputs, vectors[0], vectors[1]))
    qkv_bias = jnp.concatenate([vectors[2], jnp.zeros_like(vectors[2]), vectors[3]])
    projected = low(low_back(matmul(normed, w_qkv) + qkv_bias)).reshape(images, length, 3, HEADS, HEAD_DIM)
    query_rows = projected[:, :, 0]
    key_rows = projected[:, :, 1]
    value_rows = projected[:, :, 2]
    scores = jnp.einsum('ishd,ithd->ihst', query_rows, key_rows, precision=lax.Precision.HIGHEST) * HEAD_DIM ** (-0.5)
    scores = low_back(scores)
    scores = jnp.where(live_mask[:, None, None, :] > 0, scores, -1000000000.0)
    row_max = lax.optimization_barrier(jnp.max(scores, -1, keepdims=True))
    exponent = jnp.exp(scores - row_max)
    probs = low(exponent / lax.optimization_barrier(jnp.sum(exponent, -1, keepdims=True)))
    attended = jnp.einsum('ihst,ithd->ishd', probs, value_rows, precision=lax.Precision.HIGHEST)
    attended = low(low_back(attended.reshape(images, length, features)))
    middle = inputs + low_back(matmul(attended, w_proj) + vectors[4])
    normed_mid = low(layer_norm(middle, vectors[5], vectors[6]))
    hidden = low_back(matmul(normed_mid, w_fc1) + vectors[8:].reshape(-1))
    active = low(jax.nn.gelu(hidden, approximate=False))
    return middle + low_back(matmul(active, w_fc2) + vectors[7])

def adamw(master, first, second, gradient, step_rate, weight_decay):
    first_new = 0.9 * first + 0.1 * gradient
    second_new = 0.999 * second + 0.001 * gradient * gradient
    step_size = first_new / (1.0 - 0.9 ** STEP) / (jnp.sqrt(second_new / (1.0 - 0.999 ** STEP)) + 1e-08)
    return (first_new, second_new, master - step_rate * (step_size + weight_decay * master))

def reference(tokens, cotangent, keep_mask, source, qkv_master, proj_master, fc1_master, fc2_master, vec_master, qkv_first, proj_first, fc1_first, fc2_first, vec_first, qkv_second, proj_second, fc1_second, fc2_second, vec_second):
    params = (qkv_master, proj_master, fc1_master, fc2_master, vec_master)
    live_mask = keep_mask.astype(jnp.float32)
    kept_rows = lax.optimization_barrier(jnp.sum(live_mask, 1))
    totals = jnp.zeros((SOURCES,), jnp.float32).at[source].add(kept_rows)
    token_weight = live_mask * (SEQ / totals[source])[:, None]
    blocks = IMAGES // IMG_DEV
    inputs_all = tokens.astype(jnp.float32).reshape(blocks, IMG_DEV, SEQ, D)
    cot_all = (cotangent.astype(jnp.float32) * token_weight[:, :, None]).reshape(blocks, IMG_DEV, SEQ, D)
    mask_all = live_mask.reshape(blocks, IMG_DEV, SEQ)

    def one_block(running, pieces):
        inputs, block_mask, block_cot = pieces
        outputs, pull_back = jax.vjp(lambda weights, values: forward(weights, values, block_mask), params, inputs)
        weight_grads, block_grad = pull_back(block_cot)
        running = jax.tree.map(jnp.add, running, weight_grads)
        return (running, (outputs.astype(jnp.bfloat16), block_grad))
    zero_grads = tuple((jnp.zeros_like(weight_item) for weight_item in params))
    gradients, (outputs_all, grads_all) = lax.scan(one_block, zero_grads, (inputs_all, mask_all, cot_all))
    layer_out = outputs_all.reshape(IMAGES, SEQ, D)
    input_grad = grads_all.reshape(IMAGES, SEQ, D)
    qkv_state = adamw(qkv_master, qkv_first, qkv_second, gradients[0], step_rates[0], decays[0])
    proj_state = adamw(proj_master, proj_first, proj_second, gradients[1], step_rates[1], decays[1])
    fc1_state = adamw(fc1_master, fc1_first, fc1_second, gradients[2], step_rates[2], decays[2])
    fc2_state = adamw(fc2_master, fc2_first, fc2_second, gradients[3], step_rates[3], decays[3])
    vec_state = adamw(vec_master, vec_first, vec_second, gradients[4], step_rates[4], decays[4])
    return (layer_out, input_grad, qkv_state[0], qkv_state[1], qkv_state[2], proj_state[0], proj_state[1], proj_state[2], fc1_state[0], fc1_state[1], fc1_state[2], fc2_state[0], fc2_state[1], fc2_state[2], vec_state[0], vec_state[1], vec_state[2])
```

```python
import functools

import jax
import jax.numpy as jnp
from jax import lax
from jax.experimental import pallas as pl
from jax.experimental.pallas import tpu as pltpu
from jax.sharding import PartitionSpec as P

HEADS = 6
HEAD_DIM = 64
STEP = 10
PAIRS = HEADS // 2
SCALE = HEAD_DIM ** (-0.5)

norm_eps = 1e-06
step_rates = (0.1, 0.4, 0.1, 0.05, 0.5)
decays = (0.05, 0.05, 0.05, 0.05, 0.0)

F32 = jnp.float32
BF16 = jnp.bfloat16


def dot(left, right):
    return lax.dot_general(left, right, (((1,), (0,)), ((), ())), preferred_element_type=F32)


def across(left, right):
    return lax.dot_general(left, right, (((0,), (0,)), ((), ())), preferred_element_type=F32)


def against(left, right):
    return lax.dot_general(left, right, (((1,), (1,)), ((), ())), preferred_element_type=F32)


def normalise(values):
    average = jnp.mean(values, -1, keepdims=True)
    centred = values - average
    variance = jnp.mean(centred * centred, -1, keepdims=True)
    inverse = lax.rsqrt(variance + norm_eps)
    return centred * inverse, inverse


def norm_back(grad, unit, inverse, gain_row):
    scaled = grad * gain_row
    first = jnp.mean(scaled, -1, keepdims=True)
    second = jnp.mean(scaled * unit, -1, keepdims=True)
    return inverse * (scaled - first - unit * second)


def fold(values):
    rows, cols = values.shape
    return jnp.sum(values.reshape(rows // 8, 8, cols), 0)


ERF_A = (0.254829592, -0.284496736, 1.421413741, -1.453152027, 1.061405429)
ERF_C = 0.3275911 * 0.7071067811865476
LOG2E_HALF = 0.7213475204444817
INV_SQRT_2PI = 0.3989422804014327


def gelu_parts(x):
    bell = jnp.exp2(x * x * (-LOG2E_HALF))
    t = 1.0 / (1.0 + ERF_C * jnp.abs(x))
    a1, a2, a3, a4, a5 = (0.5 * a for a in ERF_A)
    tail = ((((a5 * t + a4) * t + a3) * t + a2) * t + a1) * t * bell
    cdf = jnp.where(x >= 0, 1.0 - tail, tail)
    return x * cdf, cdf + x * (bell * INV_SQRT_2PI)


def layer_kernel(
    tok_ref, cot_ref, keep_ref, tw_ref, wq_ref, wp_ref, w1_ref, w2_ref, vec_ref,
    out_ref, gin_ref, gq_ref, gp_ref, g1_ref, g2_ref, gvec_ref,
    xs, normed, qkv, probs, att, middle, nmid, act, gel, gol, gms, gml, twc, sums,
    stages=99,
):
    images, length, feat = tok_ref.shape
    padded = xs.shape[1]
    hidden_units = w1_ref.shape[1] // feat
    lane = lax.broadcasted_iota(jnp.int32, (padded, 128), 1)
    low_half = lane < HEAD_DIM

    def each_image(body):
        lax.fori_loop(0, images, lambda i, c: (body(i), c)[1], 0)

    def row(n):
        return vec_ref[n : n + 1, :]

    def stacked_halves(values):
        zero = jnp.zeros_like(values)
        return jnp.concatenate(
            [jnp.where(low_half, values, zero), jnp.where(low_half, zero, values)], 0
        )

    def merged_halves(values):
        return jnp.where(low_half, values[:padded], values[padded:])

    tail = padded - 16
    xs[:, tail:, :] = jnp.zeros((images, 16, feat), BF16)
    gol[:, tail:, :] = jnp.zeros((images, 16, feat), BF16)
    sums[...] = jnp.zeros_like(sums)

    eye = lax.broadcasted_iota(jnp.int32, (padded, padded), 0) == lax.broadcasted_iota(
        jnp.int32, (padded, padded), 1
    )

    def first_norm(i):
        xs[i, 0:length, :] = tok_ref[i]
        unit, _ = normalise(xs[i].astype(F32))
        normed[i] = (unit * row(0) + row(1)).astype(BF16)
        weight_row = tw_ref[pl.ds(i, 1), :]
        column = jnp.sum(jnp.where(eye, weight_row, 0.0), 1, keepdims=True)
        twc[i] = jnp.broadcast_to(column, (padded, 128))
        wide = jnp.concatenate([twc[i]] * (feat // 128), 1)[:length]
        gol[i, 0:length, :] = (cot_ref[i].astype(F32) * wide).astype(BF16)

    each_image(first_norm)
    if stages <= 1:
        return

    def project(i):
        values = normed[i]
        for h in range(PAIRS):
            part = pl.ds(128 * h, 128)
            bias = jnp.concatenate(
                [vec_ref[2:3, part], jnp.zeros((1, 128), F32), vec_ref[3:4, part]], 1
            )
            qkv[h, i] = (dot(values, wq_ref[h]) + bias).astype(BF16)

    each_image(project)
    if stages <= 2:
        return

    def attend(i):
        alive = keep_ref[pl.ds(i, 1), :] > 0
        for h in range(PAIRS):
            query = stacked_halves(qkv[h, i, :, 0:128] * BF16(SCALE))
            scores = against(query, qkv[h, i, :, 128:256])
            scores = jnp.where(alive, scores, -1e9)
            top = jnp.max(scores, -1, keepdims=True)
            raised = jnp.exp(scores - top)
            share = raised * (1.0 / jnp.sum(raised, -1, keepdims=True))
            share = share.astype(BF16)
            probs[h, i] = share
            att[i, :, 128 * h : 128 * h + 128] = merged_halves(
                dot(share, qkv[h, i, :, 256:384])
            ).astype(BF16)

    each_image(attend)
    if stages <= 3:
        return

    def second_norm(i):
        mid = xs[i].astype(F32) + (dot(att[i], wp_ref[...]) + row(4))
        middle[i] = mid
        unit, _ = normalise(mid)
        nmid[i] = (unit * row(5) + row(6)).astype(BF16)

    each_image(second_norm)
    if stages <= 4:
        return

    def expand(i):
        values = nmid[i]
        for j in range(hidden_units):
            cols = slice(feat * j, feat * j + feat)
            pre = dot(values, w1_ref[:, cols]) + row(8 + j)
            active, slope = gelu_parts(pre)
            act[i, :, cols] = active.astype(BF16)
            gel[i, :, cols] = slope.astype(BF16)

    each_image(expand)
    if stages <= 5:
        return

    def contract(i):
        total = middle[i] + (dot(act[i], w2_ref[...]) + row(7))
        out_ref[i] = total[:length].astype(BF16)

    each_image(contract)
    if stages <= 6:
        return

    def hidden_back(i):
        grad = gol[i]
        sums[7] += fold(grad.astype(F32))
        for j in range(hidden_units):
            cols = slice(feat * j, feat * j + feat)
            back = against(grad, w2_ref[cols, :]) * gel[i, :, cols].astype(F32)
            back = back.astype(BF16)
            gel[i, :, cols] = back
            sums[8 + j] += fold(back.astype(F32))

    each_image(hidden_back)
    if stages <= 7:
        return

    g2_ref[...] = jnp.zeros_like(g2_ref)

    def fc2_grad(i):
        for j in range(hidden_units):
            cols = slice(feat * j, feat * j + feat)
            g2_ref[cols, :] += across(act[i, :, cols], gol[i])

    each_image(fc2_grad)
    if stages <= 8:
        return

    def middle_back(i):
        unit, inverse = normalise(middle[i])
        grad = against(gel[i], w1_ref[...])
        sums[5] += fold(grad * unit)
        sums[6] += fold(grad)
        back = norm_back(grad, unit, inverse, row(5))
        wide = jnp.concatenate([twc[i]] * (feat // 128), 1)[:length]
        gms[i] = back
        gms[i, 0:length, :] += cot_ref[i].astype(F32) * wide
        low = gms[i].astype(BF16)
        gml[i] = low
        sums[4] += fold(low.astype(F32))

    each_image(middle_back)
    if stages <= 9:
        return

    g1_ref[...] = jnp.zeros_like(g1_ref)
    gp_ref[...] = jnp.zeros_like(gp_ref)

    def fc1_grad(i):
        for j in range(hidden_units):
            cols = slice(feat * j, feat * j + feat)
            g1_ref[:, cols] += across(nmid[i], gel[i, :, cols])
        gp_ref[...] += across(att[i], gml[i])

    each_image(fc1_grad)
    if stages <= 10:
        return

    def attend_back(i):
        grad_att = against(gml[i], wp_ref[...]).astype(BF16)
        for h in range(PAIRS):
            grad = stacked_halves(grad_att[:, 128 * h : 128 * h + 128])
            key = qkv[h, i, :, 128:256]
            query = stacked_halves(qkv[h, i, :, 0:128] * BF16(SCALE))
            share_low = probs[h, i]
            share = share_low.astype(F32)
            grad_share = against(grad, qkv[h, i, :, 256:384])
            inner = jnp.sum(share * grad_share, -1, keepdims=True)
            grad_score = (share * (grad_share - inner)).astype(BF16)
            grad_query = (merged_halves(dot(grad_score, key)) * SCALE).astype(BF16)
            grad_key = across(grad_score, query).astype(BF16)
            grad_value = across(share_low, grad).astype(BF16)
            qkv[h, i, :, 0:128] = grad_query
            qkv[h, i, :, 128:256] = grad_key
            qkv[h, i, :, 256:384] = grad_value
            part = slice(128 * h, 128 * h + 128)
            sums[2, :, part] += fold(grad_query.astype(F32))
            sums[3, :, part] += fold(grad_value.astype(F32))

    each_image(attend_back)
    if stages <= 11:
        return

    gq_ref[...] = jnp.zeros_like(gq_ref)

    def qkv_grad(i):
        for h in range(PAIRS):
            gq_ref[h] += across(normed[i], qkv[h, i])

    each_image(qkv_grad)
    if stages <= 12:
        return

    def input_back(i):
        unit, inverse = normalise(xs[i].astype(F32))
        grad = against(qkv[0, i], wq_ref[0])
        for h in range(1, PAIRS):
            grad = grad + against(qkv[h, i], wq_ref[h])
        sums[0] += fold(grad * unit)
        sums[1] += fold(grad)
        total = gms[i] + norm_back(grad, unit, inverse, row(0))
        gin_ref[i] = total[:length]

    each_image(input_back)
    for n in range(12):
        gvec_ref[n : n + 1, :] = jnp.sum(sums[n], 0, keepdims=True)


def run_layer(tokens, cotangent, keep, weight, wq, wp, w1, w2, vec, stages=99):
    images, length, feat = tokens.shape
    padded = -(-length // 16) * 16
    hidden = w1.shape[1]
    vmem = pl.BlockSpec(memory_space=pltpu.VMEM)
    shape = jax.ShapeDtypeStruct
    keep = jnp.pad(keep.astype(F32), ((0, 0), (0, padded - length)))
    weight = jnp.pad(weight, ((0, 0), (0, padded - length)))
    return pl.pallas_call(
        functools.partial(layer_kernel, stages=stages),
        out_shape=(
            shape((images, length, feat), BF16),
            shape((images, length, feat), F32),
            shape(wq.shape, F32),
            shape(wp.shape, F32),
            shape(w1.shape, F32),
            shape(w2.shape, F32),
            shape(vec.shape, F32),
        ),
        in_specs=[vmem] * 9,
        out_specs=[vmem] * 7,
        scratch_shapes=[
            pltpu.VMEM((images, padded, feat), BF16),
            pltpu.VMEM((images, padded, feat), BF16),
            pltpu.VMEM((PAIRS, images, padded, feat), BF16),
            pltpu.VMEM((PAIRS, images, 2 * padded, padded), BF16),
            pltpu.VMEM((images, padded, feat), BF16),
            pltpu.VMEM((images, padded, feat), F32),
            pltpu.VMEM((images, padded, feat), BF16),
            pltpu.VMEM((images, padded, hidden), BF16),
            pltpu.VMEM((images, padded, hidden), BF16),
            pltpu.VMEM((images, padded, feat), BF16),
            pltpu.VMEM((images, padded, feat), F32),
            pltpu.VMEM((images, padded, feat), BF16),
            pltpu.VMEM((images, padded, 128), F32),
            pltpu.VMEM((12, 8, feat), F32),
        ],
        compiler_params=pltpu.CompilerParams(vmem_limit_bytes=64 * 1024 * 1024),
        name="layer",
    )(tokens, cotangent, keep, weight, wq, wp, w1, w2, vec)


def adamw(master, first, second, gradient, step_rate, weight_decay):
    first_new = 0.9 * first + 0.1 * gradient
    second_new = 0.999 * second + 0.001 * gradient * gradient
    step_size = first_new / (1.0 - 0.9**STEP) / (jnp.sqrt(second_new / (1.0 - 0.999**STEP)) + 1e-08)
    return (first_new, second_new, master - step_rate * (step_size + weight_decay * master))


def by_pair(weight):
    rows, cols = weight.shape
    return weight.reshape(rows, 3, PAIRS, cols // (3 * PAIRS)).transpose(2, 0, 1, 3).reshape(
        PAIRS, rows, cols // PAIRS
    )


def from_pairs(grad):
    pairs, rows, cols = grad.shape
    return grad.reshape(pairs, rows, 3, cols // 3).transpose(1, 2, 0, 3).reshape(rows, pairs * cols)


def on_device(
    tokens, cotangent, keep_mask, source,
    qkv_master, proj_master, fc1_master, fc2_master, vec_master,
    qkv_first, proj_first, fc1_first, fc2_first, vec_first,
    qkv_second, proj_second, fc1_second, fc2_second, vec_second,
):
    gather = functools.partial(lax.all_gather, axis_name="dp", tiled=True)
    w_qkv = gather(qkv_master.astype(BF16), axis=0)
    w_proj = gather(proj_master.astype(BF16), axis=0)
    w_fc1 = gather(fc1_master.astype(BF16), axis=0)
    w_fc2 = gather(fc2_master.astype(BF16), axis=0)
    vectors = gather(vec_master.astype(BF16), axis=1).astype(F32)
    images, length, feat = tokens.shape
    live_mask = keep_mask.astype(F32)
    kept_rows = jnp.sum(live_mask, 1)
    total_sources = images * lax.axis_size("head") * lax.axis_size("dp") // 3
    onehot = (source[:, None] == jnp.arange(total_sources, dtype=jnp.int32)[None, :]).astype(F32)
    totals = lax.psum(jnp.sum(onehot * kept_rows[:, None], 0), ("dp", "head"))
    image_total = jnp.sum(onehot * totals[None, :], 1)
    token_weight = live_mask * (length / image_total)[:, None]
    layer_out, input_grad, gq, gp, g1, g2, gvec = run_layer(
        tokens, cotangent, live_mask, token_weight, by_pair(w_qkv), w_proj, w_fc1, w_fc2, vectors
    )
    gradients = (from_pairs(gq), gp, g1, g2, gvec)
    dims = (0, 0, 0, 0, 1)
    shares = [
        lax.psum_scatter(
            lax.psum(g.astype(BF16), "head").astype(F32), "dp", scatter_dimension=d, tiled=True
        )
        for g, d in zip(gradients, dims)
    ]
    masters = (qkv_master, proj_master, fc1_master, fc2_master, vec_master)
    firsts = (qkv_first, proj_first, fc1_first, fc2_first, vec_first)
    seconds = (qkv_second, proj_second, fc1_second, fc2_second, vec_second)
    states = []
    for parts in zip(masters, firsts, seconds, shares, step_rates, decays):
        states.extend(adamw(*parts))
    return (layer_out, input_grad, *states)


def solution(mesh):
    split = P(("dp", "head"), None, None)
    rows, cols = P("dp", None), P(None, "dp")
    weights = (rows, rows, rows, rows, cols)
    return jax.shard_map(
        on_device,
        mesh=mesh,
        in_specs=(split, split, P(("dp", "head"), None), P(("dp", "head"))) + weights * 3,
        out_specs=(split, split) + (rows,) * 12 + (cols,) * 3,
        check_vma=False,
    )
```

```python
import functools

import jax
import jax.numpy as jnp
from jax import lax
from jax.experimental import pallas as pl
from jax.experimental.pallas import tpu as pltpu
from jax.sharding import PartitionSpec as P

HEADS = 6
HEAD_DIM = 64
STEP = 10
PAIRS = HEADS // 2
SCALE = HEAD_DIM ** (-0.5)

norm_eps = 1e-06
step_rates = (0.1, 0.4, 0.1, 0.05, 0.5)
decays = (0.05, 0.05, 0.05, 0.05, 0.0)

UNITS = 12
PLANE = 4

F32 = jnp.float32
BF16 = jnp.bfloat16


def dot(left, right):
    return lax.dot_general(left, right, (((1,), (0,)), ((), ())), preferred_element_type=F32)


def across(left, right):
    return lax.dot_general(left, right, (((0,), (0,)), ((), ())), preferred_element_type=F32)


def against(left, right):
    return lax.dot_general(left, right, (((1,), (1,)), ((), ())), preferred_element_type=F32)


def normalise(values):
    average = jnp.mean(values, -1, keepdims=True)
    centred = values - average
    variance = jnp.mean(centred * centred, -1, keepdims=True)
    inverse = lax.rsqrt(variance + norm_eps)
    return centred * inverse, inverse


def norm_back(grad, unit, inverse, gain_row):
    scaled = grad * gain_row
    first = jnp.mean(scaled, -1, keepdims=True)
    second = jnp.mean(scaled * unit, -1, keepdims=True)
    return inverse * (scaled - first - unit * second)


def fold(values):
    rows, cols = values.shape
    return jnp.sum(values.reshape(rows // 8, 8, cols), 0)


ERF_A = (0.254829592, -0.284496736, 1.421413741, -1.453152027, 1.061405429)
ERF_C = 0.3275911 * 0.7071067811865476
LOG2E_HALF = 0.7213475204444817
INV_SQRT_2PI = 0.3989422804014327


def gelu_parts(x):
    bell = jnp.exp2(x * x * (-LOG2E_HALF))
    t = 1.0 / (1.0 + ERF_C * jnp.abs(x))
    a1, a2, a3, a4, a5 = (0.5 * a for a in ERF_A)
    tail = ((((a5 * t + a4) * t + a3) * t + a2) * t + a1) * t * bell
    cdf = jnp.where(x >= 0, 1.0 - tail, tail)
    return x * cdf, cdf + x * (bell * INV_SQRT_2PI)


def layer_kernel(linked, dp, sources, *refs):
    refs = list(refs)

    def take(count):
        taken = refs[:count]
        del refs[:count]
        return taken

    tok_hbm, cot_hbm, keep_ref = take(3)
    if linked:
        src_ref, qm_ref, pm_ref, f1_ref, f2_ref, vm_ref = take(6)
        out_hbm, gin_hbm, share_ref, vshare_ref = take(4)
        wq_ref, wp_ref, w1_ref, w2_ref, vec_ref = take(5)
        slabs, vslabs, tot_mine, tot_in, pair_in, pair_sum, plane_in, layer_out, layer_in = take(9)
        vsum, vin, share_in, send, recv = take(5)
    else:
        tw_ref, wq_ref, wp_ref, w1_ref, w2_ref, vec_ref = take(6)
        out_hbm, gin_hbm, gq_ref, gp_ref, g1_ref, g2_ref, gvec_ref = take(7)
    tok, cot, xs, normed, qkv, probs, att, middle, nmid, act, gel, gol, gml, twc, sums, acc = take(16)
    outs, gins, keepf, tws, local = take(5)

    images, length, feat = tok.shape
    padded = xs.shape[1]
    hidden_units = w1_ref.shape[1] // feat
    lane = lax.broadcasted_iota(jnp.int32, (padded, 128), 1)
    low_half = lane < HEAD_DIM

    def each_image(body, first=0, last=None):
        lax.fori_loop(first, images if last is None else last, lambda i, c: (body(i), c)[1], 0)

    def row(n):
        return vec_ref[n : n + 1, :]

    def stacked_halves(values):
        zero = jnp.zeros_like(values)
        return jnp.concatenate(
            [jnp.where(low_half, values, zero), jnp.where(low_half, zero, values)], 0
        )

    def merged_halves(values):
        return jnp.where(low_half, values[:padded], values[padded:])

    tok_in = pltpu.make_async_copy(tok_hbm, tok, local.at[0])
    cot_in = pltpu.make_async_copy(cot_hbm, cot, local.at[1])
    out_copy = pltpu.make_async_copy(outs, out_hbm, local.at[2])
    gin_copy = pltpu.make_async_copy(gins, gin_hbm, local.at[3])
    tok_in.start()
    cot_in.start()

    started = []
    if linked:
        me = lax.axis_index("dp")
        core = lax.axis_index("head")
        layers = dp // PLANE
        layer, place = me // PLANE, me % PLANE
        counter = [0]
        shard = 24

        def peers(kind):
            if kind == "layer":
                return [(((layer + r) % layers) * PLANE + place, core) for r in range(1, layers)]
            if kind == "plane":
                return [(layer * PLANE + (place + r) % PLANE, core) for r in range(1, PLANE)]
            return [(me, 1 - core)]

        def push(kind, pick):
            copies = []
            for r, device in enumerate(peers(kind), 1):
                src, dst = pick(r)
                k = counter[0]
                counter[0] += 1
                copy = pltpu.make_async_remote_copy(
                    src_ref=src,
                    dst_ref=dst,
                    send_sem=send.at[k],
                    recv_sem=recv.at[k],
                    device_id=device,
                    device_id_type=pl.DeviceIdType.MESH,
                )
                copy.start()
                copies.append(copy)
            started.extend(copies)
            return copies

        def arrive(copies):
            for copy in copies:
                copy.wait_recv()

        barrier = pltpu.get_barrier_semaphore()
        everyone = peers("layer") + peers("plane") + peers("core")
        for device in everyone:
            pl.semaphore_signal(
                barrier, inc=1, device_id=device, device_id_type=pl.DeviceIdType.MESH
            )

        def own_block(u):
            if u < PAIRS:
                parts = [qm_ref[:, n * feat + 128 * u : n * feat + 128 * u + 128] for n in range(3)]
                return jnp.concatenate(parts, 1)
            if u == 3:
                return pm_ref[...]
            if u < 8:
                return f1_ref[:, feat * (u - 4) : feat * (u - 3)]
            return f2_ref[shard * (u - 8) : shard * (u - 7), :]

        vslabs[place, layer] = jnp.zeros((16, 128), BF16)
        vslabs[place, layer, 0:12, 0:shard] = vm_ref[...].astype(BF16)
        for u, other in ((0, 1), (2, 3), (4, 6), (5, 7), (8, 10), (9, 11)):
            mine_now = u + (other - u) * core
            slabs[mine_now, place, layer] = jnp.where(
                core == 0, own_block(u), own_block(other)
            ).astype(BF16)

        kept = jnp.sum(keep_ref[...].astype(F32), 1, keepdims=True)
        width = tot_mine.shape[1]
        source_lane = lax.broadcasted_iota(jnp.int32, (1, width), 1)
        mine = jnp.zeros((1, width), F32)
        for i in range(images):
            mine = mine + jnp.where(source_lane == src_ref[i], kept[i : i + 1], 0.0)
        tot_mine[0:8] = jnp.broadcast_to(mine, (8, width))

        pl.semaphore_wait(barrier, len(everyone))

        def vec_push(kind):
            if kind == "layer":
                return push(kind, lambda r: (vslabs.at[place, layer],) * 2)
            return push(kind, lambda r: (vslabs.at[place],) * 2)

        def tot_push(kind, stage):
            part = pl.ds(8 * stage, 8)
            return push(kind, lambda r: (tot_mine.at[part], tot_in.at[3 * stage + r - 1]))

        def tot_sum(stage, count):
            total = tot_mine[8 * stage : 8 * stage + 8]
            for r in range(count):
                total = total + tot_in[3 * stage + r]
            tot_mine[8 * stage + 8 : 8 * stage + 16] = total

        def step_units(step):
            return (pl.ds(core, 1), pl.ds(2 + core, 1), pl.ds(4 + 2 * core, 2), pl.ds(8 + 2 * core, 2))[
                step
            ]

        def weights_push(step, kind):
            units = step_units(step)
            if kind == "layer":
                return push(kind, lambda r: (slabs.at[units, place, layer],) * 2)
            if kind == "plane":
                return push(kind, lambda r: (slabs.at[units, place],) * 2)
            return push(kind, lambda r: (slabs.at[units],) * 2)

        def assemble(u):
            for q in range(layers):
                for k in range(0, PLANE, 2):
                    both = jnp.concatenate(
                        [slabs[u, k, q].astype(F32), slabs[u, k + 1, q].astype(F32)], 0
                    ).astype(BF16)
                    first = shard * (PLANE * q + k)
                    rows = slice(first, first + 2 * shard)
                    if u < PAIRS:
                        wq_ref[u, rows, :] = both
                    elif u == 3:
                        wp_ref[rows, :] = both
                    else:
                        w1_ref[rows, feat * (u - 4) : feat * (u - 3)] = both

        def assemble_w2():
            for q in range(layers):
                for k in range(PLANE):
                    for j in range(0, 4, 2):
                        both = jnp.concatenate(
                            [slabs[8 + j, k, q].astype(F32), slabs[9 + j, k, q].astype(F32)], 0
                        ).astype(BF16)
                        first = 4 * shard * (PLANE * q + k) + shard * j
                        w2_ref[first : first + 2 * shard, :] = both

        def spread(values, owner):
            lanes = lax.broadcasted_iota(jnp.int32, (16, 128), 1)
            shift = (shard * owner) % 128
            moved = pltpu.roll(values, shift, 1) if shift else values
            block = shard * owner // 128
            here = jnp.where(lanes >= shift, moved, 0.0)
            vec_ref[:, 128 * block : 128 * block + 128] += here
            if shift + shard > 128:
                rest = jnp.where(lanes < shift, moved, 0.0)
                vec_ref[:, 128 * block + 128 : 128 * block + 256] += rest

        vec_go = vec_push("layer")
        go0 = weights_push(0, "layer")
        tot_go = tot_push("layer", 0)
        arrive(vec_go)
        vec_go = vec_push("plane")
        arrive(go0)
        go0 = weights_push(0, "plane")
        go1 = weights_push(1, "layer")
        arrive(tot_go)
        tot_sum(0, layers - 1)
        tot_go = tot_push("plane", 1)
        arrive(vec_go)
        vec_ref[...] = jnp.zeros_like(vec_ref)
        for owner in range(dp):
            spread(vslabs[owner % PLANE, owner // PLANE].astype(F32), owner)

    tail = padded - 16
    xs[:, tail:, :] = jnp.zeros((images, 16, feat), BF16)
    gol[:, tail:, :] = jnp.zeros((images, 16, feat), BF16)
    sums[...] = jnp.zeros_like(sums)
    keepf[...] = jnp.zeros_like(keepf)
    keepf[0:images, 0:length] = keep_ref[...].astype(F32)

    def first_norm(i):
        xs[i, 0:length, :] = tok[i]
        unit, _ = normalise(xs[i].astype(F32))
        normed[i] = (unit * row(0) + row(1)).astype(BF16)

    tok_in.wait()
    each_image(first_norm)

    if linked:
        arrive(go0)
        go0 = weights_push(0, "core")
        arrive(go1)
        go1 = weights_push(1, "plane")
        go2 = weights_push(2, "layer")
        arrive(tot_go)
        tot_sum(1, PLANE - 1)
        tot_go = tot_push("core", 2)
        arrive(go0)
        assemble(0)
        assemble(1)

    def project(h, i):
        part = pl.ds(128 * h, 128)
        bias = jnp.concatenate(
            [vec_ref[2:3, part], jnp.zeros((1, 128), F32), vec_ref[3:4, part]], 1
        )
        qkv[h, i] = (dot(normed[i], wq_ref[h]) + bias).astype(BF16)

    def attend(h, i):
        alive = keepf[pl.ds(i, 1), 0:padded] > 0
        query = stacked_halves(qkv[h, i, :, 0:128] * BF16(SCALE))
        scores = against(query, qkv[h, i, :, 128:256])
        scores = jnp.where(alive, scores, -1e9)
        top = jnp.max(scores, -1, keepdims=True)
        raised = jnp.exp(scores - top)
        share = raised * (1.0 / jnp.sum(raised, -1, keepdims=True))
        share = share.astype(BF16)
        probs[h, i] = share
        att[i, :, 128 * h : 128 * h + 128] = merged_halves(
            dot(share, qkv[h, i, :, 256:384])
        ).astype(BF16)

    for h in range(PAIRS):
        if linked and h == 1:
            arrive(go1)
            go1 = weights_push(1, "core")
            arrive(go2)
            go2 = weights_push(2, "plane")
            go3 = weights_push(3, "layer")
        if linked and h == 2:
            arrive(go1)
            assemble(2)
            assemble(3)
            arrive(go2)
            go2 = weights_push(2, "core")
            arrive(go3)
            go3 = weights_push(3, "plane")
        each_image(functools.partial(project, h))
        each_image(functools.partial(attend, h))

    if linked:
        arrive(tot_go)
        tot_sum(2, 1)
        totals = tot_mine[24:25]
        for i in range(images):
            total = jnp.sum(
                jnp.where(source_lane == src_ref[i], totals, 0.0), 1, keepdims=True
            )
            tws[i : i + 1] = keepf[i : i + 1] * (length / total)
    else:
        tws[...] = jnp.zeros_like(tws)
        tws[0:images, 0:length] = tw_ref[...]

    def second_norm(i):
        mid = xs[i].astype(F32) + (dot(att[i], wp_ref[...]) + row(4))
        middle[i] = mid
        unit, _ = normalise(mid)
        nmid[i] = (unit * row(5) + row(6)).astype(BF16)

    each_image(second_norm)
    if linked:
        arrive(go2)
        for u in range(4, 8):
            assemble(u)
        arrive(go3)
        go3 = weights_push(3, "core")

    def expand(i):
        values = nmid[i]
        for j in range(hidden_units):
            cols = slice(feat * j, feat * j + feat)
            pre = dot(values, w1_ref[:, cols]) + row(8 + j)
            active, slope = gelu_parts(pre)
            act[i, :, cols] = active.astype(BF16)
            gel[i, :, cols] = slope.astype(BF16)

    each_image(expand)
    if linked:
        arrive(go3)
        assemble_w2()

    def contract(i):
        total = middle[i] + (dot(act[i], w2_ref[...]) + row(7))
        outs[i] = total[:length].astype(BF16)

    each_image(contract)
    out_copy.start()

    eye = lax.broadcasted_iota(jnp.int32, (padded, padded), 0) == lax.broadcasted_iota(
        jnp.int32, (padded, padded), 1
    )

    def hidden_back(i):
        weight_row = tws[pl.ds(i, 1), 0:padded]
        column = jnp.sum(jnp.where(eye, weight_row, 0.0), 1, keepdims=True)
        twc[i] = jnp.broadcast_to(column, (padded, 128))
        wide = jnp.concatenate([twc[i]] * (feat // 128), 1)[:length]
        gol[i, 0:length, :] = (cot[i].astype(F32) * wide).astype(BF16)
        grad = gol[i]
        sums[7] += fold(grad.astype(F32))
        for j in range(hidden_units):
            cols = slice(feat * j, feat * j + feat)
            back = against(grad, w2_ref[cols, :]) * gel[i, :, cols].astype(F32)
            back = back.astype(BF16)
            gel[i, :, cols] = back
            sums[8 + j] += fold(back.astype(F32))

    cot_in.wait()
    each_image(hidden_back)

    acc[...] = jnp.zeros_like(acc)

    def fc2_grad(i):
        for j in range(hidden_units):
            acc[j] += across(act[i, :, feat * j : feat * j + feat], gol[i])

    each_image(fc2_grad)

    if linked:
        def job_units(job, owner):
            return (pl.ds(8 + 2 * owner, 2), pl.ds(4 + 2 * owner, 2), pl.ds(2 + owner, 1), pl.ds(owner, 1))[job]

        def job_slots(job):
            return (0, 2), (2, 4), (4, 5), (5, 6)

        job_slot = ((0, 2), (2, 4), (4, 5), (5, 6))

        def emit(u, source_block):
            for owner in range(dp):
                slabs[u, owner % PLANE, owner // PLANE] = source_block(owner).astype(BF16)

        def grads_pair(job):
            first, last = job_slot[job]
            theirs = job_units(job, 1 - core)
            return push("core", lambda r: (slabs.at[theirs], pair_in.at[pl.ds(first, last - first)]))

        def first_unit(job):
            return (8 + 2 * core, 4 + 2 * core, 2 + core, core)[job]

        def grads_plane(job):
            first, last = job_slot[job]
            for s in range(first, last):
                unit = first_unit(job) + (s - first)
                for k in range(PLANE):
                    for q in range(layers):
                        pair_sum[s, k, q] = (
                            slabs[unit, k, q].astype(F32) + pair_in[s, k, q].astype(F32)
                        ).astype(BF16)
            size = pl.ds(first, last - first)
            return push(
                "plane",
                lambda r: (pair_sum.at[size, (place + r) % PLANE], plane_in.at[r - 1, size]),
            )

        def grads_layer(job):
            first, last = job_slot[job]
            for s in range(first, last):
                for q in range(layers):
                    total = pair_sum[s, place, q].astype(F32)
                    for r in range(PLANE - 1):
                        total = total + plane_in[r, s, q].astype(F32)
                    layer_out[s, q] = total.astype(BF16)
            size = pl.ds(first, last - first)
            return push(
                "layer",
                lambda r: (layer_out.at[size, (layer + r) % layers], layer_in.at[r - 1, size]),
            )

        def grads_share(job):
            first, last = job_slot[job]
            units = job_units(job, core)
            for s in range(first, last):
                total = layer_out[s, layer].astype(F32)
                for r in range(layers - 1):
                    total = total + layer_in[r, s].astype(F32)
                share_in[first_unit(job) + (s - first)] = total
            return push("core", lambda r: (share_in.at[units], share_in.at[units]))

        for copy in started:
            copy.wait_send()
        started.clear()
        shares = []
        for j in range(4):
            emit(8 + j, lambda owner: acc[
                4 * shard * owner // feat,
                (4 * shard * owner) % feat + shard * j : (4 * shard * owner) % feat + shard * j + shard,
            ])
        jobs = [grads_pair(0)]
    else:
        for j in range(hidden_units):
            g2_ref[feat * j : feat * j + feat, :] = acc[j]

    def middle_back(i):
        unit, inverse = normalise(middle[i])
        grad = against(gel[i], w1_ref[...])
        sums[5] += fold(grad * unit)
        sums[6] += fold(grad)
        middle[i] = norm_back(grad, unit, inverse, row(5))
        wide = jnp.concatenate([twc[i]] * (feat // 128), 1)[:length]
        middle[i, 0:length, :] += cot[i].astype(F32) * wide
        low = middle[i].astype(BF16)
        gml[i] = low
        sums[4] += fold(low.astype(F32))

    each_image(middle_back)
    if linked:
        arrive(jobs[0])
        jobs[0] = grads_plane(0)

    acc[...] = jnp.zeros_like(acc)

    def fc1_grad(i):
        for j in range(hidden_units):
            acc[j] += across(nmid[i], gel[i, :, feat * j : feat * j + feat])

    each_image(fc1_grad)
    if linked:
        for j in range(4):
            emit(4 + j, lambda owner: acc[j, shard * owner : shard * owner + shard])
        jobs.append(grads_pair(1))
    else:
        for j in range(hidden_units):
            g1_ref[:, feat * j : feat * j + feat] = acc[j]

    acc[...] = jnp.zeros_like(acc)

    def proj_grad(i):
        acc[3] += across(att[i], gml[i])

    each_image(proj_grad)
    if linked:
        arrive(jobs[0])
        jobs[0] = grads_layer(0)
        arrive(jobs[1])
        jobs[1] = grads_plane(1)
        emit(3, lambda owner: acc[3, shard * owner : shard * owner + shard])
    else:
        gp_ref[...] = acc[3]

    def grad_attended(i):
        att[i] = against(gml[i], wp_ref[...]).astype(BF16)

    each_image(grad_attended)

    def attend_back(h, i):
        grad = stacked_halves(att[i, :, 128 * h : 128 * h + 128])
        key = qkv[h, i, :, 128:256]
        query = stacked_halves(qkv[h, i, :, 0:128] * BF16(SCALE))
        share_low = probs[h, i]
        share = share_low.astype(F32)
        grad_share = against(grad, qkv[h, i, :, 256:384])
        inner = jnp.sum(share * grad_share, -1, keepdims=True)
        grad_score = (share * (grad_share - inner)).astype(BF16)
        grad_query = (merged_halves(dot(grad_score, key)) * SCALE).astype(BF16)
        grad_key = across(grad_score, query).astype(BF16)
        grad_value = across(share_low, grad).astype(BF16)
        qkv[h, i, :, 0:128] = grad_query
        qkv[h, i, :, 128:256] = grad_key
        qkv[h, i, :, 256:384] = grad_value
        part = slice(128 * h, 128 * h + 128)
        sums[2, :, part] += fold(grad_query.astype(F32))
        sums[3, :, part] += fold(grad_value.astype(F32))

    def qkv_grad(h, i):
        acc[h] += across(normed[i], qkv[h, i])

    for h in reversed(range(PAIRS)):
        each_image(functools.partial(attend_back, h))
        each_image(functools.partial(qkv_grad, h))
        if linked:
            emit(h, lambda owner: acc[h, shard * owner : shard * owner + shard])
            if h == 2:
                jobs.append(grads_pair(2))
                arrive(jobs[0])
                shares.append(grads_share(0))
                arrive(jobs[1])
                jobs[1] = grads_layer(1)
            if h == 1:
                arrive(jobs[2])
                jobs[2] = grads_plane(2)
                arrive(jobs[1])
                shares.append(grads_share(1))
        else:
            gq_ref[h] = acc[h]

    def input_back(i):
        unit, inverse = normalise(xs[i].astype(F32))
        grad = against(qkv[0, i], wq_ref[0])
        for h in range(1, PAIRS):
            grad = grad + against(qkv[h, i], wq_ref[h])
        sums[0] += fold(grad * unit)
        sums[1] += fold(grad)
        total = middle[i] + norm_back(grad, unit, inverse, row(0))
        gins[i] = total[:length]

    if linked:
        jobs.append(grads_pair(3))
        arrive(jobs[2])
        jobs[2] = grads_layer(2)
        each_image(input_back, 0, images // 3)
        arrive(jobs[3])
        jobs[3] = grads_plane(3)
        each_image(input_back, images // 3, images - images // 3)
        arrive(jobs[3])
        jobs[3] = grads_layer(3)
        arrive(jobs[2])
        shares.append(grads_share(2))
        each_image(input_back, images - images // 3, images)
        gin_copy.start()
        for n in range(12):
            vsum[0, n : n + 1, :] = jnp.sum(sums[n], 0, keepdims=True)
        vsum[0, 12:16, :] = jnp.zeros((4, feat), F32)
        for stage, kind in enumerate(("core", "plane", "layer")):
            go = push(kind, lambda r: (vsum.at[stage], vin.at[3 * stage + r - 1]))
            if stage == 1:
                arrive(jobs[3])
                shares.append(grads_share(3))
            arrive(go)
            total = vsum[stage]
            for r in range(len(go)):
                total = total + vin[3 * stage + r]
            vsum[stage + 1] = total
        picked = jnp.zeros((16, 128), F32)
        for owner in range(dp):
            shift = (shard * owner) % 128
            block = shard * owner // 128
            part = vsum[3, :, 128 * block : 128 * block + 128]
            part = pltpu.roll(part, 128 - shift, 1) if shift else part
            if shift + shard > 128:
                rest = pltpu.roll(vsum[3, :, 128 * block + 128 : 128 * block + 256], 128 - shift, 1)
                lanes = lax.broadcasted_iota(jnp.int32, (16, 128), 1)
                part = jnp.where(lanes < 128 - shift, part, rest)
            picked = jnp.where(me == owner, part, picked)
        vshare_ref[...] = picked
        for go in shares:
            arrive(go)
        share_ref[...] = share_in[...]
        for copy in started:
            copy.wait_send()
    else:
        each_image(input_back)
        gin_copy.start()
        for n in range(12):
            gvec_ref[n : n + 1, :] = jnp.sum(sums[n], 0, keepdims=True)
    out_copy.wait()
    gin_copy.wait()


def layer_call(linked, dp, sources, tokens, cotangent, keep, *rest):
    images, length, feat = tokens.shape
    padded = -(-length // 16) * 16
    hidden = 4 * feat
    vmem = pl.BlockSpec(memory_space=pltpu.VMEM)
    anywhere = pl.BlockSpec(memory_space=pl.ANY)
    smem = pl.BlockSpec(memory_space=pltpu.SMEM)
    shape = jax.ShapeDtypeStruct
    outs = [shape((images, length, feat), BF16), shape((images, length, feat), F32)]
    weights = [
        pltpu.VMEM((PAIRS, feat, feat), BF16),
        pltpu.VMEM((feat, feat), BF16),
        pltpu.VMEM((feat, hidden), BF16),
        pltpu.VMEM((hidden, feat), BF16),
        pltpu.VMEM((16, feat), F32),
    ]
    if linked:
        layers = dp // PLANE
        width = -(-sources // 128) * 128
        in_specs = [anywhere, anywhere, vmem, smem] + [vmem] * 5
        outs += [shape((UNITS, 24, feat), F32), shape((16, 128), F32)]
        copies = 4 * (layers - 1 + PLANE - 1 + 1) + 2 * (layers + PLANE - 2) + 1
        copies += 4 * (1 + layers - 1 + PLANE - 1 + 1) + layers + PLANE - 1
        links = [
            pltpu.VMEM((UNITS, PLANE, layers, 24, feat), BF16),
            pltpu.VMEM((PLANE, layers, 16, 128), BF16),
            pltpu.VMEM((32, width), F32),
            pltpu.VMEM((9, 8, width), F32),
            pltpu.VMEM((UNITS // 2, PLANE, layers, 24, feat), BF16),
            pltpu.VMEM((UNITS // 2, PLANE, layers, 24, feat), BF16),
            pltpu.VMEM((PLANE - 1, UNITS // 2, layers, 24, feat), BF16),
            pltpu.VMEM((UNITS // 2, layers, 24, feat), BF16),
            pltpu.VMEM((layers - 1, UNITS // 2, 24, feat), BF16),
            pltpu.VMEM((4, 16, feat), F32),
            pltpu.VMEM((9, 16, feat), F32),
            pltpu.VMEM((UNITS, 24, feat), F32),
            pltpu.SemaphoreType.DMA((copies,)),
            pltpu.SemaphoreType.DMA((copies,)),
        ]
    else:
        in_specs = [anywhere, anywhere] + [vmem] * 7
        outs += [shape(w.shape, F32) for w in rest[1:]]
        weights, links = [], []
    params = dict(vmem_limit_bytes=64 * 1024 * 1024)
    if linked:
        params.update(collective_id=0, has_side_effects=True)
    return pl.pallas_call(
        functools.partial(layer_kernel, linked, dp, sources),
        out_shape=outs,
        in_specs=in_specs,
        out_specs=[anywhere, anywhere] + [vmem] * (len(outs) - 2),
        scratch_shapes=weights
        + links
        + [
            pltpu.VMEM((images, length, feat), BF16),
            pltpu.VMEM((images, length, feat), BF16),
            pltpu.VMEM((images, padded, feat), BF16),
            pltpu.VMEM((images, padded, feat), BF16),
            pltpu.VMEM((PAIRS, images, padded, feat), BF16),
            pltpu.VMEM((PAIRS, images, 2 * padded, padded), BF16),
            pltpu.VMEM((images, padded, feat), BF16),
            pltpu.VMEM((images, padded, feat), F32),
            pltpu.VMEM((images, padded, feat), BF16),
            pltpu.VMEM((images, padded, hidden), BF16),
            pltpu.VMEM((images, padded, hidden), BF16),
            pltpu.VMEM((images, padded, feat), BF16),
            pltpu.VMEM((images, padded, feat), BF16),
            pltpu.VMEM((images, padded, 128), F32),
            pltpu.VMEM((12, 8, feat), F32),
            pltpu.VMEM((4, feat, feat), F32),
            pltpu.VMEM((images, length, feat), BF16),
            pltpu.VMEM((images, length, feat), F32),
            pltpu.VMEM((16, 256), F32),
            pltpu.VMEM((16, 256), F32),
            pltpu.SemaphoreType.DMA((4,)),
        ],
        compiler_params=pltpu.CompilerParams(**params),
        name="layer",
    )(tokens, cotangent, keep, *rest)


def adamw(master, first, second, gradient, step_rate, weight_decay):
    first_new = 0.9 * first + 0.1 * gradient
    second_new = 0.999 * second + 0.001 * gradient * gradient
    step_size = first_new / (1.0 - 0.9**STEP) / (jnp.sqrt(second_new / (1.0 - 0.999**STEP)) + 1e-08)
    return (first_new, second_new, master - step_rate * (step_size + weight_decay * master))


def step_kernel(share_ref, vshare_ref, *refs):
    state, outs = refs[:15], refs[15:]
    feat = share_ref.shape[2]

    def update(n, here, gradient):
        new = adamw(
            state[n][here], state[5 + n][here], state[10 + n][here], gradient, step_rates[n], decays[n]
        )
        for k in range(3):
            outs[3 * n + k][here] = new[k]

    everything = slice(None)
    for u in range(PAIRS):
        for n in range(3):
            first = n * feat + 128 * u
            update(0, (everything, slice(first, first + 128)), share_ref[u, :, 128 * n : 128 * n + 128])
    update(1, (everything, everything), share_ref[3])
    for j in range(4):
        update(2, (everything, slice(feat * j, feat * j + feat)), share_ref[4 + j])
        rows = share_ref.shape[1]
        update(3, (slice(rows * j, rows * j + rows), everything), share_ref[8 + j])
    vec = state[4]
    update(4, (everything, everything), vshare_ref[0 : vec.shape[0], 0 : vec.shape[1]])


def step_call(share, vshare, states):
    vmem = pl.BlockSpec(memory_space=pltpu.VMEM)
    shape = jax.ShapeDtypeStruct
    return pl.pallas_call(
        step_kernel,
        out_shape=[shape(states[n].shape, F32) for n in range(5) for _ in range(3)],
        in_specs=[vmem] * 17,
        out_specs=[vmem] * 15,
        name="step",
    )(share, vshare, *states)


def by_pair(weight):
    rows, cols = weight.shape
    return weight.reshape(rows, 3, PAIRS, cols // (3 * PAIRS)).transpose(2, 0, 1, 3).reshape(
        PAIRS, rows, cols // PAIRS
    )


def from_pairs(grad):
    pairs, rows, cols = grad.shape
    return grad.reshape(pairs, rows, 3, cols // 3).transpose(1, 2, 0, 3).reshape(rows, pairs * cols)


def on_device(tokens, cotangent, keep_mask, source, *states):
    masters = states[:5]
    dp = lax.axis_size("dp")
    images, length, feat = tokens.shape
    sources = images * lax.axis_size("head") * dp // 3
    if dp == 16:
        layer_out, input_grad, share, vshare = layer_call(
            True, dp, sources, tokens, cotangent, keep_mask, source, *masters
        )
        return (layer_out, input_grad, *step_call(share, vshare, states))
    gather = functools.partial(lax.all_gather, axis_name="dp", tiled=True)
    low = [master.astype(BF16) for master in masters]
    w_qkv, w_proj, w_fc1, w_fc2 = (gather(w, axis=0) for w in low[:4])
    vectors = gather(low[4], axis=1).astype(F32)
    live_mask = keep_mask.astype(F32)
    kept_rows = jnp.sum(live_mask, 1)
    onehot = (source[:, None] == jnp.arange(sources, dtype=jnp.int32)[None, :]).astype(F32)
    totals = lax.psum(jnp.sum(onehot * kept_rows[:, None], 0), ("dp", "head"))
    image_total = jnp.sum(onehot * totals[None, :], 1)
    token_weight = live_mask * (length / image_total)[:, None]
    layer_out, input_grad, gq, gp, g1, g2, gvec = layer_call(
        False, dp, sources, tokens, cotangent, keep_mask,
        token_weight, by_pair(w_qkv), w_proj, w_fc1, w_fc2, vectors,
    )
    gradients = (from_pairs(gq), gp, g1, g2, gvec)
    dims = (0, 0, 0, 0, 1)
    shares = [
        lax.psum_scatter(
            lax.psum(g.astype(BF16), "head").astype(F32), "dp", scatter_dimension=d, tiled=True
        )
        for g, d in zip(gradients, dims)
    ]
    new = []
    for n in range(5):
        new.extend(
            adamw(masters[n], states[5 + n], states[10 + n], shares[n], step_rates[n], decays[n])
        )
    return (layer_out, input_grad, *new)


def solution(mesh):
    split = P(("dp", "head"), None, None)
    rows, cols = P("dp", None), P(None, "dp")
    weights = (rows, rows, rows, rows, cols)
    return jax.shard_map(
        on_device,
        mesh=mesh,
        in_specs=(split, split, P(("dp", "head"), None), P(("dp", "head"))) + weights * 3,
        out_specs=(split, split) + (rows,) * 12 + (cols,) * 3,
        check_vma=False,
    )
```

```python
import functools

import jax
import jax.numpy as jnp
from jax import lax
from jax.experimental import pallas as pl
from jax.experimental.pallas import tpu as pltpu
from jax.sharding import PartitionSpec as P

HEADS = 6
HEAD_DIM = 64
STEP = 10
PAIRS = HEADS // 2
SCALE = HEAD_DIM ** (-0.5)

norm_eps = 1e-06
step_rates = (0.1, 0.4, 0.1, 0.05, 0.5)
decays = (0.05, 0.05, 0.05, 0.05, 0.0)

UNITS = 12
PLANE = 4

F32 = jnp.float32
BF16 = jnp.bfloat16


def dot(left, right):
    return lax.dot_general(left, right, (((1,), (0,)), ((), ())), preferred_element_type=F32)


def across(left, right):
    return lax.dot_general(left, right, (((0,), (0,)), ((), ())), preferred_element_type=F32)


def against(left, right):
    return lax.dot_general(left, right, (((1,), (1,)), ((), ())), preferred_element_type=F32)


def normalise(values):
    average = jnp.mean(values, -1, keepdims=True)
    centred = values - average
    variance = jnp.mean(centred * centred, -1, keepdims=True)
    inverse = lax.rsqrt(variance + norm_eps)
    return centred * inverse, inverse


def norm_back(grad, unit, inverse, gain_row):
    scaled = grad * gain_row
    first = jnp.mean(scaled, -1, keepdims=True)
    second = jnp.mean(scaled * unit, -1, keepdims=True)
    return inverse * (scaled - first - unit * second)


def fold(values):
    rows, cols = values.shape
    return jnp.sum(values.reshape(rows // 8, 8, cols), 0)


LOG2E_HALF = 0.7213475204444817
INV_SQRT_2PI = 0.3989422804014327


def gelu_parts(x):
    cdf = 0.5 + 0.5 * lax.erf(x * 0.7071067811865476)
    bell = jnp.exp2(x * x * (-LOG2E_HALF)) * INV_SQRT_2PI
    return x * cdf, cdf + x * bell


def layer_kernel(linked, dp, sources, *refs):
    refs = list(refs)

    def take(count):
        taken = refs[:count]
        del refs[:count]
        return taken

    tok_hbm, cot_hbm, keep_ref = take(3)
    if linked:
        src_ref, qm_ref, pm_ref, f1_ref, f2_ref, vm_ref = take(6)
        out_hbm, gin_hbm, share_ref, vshare_ref = take(4)
        wq_ref, wp_ref, w1_ref, w2_ref, vec_ref = take(5)
        slabs, vslabs, tot_mine, tot_in, pair_in, plane_in, layer_out, layer_in = take(8)
        vsum, vin, share_in, send, recv = take(5)
    else:
        tw_ref, wq_ref, wp_ref, w1_ref, w2_ref, vec_ref = take(6)
        out_hbm, gin_hbm, gq_ref, gp_ref, g1_ref, g2_ref, gvec_ref = take(7)
    cot, xs, normed, qkv, probs, att, middle, nmid, act, gel, gol, gml, dsc = take(13)
    sums, sums1, b1, outs, gins, keepf, tws, local = take(8)

    images, length, feat = cot.shape
    padded = xs.shape[0] // images
    hidden = act.shape[1]
    hidden_units = hidden // feat
    group = 3 if images % 3 == 0 else 1
    chunk = 256
    lane = lax.broadcasted_iota(jnp.int32, (padded, 128), 1)
    low_half = lane < HEAD_DIM

    def image_rows(i):
        return pl.ds(pl.multiple_of(i * padded, padded), padded)

    def real_rows(i):
        return pl.ds(pl.multiple_of(i * padded, padded), length)

    def each_block(body, first=0, last=None):
        def step(t, carry):
            rows = pl.ds(pl.multiple_of(t * group * padded, padded), group * padded)
            body(rows, [t * group + k for k in range(group)])
            return carry

        lax.fori_loop(first, images // group if last is None else last, step, 0)

    def row(n):
        return vec_ref[n : n + 1, :]

    def stacked_halves(values):
        zero = jnp.zeros_like(values)
        return jnp.concatenate(
            [jnp.where(low_half, values, zero), jnp.where(low_half, zero, values)], 0
        )

    def merged_halves(values):
        return jnp.where(low_half, values[:padded], values[padded:])

    tok_in = pltpu.make_async_copy(tok_hbm, outs, local.at[0])
    cot_in = pltpu.make_async_copy(cot_hbm, cot, local.at[1])
    out_copy = pltpu.make_async_copy(outs, out_hbm, local.at[2])
    gin_copy = pltpu.make_async_copy(gins, gin_hbm, local.at[3])
    tok_in.start()
    cot_in.start()

    started = []
    if linked:
        me = lax.axis_index("dp")
        core = lax.axis_index("head")
        layers = dp // PLANE
        layer, place = me // PLANE, me % PLANE
        counter = [0]
        shard = 24

        def peers(kind):
            if kind == "layer":
                return [(((layer + r) % layers) * PLANE + place, core) for r in range(1, layers)]
            if kind == "plane":
                return [(layer * PLANE + (place + r) % PLANE, core) for r in range(1, PLANE)]
            return [(me, 1 - core)]

        def push(kind, pick):
            copies = []
            for r, device in enumerate(peers(kind), 1):
                src, dst = pick(r)
                k = counter[0]
                counter[0] += 1
                copy = pltpu.make_async_remote_copy(
                    src_ref=src,
                    dst_ref=dst,
                    send_sem=send.at[k],
                    recv_sem=recv.at[k],
                    device_id=device,
                    device_id_type=pl.DeviceIdType.MESH,
                )
                copy.start()
                copies.append(copy)
            started.extend(copies)
            return copies

        def arrive(copies):
            for copy in copies:
                copy.wait_recv()

        barrier = pltpu.get_barrier_semaphore()
        everyone = peers("layer") + peers("plane") + peers("core")
        for device in everyone:
            pl.semaphore_signal(
                barrier, inc=1, device_id=device, device_id_type=pl.DeviceIdType.MESH
            )

        def own_block(u):
            if u < PAIRS:
                parts = [qm_ref[:, n * feat + 128 * u : n * feat + 128 * u + 128] for n in range(3)]
                return jnp.concatenate(parts, 1)
            if u == 3:
                return pm_ref[...]
            if u < 8:
                return f1_ref[:, feat * (u - 4) : feat * (u - 3)]
            return f2_ref[shard * (u - 8) : shard * (u - 7), :]

        vslabs[place, layer] = jnp.zeros((16, 128), BF16)
        vslabs[place, layer, 0:12, 0:shard] = vm_ref[...].astype(BF16)
        for u, other in ((0, 1), (2, 3), (4, 6), (5, 7), (8, 10), (9, 11)):
            mine_now = u + (other - u) * core
            slabs[mine_now, place, layer] = jnp.where(
                core == 0, own_block(u), own_block(other)
            ).astype(BF16)

        kept = jnp.sum(keep_ref[...].astype(F32), 1, keepdims=True)
        width = tot_mine.shape[1]
        source_lane = lax.broadcasted_iota(jnp.int32, (1, width), 1)
        mine = jnp.zeros((1, width), F32)
        for i in range(images):
            mine = mine + jnp.where(source_lane == src_ref[i], kept[i : i + 1], 0.0)
        tot_mine[0:8] = jnp.broadcast_to(mine, (8, width))

        pl.semaphore_wait(barrier, len(everyone))

        def vec_push(kind):
            if kind == "layer":
                return push(kind, lambda r: (vslabs.at[place, layer],) * 2)
            return push(kind, lambda r: (vslabs.at[place],) * 2)

        def tot_push(kind, stage):
            part = pl.ds(8 * stage, 8)
            return push(kind, lambda r: (tot_mine.at[part], tot_in.at[3 * stage + r - 1]))

        def tot_sum(stage, count):
            total = tot_mine[8 * stage : 8 * stage + 8]
            for r in range(count):
                total = total + tot_in[3 * stage + r]
            tot_mine[8 * stage + 8 : 8 * stage + 16] = total

        def step_units(step):
            return (pl.ds(core, 1), pl.ds(2 + core, 1), pl.ds(4 + 2 * core, 2), pl.ds(8 + 2 * core, 2))[
                step
            ]

        def weights_push(step, kind):
            units = step_units(step)
            if kind == "layer":
                return push(kind, lambda r: (slabs.at[units, place, layer],) * 2)
            if kind == "plane":
                return push(kind, lambda r: (slabs.at[units, place],) * 2)
            return push(kind, lambda r: (slabs.at[units],) * 2)

        def assemble(u):
            for q in range(layers):
                for k in range(0, PLANE, 2):
                    both = jnp.concatenate(
                        [slabs[u, k, q].astype(F32), slabs[u, k + 1, q].astype(F32)], 0
                    ).astype(BF16)
                    first = shard * (PLANE * q + k)
                    rows = slice(first, first + 2 * shard)
                    if u < PAIRS:
                        wq_ref[rows, feat * u : feat * u + feat] = both
                    elif u == 3:
                        wp_ref[rows, :] = both
                    else:
                        w1_ref[rows, feat * (u - 4) : feat * (u - 3)] = both

        def assemble_w2():
            for q in range(layers):
                for k in range(PLANE):
                    for j in range(0, 4, 2):
                        both = jnp.concatenate(
                            [slabs[8 + j, k, q].astype(F32), slabs[9 + j, k, q].astype(F32)], 0
                        ).astype(BF16)
                        first = 4 * shard * (PLANE * q + k) + shard * j
                        w2_ref[first : first + 2 * shard, :] = both

        def spread(values, owner):
            lanes = lax.broadcasted_iota(jnp.int32, (16, 128), 1)
            shift = (shard * owner) % 128
            moved = pltpu.roll(values, shift, 1) if shift else values
            block = shard * owner // 128
            here = jnp.where(lanes >= shift, moved, 0.0)
            vec_ref[:, 128 * block : 128 * block + 128] += here
            if shift + shard > 128:
                rest = jnp.where(lanes < shift, moved, 0.0)
                vec_ref[:, 128 * block + 128 : 128 * block + 256] += rest

        vec_go = vec_push("layer")
        go0 = weights_push(0, "layer")
        tot_go = tot_push("layer", 0)
        arrive(vec_go)
        vec_go = vec_push("plane")
        arrive(go0)
        go0 = weights_push(0, "plane")
        go1 = weights_push(1, "layer")
        arrive(tot_go)
        tot_sum(0, layers - 1)
        tot_go = tot_push("plane", 1)
        arrive(vec_go)
        vec_ref[...] = jnp.zeros_like(vec_ref)
        for owner in range(dp):
            spread(vslabs[owner % PLANE, owner // PLANE].astype(F32), owner)

    for i in range(images):
        tail = slice(padded * (i + 1) - 16, padded * (i + 1))
        xs[tail, :] = jnp.zeros((16, feat), BF16)
        gol[tail, :] = jnp.zeros((16, feat), BF16)
    sums[...] = jnp.zeros_like(sums)
    sums1[...] = jnp.zeros_like(sums1)
    keepf[...] = jnp.zeros_like(keepf)
    keepf[0:images, 0:length] = keep_ref[...].astype(F32)
    for j in range(hidden_units):
        b1[0:1, feat * j : feat * j + feat] = row(8 + j)

    def first_norm(_, block):
        for i in block:
            xs[real_rows(i), :] = outs[i]
            unit, _ = normalise(xs[image_rows(i), :].astype(F32))
            normed[image_rows(i), :] = (unit * row(0) + row(1)).astype(BF16)

    tok_in.wait()
    each_block(first_norm)

    if linked:
        arrive(go0)
        go0 = weights_push(0, "core")
        arrive(go1)
        go1 = weights_push(1, "plane")
        go2 = weights_push(2, "layer")
        arrive(tot_go)
        tot_sum(1, PLANE - 1)
        tot_go = tot_push("core", 2)
        arrive(go0)
        assemble(0)
        assemble(1)

    def project(first, last):
        cols = slice(feat * first, feat * last)
        parts = []
        for h in range(first, last):
            part = pl.ds(128 * h, 128)
            parts += [vec_ref[2:3, part], jnp.zeros((1, 128), F32), vec_ref[3:4, part]]
        bias = jnp.concatenate(parts, 1)

        def body(rows, _):
            qkv[rows, cols] = (dot(normed[rows, :], wq_ref[:, cols]) + bias).astype(BF16)

        each_block(body)

    def attend(h):
        first = feat * h
        results = []
        for i in range(images):
            rows = image_rows(i)
            alive = keepf[i : i + 1, 0:padded] > 0
            query = stacked_halves(qkv[rows, first : first + 128] * BF16(SCALE))
            scores = against(query, qkv[rows, first + 128 : first + 256])
            scores = jnp.where(alive, scores, -1e9)
            top = jnp.max(scores, -1, keepdims=True)
            raised = jnp.exp(scores - top)
            share = raised * (1.0 / jnp.sum(raised, -1, keepdims=True))
            share = share.astype(BF16)
            mixed = dot(share, qkv[rows, first + 256 : first + 384])
            results.append((share, merged_halves(mixed).astype(BF16)))
        for i, (share, mixed) in enumerate(results):
            probs[h, i] = share
            att[image_rows(i), 128 * h : 128 * h + 128] = mixed

    project(0, 2)
    attend(0)
    if linked:
        arrive(go1)
        go1 = weights_push(1, "core")
        arrive(go2)
        go2 = weights_push(2, "plane")
        go3 = weights_push(3, "layer")
    attend(1)
    if linked:
        arrive(go1)
        assemble(2)
        assemble(3)
        arrive(go2)
        go2 = weights_push(2, "core")
        arrive(go3)
        go3 = weights_push(3, "plane")
    project(2, 3)
    attend(2)

    if linked:
        arrive(tot_go)
        tot_sum(2, 1)
        totals = tot_mine[24:25]
        for i in range(images):
            total = jnp.sum(
                jnp.where(source_lane == src_ref[i], totals, 0.0), 1, keepdims=True
            )
            tws[i : i + 1] = keepf[i : i + 1] * (length / total)
    else:
        tws[...] = jnp.zeros_like(tws)
        tws[0:images, 0:length] = tw_ref[...]

    def second_norm(rows, block):
        middle[rows, :] = xs[rows, :].astype(F32) + (dot(att[rows, :], wp_ref[...]) + row(4))
        for i in block:
            unit, _ = normalise(middle[image_rows(i), :])
            nmid[image_rows(i), :] = (unit * row(5) + row(6)).astype(BF16)

    each_block(second_norm)
    if linked:
        arrive(go2)
        for u in range(4, 8):
            assemble(u)
        arrive(go3)
        go3 = weights_push(3, "core")

    def expand(rows, _):
        values = nmid[rows, :]
        for j in range(hidden // chunk):
            cols = slice(chunk * j, chunk * j + chunk)
            active, slope = gelu_parts(dot(values, w1_ref[:, cols]) + b1[0:1, cols])
            act[rows, cols] = active.astype(BF16)
            gel[rows, cols] = slope.astype(BF16)

    each_block(expand)
    if linked:
        arrive(go3)
        assemble_w2()

    def contract(rows, block):
        total = middle[rows, :] + (dot(act[rows, :], w2_ref[...]) + row(7))
        for k, i in enumerate(block):
            outs[i] = total[padded * k : padded * k + length].astype(BF16)

    each_block(contract)
    out_copy.start()

    eye = lax.broadcasted_iota(jnp.int32, (padded, padded), 0) == lax.broadcasted_iota(
        jnp.int32, (padded, padded), 1
    )

    def weigh(_, block):
        for i in block:
            weight_row = tws[pl.ds(i, 1), 0:padded]
            column = jnp.sum(jnp.where(eye, weight_row, 0.0), 1, keepdims=True)
            grad = cot[i].astype(F32) * column[:length]
            gins[i] = grad
            gol[real_rows(i), :] = grad.astype(BF16)

    def hidden_back(rows, _):
        grad = gol[rows, :]
        sums[7] += fold(grad.astype(F32))
        for j in range(hidden // chunk):
            cols = slice(chunk * j, chunk * j + chunk)
            back = against(grad, w2_ref[cols, :]) * gel[rows, cols].astype(F32)
            back = back.astype(BF16)
            gel[rows, cols] = back
            sums1[:, cols] += fold(back.astype(F32))

    cot_in.wait()
    each_block(weigh)
    each_block(hidden_back)

    if linked:
        def job_units(job, owner):
            return (pl.ds(8 + 2 * owner, 2), pl.ds(4 + 2 * owner, 2), pl.ds(2 + owner, 1), pl.ds(owner, 1))[job]

        def job_slots(job):
            return (0, 2), (2, 4), (4, 5), (5, 6)

        job_slot = ((0, 2), (2, 4), (4, 5), (5, 6))

        def emit(u, grad):
            for owner in range(dp):
                slabs[u, owner % PLANE, owner // PLANE] = grad[
                    shard * owner : shard * owner + shard
                ].astype(BF16)

        def grads_pair(job):
            first, last = job_slot[job]
            theirs = job_units(job, 1 - core)
            return push("core", lambda r: (slabs.at[theirs], pair_in.at[pl.ds(first, last - first)]))

        def first_unit(job):
            return (8 + 2 * core, 4 + 2 * core, 2 + core, core)[job]

        def grads_plane(job):
            first, last = job_slot[job]
            for s in range(first, last):
                unit = first_unit(job) + (s - first)
                for k in range(PLANE):
                    for q in range(layers):
                        slabs[unit, k, q] = (
                            slabs[unit, k, q].astype(F32) + pair_in[s, k, q].astype(F32)
                        ).astype(BF16)
            size = pl.ds(first, last - first)
            units = job_units(job, core)
            return push(
                "plane",
                lambda r: (slabs.at[units, (place + r) % PLANE], plane_in.at[r - 1, size]),
            )

        def grads_layer(job):
            first, last = job_slot[job]
            for s in range(first, last):
                for q in range(layers):
                    total = slabs[first_unit(job) + (s - first), place, q].astype(F32)
                    for r in range(PLANE - 1):
                        total = total + plane_in[r, s, q].astype(F32)
                    layer_out[s, q] = total.astype(BF16)
            size = pl.ds(first, last - first)
            return push(
                "layer",
                lambda r: (layer_out.at[size, (layer + r) % layers], layer_in.at[r - 1, size]),
            )

        def grads_share(job):
            first, last = job_slot[job]
            units = job_units(job, core)
            for s in range(first, last):
                total = layer_out[s, layer].astype(F32)
                for r in range(layers - 1):
                    total = total + layer_in[r, s].astype(F32)
                share_in[first_unit(job) + (s - first)] = total
            return push("core", lambda r: (share_in.at[units], share_in.at[units]))

        for copy in started:
            copy.wait_send()
        started.clear()
        shares = []

    half = hidden // 2
    for n in range(2):
        grad = across(act[:, half * n : half * n + half], gol[...])
        if linked:
            block = 4 * shard
            for k in range(dp // 2):
                owner = n * dp // 2 + k
                for j in range(4):
                    first = block * k + shard * j
                    slabs[8 + j, owner % PLANE, owner // PLANE] = grad[
                        first : first + shard
                    ].astype(BF16)
        else:
            g2_ref[half * n : half * n + half, :] = grad
    if linked:
        jobs = [grads_pair(0)]

    def middle_back(rows, block):
        grads = against(gel[rows, :], w1_ref[...])
        for k, i in enumerate(block):
            here = image_rows(i)
            grad = grads[padded * k : padded * k + padded]
            unit, inverse = normalise(middle[here, :])
            sums[5] += fold(grad * unit)
            sums[6] += fold(grad)
            middle[here, :] = norm_back(grad, unit, inverse, row(5))
            middle[real_rows(i), :] += gins[i]
            low = middle[here, :].astype(BF16)
            gml[here, :] = low
            sums[4] += fold(low.astype(F32))

    each_block(middle_back)
    if linked:
        arrive(jobs[0])
        jobs[0] = grads_plane(0)

    for n in range(2):
        grad = across(nmid[...], gel[:, half * n : half * n + half])
        if linked:
            emit(4 + 2 * n, grad[:, 0:feat])
            emit(5 + 2 * n, grad[:, feat:])
        else:
            g1_ref[:, half * n : half * n + half] = grad
    if linked:
        jobs.append(grads_pair(1))

    grad = across(att[...], gml[...])
    if linked:
        emit(3, grad)
        arrive(jobs[0])
        jobs[0] = grads_layer(0)
        arrive(jobs[1])
        jobs[1] = grads_plane(1)
    else:
        gp_ref[...] = grad

    def grad_attended(rows, _):
        att[rows, :] = against(gml[rows, :], wp_ref[...]).astype(BF16)

    each_block(grad_attended)

    def attend_back(h):
        first = feat * h
        results = []
        for i in range(images):
            rows = image_rows(i)
            grad = stacked_halves(att[rows, 128 * h : 128 * h + 128])
            share = probs[h, i].astype(F32)
            grad_share = against(grad, qkv[rows, first + 256 : first + 384])
            inner = jnp.sum(share * grad_share, -1, keepdims=True)
            grad_score = (share * (grad_share - inner)).astype(BF16)
            key = qkv[rows, first + 128 : first + 256]
            grad_query = (merged_halves(dot(grad_score, key)) * SCALE).astype(BF16)
            results.append((grad_score, grad_query))
        for i, (grad_score, _) in enumerate(results):
            dsc[i] = grad_score
        results = [grad_query for _, grad_query in results]
        for i in range(images):
            rows = image_rows(i)
            query = stacked_halves(qkv[rows, first : first + 128] * BF16(SCALE))
            grad = stacked_halves(att[rows, 128 * h : 128 * h + 128])
            qkv[rows, first + 128 : first + 256] = across(dsc[i], query).astype(BF16)
            qkv[rows, first + 256 : first + 384] = across(probs[h, i], grad).astype(BF16)
            qkv[rows, first : first + 128] = results[i]

    def qkv_grad(first, last):
        cols = slice(feat * first, feat * last)
        grad = across(normed[...], qkv[:, cols])
        for h in range(first, last):
            part = grad[:, feat * (h - first) : feat * (h - first + 1)]
            if linked:
                emit(h, part)
            else:
                gq_ref[:, feat * h : feat * h + feat] = part

    attend_back(2)
    qkv_grad(2, 3)
    if linked:
        jobs.append(grads_pair(2))
        arrive(jobs[0])
        shares.append(grads_share(0))
        arrive(jobs[1])
        jobs[1] = grads_layer(1)
    attend_back(1)
    if linked:
        arrive(jobs[2])
        jobs[2] = grads_plane(2)
        arrive(jobs[1])
        shares.append(grads_share(1))
    attend_back(0)
    qkv_grad(0, 2)

    def input_back(rows, block):
        moved = qkv[rows, :]
        folded = fold(moved.astype(F32))
        for h in range(PAIRS):
            part = slice(128 * h, 128 * h + 128)
            sums[2, :, part] += folded[:, feat * h : feat * h + 128]
            sums[3, :, part] += folded[:, feat * h + 256 : feat * h + 384]
        grads = against(moved, wq_ref[...])
        for k, i in enumerate(block):
            here = image_rows(i)
            grad = grads[padded * k : padded * k + padded]
            unit, inverse = normalise(xs[here, :].astype(F32))
            sums[0] += fold(grad * unit)
            sums[1] += fold(grad)
            total = middle[here, :] + norm_back(grad, unit, inverse, row(0))
            gins[i] = total[:length]

    blocks = images // group
    if linked:
        jobs.append(grads_pair(3))
        arrive(jobs[2])
        jobs[2] = grads_layer(2)
        each_block(input_back, 0, 1)
        arrive(jobs[3])
        jobs[3] = grads_plane(3)
        each_block(input_back, 1, blocks - 1)
        arrive(jobs[3])
        jobs[3] = grads_layer(3)
        arrive(jobs[2])
        shares.append(grads_share(2))
        each_block(input_back, blocks - 1, blocks)
        gin_copy.start()
        for n in range(8):
            vsum[0, n : n + 1, :] = jnp.sum(sums[n], 0, keepdims=True)
        for j in range(hidden_units):
            vsum[0, 8 + j : 9 + j, :] = jnp.sum(
                sums1[:, feat * j : feat * j + feat], 0, keepdims=True
            )
        vsum[0, 12:16, :] = jnp.zeros((4, feat), F32)
        for stage, kind in enumerate(("core", "plane", "layer")):
            go = push(kind, lambda r: (vsum.at[stage], vin.at[3 * stage + r - 1]))
            if stage == 1:
                arrive(jobs[3])
                shares.append(grads_share(3))
            arrive(go)
            total = vsum[stage]
            for r in range(len(go)):
                total = total + vin[3 * stage + r]
            vsum[stage + 1] = total
        picked = jnp.zeros((16, 128), F32)
        for owner in range(dp):
            shift = (shard * owner) % 128
            block = shard * owner // 128
            part = vsum[3, :, 128 * block : 128 * block + 128]
            part = pltpu.roll(part, 128 - shift, 1) if shift else part
            if shift + shard > 128:
                rest = pltpu.roll(vsum[3, :, 128 * block + 128 : 128 * block + 256], 128 - shift, 1)
                lanes = lax.broadcasted_iota(jnp.int32, (16, 128), 1)
                part = jnp.where(lanes < 128 - shift, part, rest)
            picked = jnp.where(me == owner, part, picked)
        vshare_ref[...] = picked
        for go in shares:
            arrive(go)
        share_ref[...] = share_in[...]
        for copy in started:
            copy.wait_send()
    else:
        each_block(input_back)
        gin_copy.start()
        for n in range(8):
            gvec_ref[n : n + 1, :] = jnp.sum(sums[n], 0, keepdims=True)
        for j in range(hidden_units):
            gvec_ref[8 + j : 9 + j, :] = jnp.sum(
                sums1[:, feat * j : feat * j + feat], 0, keepdims=True
            )
    out_copy.wait()
    gin_copy.wait()


def layer_call(linked, dp, sources, tokens, cotangent, keep, *rest):
    images, length, feat = tokens.shape
    padded = -(-length // 16) * 16
    hidden = 4 * feat
    rows = images * padded
    vmem = pl.BlockSpec(memory_space=pltpu.VMEM)
    anywhere = pl.BlockSpec(memory_space=pl.ANY)
    smem = pl.BlockSpec(memory_space=pltpu.SMEM)
    shape = jax.ShapeDtypeStruct
    outs = [shape((images, length, feat), BF16), shape((images, length, feat), F32)]
    weights = [
        pltpu.VMEM((feat, PAIRS * feat), BF16),
        pltpu.VMEM((feat, feat), BF16),
        pltpu.VMEM((feat, hidden), BF16),
        pltpu.VMEM((hidden, feat), BF16),
        pltpu.VMEM((16, feat), F32),
    ]
    if linked:
        layers = dp // PLANE
        width = -(-sources // 128) * 128
        in_specs = [anywhere, anywhere, vmem, smem] + [vmem] * 5
        outs += [shape((UNITS, 24, feat), F32), shape((16, 128), F32)]
        copies = 4 * (layers - 1 + PLANE - 1 + 1) + 2 * (layers + PLANE - 2) + 1
        copies += 4 * (1 + layers - 1 + PLANE - 1 + 1) + layers + PLANE - 1
        links = [
            pltpu.VMEM((UNITS, PLANE, layers, 24, feat), BF16),
            pltpu.VMEM((PLANE, layers, 16, 128), BF16),
            pltpu.VMEM((32, width), F32),
            pltpu.VMEM((9, 8, width), F32),
            pltpu.VMEM((UNITS // 2, PLANE, layers, 24, feat), BF16),
            pltpu.VMEM((PLANE - 1, UNITS // 2, layers, 24, feat), BF16),
            pltpu.VMEM((UNITS // 2, layers, 24, feat), BF16),
            pltpu.VMEM((layers - 1, UNITS // 2, 24, feat), BF16),
            pltpu.VMEM((4, 16, feat), F32),
            pltpu.VMEM((9, 16, feat), F32),
            pltpu.VMEM((UNITS, 24, feat), F32),
            pltpu.SemaphoreType.DMA((copies,)),
            pltpu.SemaphoreType.DMA((copies,)),
        ]
    else:
        in_specs = [anywhere, anywhere] + [vmem] * 7
        outs += [shape(w.shape, F32) for w in rest[1:]]
        weights, links = [], []
    params = dict(vmem_limit_bytes=64 * 1024 * 1024)
    if linked:
        params.update(collective_id=0, has_side_effects=True)
    return pl.pallas_call(
        functools.partial(layer_kernel, linked, dp, sources),
        out_shape=outs,
        in_specs=in_specs,
        out_specs=[anywhere, anywhere] + [vmem] * (len(outs) - 2),
        scratch_shapes=weights
        + links
        + [
            pltpu.VMEM((images, length, feat), BF16),
            pltpu.VMEM((rows, feat), BF16),
            pltpu.VMEM((rows, feat), BF16),
            pltpu.VMEM((rows, PAIRS * feat), BF16),
            pltpu.VMEM((PAIRS, images, 2 * padded, padded), BF16),
            pltpu.VMEM((rows, feat), BF16),
            pltpu.VMEM((rows, feat), F32),
            pltpu.VMEM((rows, feat), BF16),
            pltpu.VMEM((rows, hidden), BF16),
            pltpu.VMEM((rows, hidden), BF16),
            pltpu.VMEM((rows, feat), BF16),
            pltpu.VMEM((rows, feat), BF16),
            pltpu.VMEM((images, 2 * padded, padded), BF16),
            pltpu.VMEM((8, 8, feat), F32),
            pltpu.VMEM((8, hidden), F32),
            pltpu.VMEM((8, hidden), F32),
            pltpu.VMEM((images, length, feat), BF16),
            pltpu.VMEM((images, length, feat), F32),
            pltpu.VMEM((16, 256), F32),
            pltpu.VMEM((16, 256), F32),
            pltpu.SemaphoreType.DMA((4,)),
        ],
        compiler_params=pltpu.CompilerParams(**params),
        name="layer",
    )(tokens, cotangent, keep, *rest)


def adamw(master, first, second, gradient, step_rate, weight_decay):
    first_new = 0.9 * first + 0.1 * gradient
    second_new = 0.999 * second + 0.001 * gradient * gradient
    step_size = first_new / (1.0 - 0.9**STEP) / (jnp.sqrt(second_new / (1.0 - 0.999**STEP)) + 1e-08)
    return (first_new, second_new, master - step_rate * (step_size + weight_decay * master))


def step_kernel(share_ref, vshare_ref, *refs):
    state, outs = refs[:15], refs[15:]
    feat = share_ref.shape[2]

    def update(n, here, gradient):
        new = adamw(
            state[n][here], state[5 + n][here], state[10 + n][here], gradient, step_rates[n], decays[n]
        )
        for k in range(3):
            outs[3 * n + k][here] = new[k]

    everything = slice(None)
    for u in range(PAIRS):
        for n in range(3):
            first = n * feat + 128 * u
            update(0, (everything, slice(first, first + 128)), share_ref[u, :, 128 * n : 128 * n + 128])
    update(1, (everything, everything), share_ref[3])
    for j in range(4):
        update(2, (everything, slice(feat * j, feat * j + feat)), share_ref[4 + j])
        rows = share_ref.shape[1]
        update(3, (slice(rows * j, rows * j + rows), everything), share_ref[8 + j])
    vec = state[4]
    update(4, (everything, everything), vshare_ref[0 : vec.shape[0], 0 : vec.shape[1]])


def step_call(share, vshare, states):
    vmem = pl.BlockSpec(memory_space=pltpu.VMEM)
    shape = jax.ShapeDtypeStruct
    return pl.pallas_call(
        step_kernel,
        out_shape=[shape(states[n].shape, F32) for n in range(5) for _ in range(3)],
        in_specs=[vmem] * 17,
        out_specs=[vmem] * 15,
        name="step",
    )(share, vshare, *states)


def by_pair(weight):
    rows, cols = weight.shape
    return weight.reshape(rows, 3, PAIRS, 128).transpose(0, 2, 1, 3).reshape(rows, cols)


def from_pairs(grad):
    rows, cols = grad.shape
    return grad.reshape(rows, PAIRS, 3, 128).transpose(0, 2, 1, 3).reshape(rows, cols)


def on_device(tokens, cotangent, keep_mask, source, *states):
    masters = states[:5]
    dp = lax.axis_size("dp")
    images, length, feat = tokens.shape
    sources = images * lax.axis_size("head") * dp // 3
    if dp == 16:
        layer_out, input_grad, share, vshare = layer_call(
            True, dp, sources, tokens, cotangent, keep_mask, source, *masters
        )
        return (layer_out, input_grad, *step_call(share, vshare, states))
    gather = functools.partial(lax.all_gather, axis_name="dp", tiled=True)
    low = [master.astype(BF16) for master in masters]
    w_qkv, w_proj, w_fc1, w_fc2 = (gather(w, axis=0) for w in low[:4])
    vectors = gather(low[4], axis=1).astype(F32)
    live_mask = keep_mask.astype(F32)
    kept_rows = jnp.sum(live_mask, 1)
    onehot = (source[:, None] == jnp.arange(sources, dtype=jnp.int32)[None, :]).astype(F32)
    totals = lax.psum(jnp.sum(onehot * kept_rows[:, None], 0), ("dp", "head"))
    image_total = jnp.sum(onehot * totals[None, :], 1)
    token_weight = live_mask * (length / image_total)[:, None]
    layer_out, input_grad, gq, gp, g1, g2, gvec = layer_call(
        False, dp, sources, tokens, cotangent, keep_mask,
        token_weight, by_pair(w_qkv), w_proj, w_fc1, w_fc2, vectors,
    )
    gradients = (from_pairs(gq), gp, g1, g2, gvec)
    dims = (0, 0, 0, 0, 1)
    shares = [
        lax.psum_scatter(
            lax.psum(g.astype(BF16), "head").astype(F32), "dp", scatter_dimension=d, tiled=True
        )
        for g, d in zip(gradients, dims)
    ]
    new = []
    for n in range(5):
        new.extend(
            adamw(masters[n], states[5 + n], states[10 + n], shares[n], step_rates[n], decays[n])
        )
    return (layer_out, input_grad, *new)


def solution(mesh):
    split = P(("dp", "head"), None, None)
    rows, cols = P("dp", None), P(None, "dp")
    weights = (rows, rows, rows, rows, cols)
    return jax.shard_map(
        on_device,
        mesh=mesh,
        in_specs=(split, split, P(("dp", "head"), None), P(("dp", "head"))) + weights * 3,
        out_specs=(split, split) + (rows,) * 12 + (cols,) * 3,
        check_vma=False,
    )
```

```python
import functools

import jax
import jax.numpy as jnp
from jax import lax
from jax.experimental import pallas as pl
from jax.experimental.pallas import tpu as pltpu
from jax.sharding import PartitionSpec as P

HEADS = 6
HEAD_DIM = 64
STEP = 10
PAIRS = HEADS // 2
SCALE = HEAD_DIM ** (-0.5)

norm_eps = 1e-06
step_rates = (0.1, 0.4, 0.1, 0.05, 0.5)
decays = (0.05, 0.05, 0.05, 0.05, 0.0)

UNITS = 12
PLANE = 4
SHARD = 24

ROW_PROJ, ROW_FC2, ROW_FC1, SUM_ROWS = 3, 4, 5, 16

F32 = jnp.float32
BF16 = jnp.bfloat16


def dot(left, right):
    return lax.dot_general(left, right, (((1,), (0,)), ((), ())), preferred_element_type=F32)


def across(left, right):
    return lax.dot_general(left, right, (((0,), (0,)), ((), ())), preferred_element_type=F32)


def against(left, right):
    return lax.dot_general(left, right, (((1,), (1,)), ((), ())), preferred_element_type=F32)


def normalise(values):
    average = jnp.mean(values, -1, keepdims=True)
    centred = values - average
    variance = jnp.mean(centred * centred, -1, keepdims=True)
    inverse = lax.rsqrt(variance + norm_eps)
    return centred * inverse, inverse


def norm_back(grad, unit, inverse, gain_row):
    scaled = grad * gain_row
    first = jnp.mean(scaled, -1, keepdims=True)
    second = jnp.mean(scaled * unit, -1, keepdims=True)
    return inverse * (scaled - first - unit * second)


def fold(values):
    rows, cols = values.shape
    return jnp.sum(values.reshape(rows // 8, 8, cols), 0)


LOG2E_HALF = 0.7213475204444817
INV_SQRT_2PI = 0.3989422804014327


def gelu_parts(x):
    cdf = 0.5 + 0.5 * lax.erf(x * 0.7071067811865476)
    bell = jnp.exp2(x * x * (-LOG2E_HALF)) * INV_SQRT_2PI
    return x * cdf, cdf + x * bell


def layer_kernel(linked, dp, sources, *refs):
    refs = list(refs)

    def take(count):
        taken = refs[:count]
        del refs[:count]
        return taken

    tok_hbm, cot_hbm, keep_ref = take(3)
    if linked:
        src_ref, qm_ref, pm_ref, f1_ref, f2_ref, vm_ref = take(6)
        out_hbm, gin_hbm, share_ref, vsum_ref = take(4)
        wq_ref, wp_ref, w1_ref, w2_ref, vec_ref = take(5)
        slabs, vslabs, tot_mine, tot_in, pair_in, plane_in, layer_out, layer_in, layer_in2 = take(9)
        vsum, vin, share_in, send, recv = take(5)
    else:
        tw_ref, wq_ref, wp_ref, w1_ref, w2_ref, vec_ref = take(6)
        out_hbm, gin_hbm, gq_ref, gp_ref, g1_ref, g2_ref, vsum_ref = take(7)
    cot, xs, normed, qkv, probs, att, middle, nmid, act, gel, gol, gml, dsc = take(13)
    sums, sums1, b1, outs, gins, keepf, tws, local = take(8)

    images, length, feat = cot.shape
    padded = xs.shape[0] // images
    hidden = act.shape[1]
    hidden_units = hidden // feat
    group = 3 if images % 3 == 0 else 1
    blocks = images // group
    chunk = 256
    half = hidden // 2
    lane = lax.broadcasted_iota(jnp.int32, (padded, 128), 1)
    low_half = lane < HEAD_DIM

    def image_rows(i):
        return pl.ds(pl.multiple_of(i * padded, padded), padded)

    def real_rows(i):
        return pl.ds(pl.multiple_of(i * padded, padded), length)

    def each_block(body, first=0, last=None):
        def step(t, carry):
            rows = pl.ds(pl.multiple_of(t * group * padded, padded), group * padded)
            body(rows, [t * group + k for k in range(group)])
            return carry

        lax.fori_loop(first, blocks if last is None else last, step, 0)

    def row(n):
        return vec_ref[n : n + 1, :]

    def stacked_halves(values):
        zero = jnp.zeros_like(values)
        return jnp.concatenate(
            [jnp.where(low_half, values, zero), jnp.where(low_half, zero, values)], 0
        )

    def merged_halves(values):
        return jnp.where(low_half, values[:padded], values[padded:])

    tok_in = pltpu.make_async_copy(tok_hbm, outs, local.at[0])
    cot_in = pltpu.make_async_copy(cot_hbm, cot, local.at[1])
    out_copy = pltpu.make_async_copy(outs, out_hbm, local.at[2])
    gin_copy = pltpu.make_async_copy(gins, gin_hbm, local.at[3])
    tok_in.start()
    cot_in.start()

    if linked:
        me = lax.axis_index("dp")
        core = lax.axis_index("head")
        layers = dp // PLANE
        layer, place = me // PLANE, me % PLANE
        counter = [0]
        started = []

        def peers(kind):
            if kind == "layer":
                return [(((layer + r) % layers) * PLANE + place, core) for r in range(1, layers)]
            if kind == "cross":
                return [
                    (((layer + r) % layers) * PLANE + place, 1 - core) for r in range(1, layers)
                ]
            if kind == "plane":
                return [(layer * PLANE + (place + r) % PLANE, core) for r in range(1, PLANE)]
            return [(me, 1 - core)]

        def push(kind, pick):
            copies = []
            for r, device in enumerate(peers(kind), 1):
                src, dst = pick(r)
                k = counter[0]
                counter[0] += 1
                copy = pltpu.make_async_remote_copy(
                    src_ref=src,
                    dst_ref=dst,
                    send_sem=send.at[k],
                    recv_sem=recv.at[k],
                    device_id=device,
                    device_id_type=pl.DeviceIdType.MESH,
                )
                copy.start()
                copies.append(copy)
            started.extend(copies)
            return copies

        def arrive(copies):
            for copy in copies:
                copy.wait_recv()

        barrier = pltpu.get_barrier_semaphore()
        everyone = peers("layer") + peers("plane") + peers("core") + peers("cross")
        for device in everyone:
            pl.semaphore_signal(
                barrier, inc=1, device_id=device, device_id_type=pl.DeviceIdType.MESH
            )

        def own_block(u):
            if u < PAIRS:
                parts = [qm_ref[:, n * feat + 128 * u : n * feat + 128 * u + 128] for n in range(3)]
                return jnp.concatenate(parts, 1)
            if u == 3:
                return pm_ref[...]
            if u < 8:
                return f1_ref[:, feat * (u - 4) : feat * (u - 3)]
            return f2_ref[SHARD * (u - 8) : SHARD * (u - 7), :]

        def own_slab(u, other):
            slabs[u + (other - u) * core, place, layer] = jnp.where(
                core == 0, own_block(u), own_block(other)
            ).astype(BF16)

        def vec_push(kind):
            if kind == "layer":
                return push(kind, lambda r: (vslabs.at[place, layer],) * 2)
            return push(kind, lambda r: (vslabs.at[place],) * 2)

        def tot_push(kind, stage):
            part = pl.ds(8 * stage, 8)
            return push(kind, lambda r: (tot_mine.at[part], tot_in.at[3 * stage + r - 1]))

        def tot_sum(stage, count):
            total = tot_mine[8 * stage : 8 * stage + 8]
            for r in range(count):
                total = total + tot_in[3 * stage + r]
            tot_mine[8 * stage + 8 : 8 * stage + 16] = total

        def step_units(step):
            return (pl.ds(core, 1), pl.ds(2 + core, 1), pl.ds(4 + 2 * core, 2), pl.ds(8 + 2 * core, 2))[
                step
            ]

        def weights_push(step, kind):
            units = step_units(step)
            if kind == "layer":
                return push(kind, lambda r: (slabs.at[units, place, layer],) * 2)
            if kind == "plane":
                return push(kind, lambda r: (slabs.at[units, place],) * 2)
            return push(kind, lambda r: (slabs.at[units],) * 2)

        def two_shards(first, second):
            return jnp.concatenate([first.astype(F32), second.astype(F32)], 0).astype(BF16)

        def assemble(u):
            for q in range(layers):
                for k in range(0, PLANE, 2):
                    both = two_shards(slabs[u, k, q], slabs[u, k + 1, q])
                    first = SHARD * (PLANE * q + k)
                    rows = slice(first, first + 2 * SHARD)
                    if u < PAIRS:
                        wq_ref[rows, feat * u : feat * u + feat] = both
                    elif u == 3:
                        wp_ref[rows, :] = both
                    else:
                        w1_ref[rows, feat * (u - 4) : feat * (u - 3)] = both

        def assemble_w2():
            for q in range(layers):
                for k in range(PLANE):
                    for j in range(0, 4, 2):
                        first = 4 * SHARD * (PLANE * q + k) + SHARD * j
                        w2_ref[first : first + 2 * SHARD, :] = two_shards(
                            slabs[8 + j, k, q], slabs[9 + j, k, q]
                        )

        def spread(values, owner):
            lanes = lax.broadcasted_iota(jnp.int32, (16, 128), 1)
            shift = (SHARD * owner) % 128
            moved = pltpu.roll(values, shift, 1) if shift else values
            block = SHARD * owner // 128
            here = jnp.where(lanes >= shift, moved, 0.0)
            vec_ref[:, 128 * block : 128 * block + 128] += here
            if shift + SHARD > 128:
                rest = jnp.where(lanes < shift, moved, 0.0)
                vec_ref[:, 128 * block + 128 : 128 * block + 256] += rest

        vslabs[place, layer] = jnp.zeros((16, 128), BF16)
        vslabs[place, layer, 0:12, 0:SHARD] = vm_ref[...].astype(BF16)
        own_slab(0, 1)
        kept = jnp.sum(keep_ref[...].astype(F32), 1, keepdims=True)
        width = tot_mine.shape[1]
        source_lane = lax.broadcasted_iota(jnp.int32, (1, width), 1)
        mine = jnp.zeros((1, width), F32)
        for i in range(images):
            mine = mine + jnp.where(source_lane == src_ref[i], kept[i : i + 1], 0.0)
        tot_mine[0:8] = jnp.broadcast_to(mine, (8, width))
        pl.semaphore_wait(barrier, len(everyone))
        vec_go = vec_push("layer")
        go0 = weights_push(0, "layer")
        tot_go = tot_push("layer", 0)
        own_slab(2, 3)
        go1 = weights_push(1, "layer")
        for pair in ((4, 6), (5, 7), (8, 10), (9, 11)):
            own_slab(*pair)

    for i in range(images):
        tail = slice(padded * (i + 1) - 16, padded * (i + 1))
        xs[tail, :] = jnp.zeros((16, feat), BF16)
        gol[tail, :] = jnp.zeros((16, feat), BF16)
    sums[...] = jnp.zeros_like(sums)
    sums1[...] = jnp.zeros_like(sums1)
    keepf[...] = jnp.zeros_like(keepf)
    keepf[0:images, 0:length] = keep_ref[...].astype(F32)

    def first_norm(_, block):
        for i in block:
            xs[real_rows(i), :] = outs[i]
            unit, _ = normalise(xs[image_rows(i), :].astype(F32))
            middle[image_rows(i), :] = unit

    def first_scale(rows, _):
        normed[rows, :] = (middle[rows, :] * row(0) + row(1)).astype(BF16)

    tok_in.wait()
    each_block(first_norm)

    if linked:
        arrive(vec_go)
        vec_go = vec_push("plane")
        arrive(go0)
        go0 = weights_push(0, "plane")
        arrive(tot_go)
        tot_sum(0, layers - 1)
        tot_go = tot_push("plane", 1)
        arrive(vec_go)
        vec_ref[...] = jnp.zeros_like(vec_ref)
        for owner in range(dp):
            spread(vslabs[owner % PLANE, owner // PLANE].astype(F32), owner)

    for j in range(hidden_units):
        b1[0:1, feat * j : feat * j + feat] = row(8 + j)
    each_block(first_scale)

    if linked:
        arrive(go1)
        arrive(go0)
        go0 = weights_push(0, "core")
        go1 = weights_push(1, "plane")
        go2 = weights_push(2, "layer")
        arrive(tot_go)
        tot_sum(1, PLANE - 1)
        tot_go = tot_push("core", 2)
        arrive(go0)
        assemble(0)
        assemble(1)

    def project(first, last):
        cols = slice(feat * first, feat * last)
        parts = []
        for h in range(first, last):
            part = pl.ds(128 * h, 128)
            parts += [vec_ref[2:3, part], jnp.zeros((1, 128), F32), vec_ref[3:4, part]]
        bias = jnp.concatenate(parts, 1)

        def body(rows, _):
            qkv[rows, cols] = (dot(normed[rows, :], wq_ref[:, cols]) + bias).astype(BF16)

        each_block(body)

    def attend(h):
        first = feat * h
        results = []
        for i in range(images):
            rows = image_rows(i)
            alive = keepf[i : i + 1, 0:padded] > 0
            query = stacked_halves(qkv[rows, first : first + 128] * BF16(SCALE))
            scores = against(query, qkv[rows, first + 128 : first + 256])
            scores = jnp.where(alive, scores, -1e9)
            top = jnp.max(scores, -1, keepdims=True)
            raised = jnp.exp(scores - top)
            share = raised * (1.0 / jnp.sum(raised, -1, keepdims=True))
            share = share.astype(BF16)
            mixed = dot(share, qkv[rows, first + 256 : first + 384])
            results.append((share, merged_halves(mixed).astype(BF16)))
        for i, (share, mixed) in enumerate(results):
            probs[h, i] = share
            att[image_rows(i), 128 * h : 128 * h + 128] = mixed

    project(0, 2)
    attend(0)
    if linked:
        arrive(go2)
        go2 = weights_push(2, "plane")
        go3 = weights_push(3, "layer")
        arrive(go1)
        go1 = weights_push(1, "core")
    attend(1)
    if linked:
        arrive(go1)
        assemble(2)
        assemble(3)
    project(2, 3)
    attend(2)
    if linked:
        arrive(go3)
        go3 = weights_push(3, "plane")

    def second_norm(rows, block):
        middle[rows, :] = xs[rows, :].astype(F32) + (dot(att[rows, :], wp_ref[...]) + row(4))
        for i in block:
            unit, _ = normalise(middle[image_rows(i), :])
            nmid[image_rows(i), :] = (unit * row(5) + row(6)).astype(BF16)

    each_block(second_norm)
    if linked:
        arrive(go2)
        go2 = weights_push(2, "core")

    if linked:
        arrive(tot_go)
        tot_sum(2, 1)
        totals = tot_mine[24:25]
        for i in range(images):
            total = jnp.sum(
                jnp.where(source_lane == src_ref[i], totals, 0.0), 1, keepdims=True
            )
            tws[i : i + 1] = keepf[i : i + 1] * (length / total)
    else:
        tws[...] = jnp.zeros_like(tws)
        tws[0:images, 0:length] = tw_ref[...]
    eye = lax.broadcasted_iota(jnp.int32, (padded, padded), 0) == lax.broadcasted_iota(
        jnp.int32, (padded, padded), 1
    )

    def weigh(_, block):
        for i in block:
            weight_row = tws[pl.ds(i, 1), 0:padded]
            column = jnp.sum(jnp.where(eye, weight_row, 0.0), 1, keepdims=True)
            grad = cot[i].astype(F32) * column[:length]
            gins[i] = grad
            gol[real_rows(i), :] = grad.astype(BF16)

    cot_in.wait()
    each_block(weigh)

    if linked:
        arrive(go2)
        for u in range(4, 8):
            assemble(u)

    def expand(rows, _):
        values = nmid[rows, :]
        for j in range(hidden // chunk):
            cols = slice(chunk * j, chunk * j + chunk)
            active, slope = gelu_parts(dot(values, w1_ref[:, cols]) + b1[0:1, cols])
            act[rows, cols] = active.astype(BF16)
            gel[rows, cols] = slope.astype(BF16)

    each_block(expand, 0, blocks - 1)
    if linked:
        arrive(go3)
        go3 = weights_push(3, "core")
    each_block(expand, blocks - 1, blocks)
    if linked:
        arrive(go3)
        assemble_w2()
        for copy in started:
            copy.wait_send()
        started.clear()

    def hidden_back(rows, _):
        grad = gol[rows, :]
        sums[ROW_FC2] += fold(grad.astype(F32))
        for j in range(hidden // chunk):
            cols = slice(chunk * j, chunk * j + chunk)
            back = against(grad, w2_ref[cols, :]) * gel[rows, cols].astype(F32)
            back = back.astype(BF16)
            gel[rows, cols] = back
            sums1[:, cols] += fold(back.astype(F32))

    each_block(hidden_back)

    if linked:
        slots = ((0, 2), (2, 4), (4, 5), (5, 6))

        def first_unit(job, owner):
            return (8 + 2 * owner, 4 + 2 * owner, 2 + owner, owner)[job]

        def job_units(job, owner):
            first, last = slots[job]
            return pl.ds(first_unit(job, owner), last - first)

        def job_slots(job):
            first, last = slots[job]
            return pl.ds(first, last - first)

        def emit(u, grad):
            for owner in range(dp):
                slabs[u, owner % PLANE, owner // PLANE] = grad[
                    SHARD * owner : SHARD * owner + SHARD
                ].astype(BF16)

        def grads_pair(job):
            theirs = job_units(job, 1 - core)
            return push("core", lambda r: (slabs.at[theirs], pair_in.at[job_slots(job)]))

        def grads_plane(job):
            first, last = slots[job]
            for s in range(first, last):
                unit = first_unit(job, core) + (s - first)
                for k in range(PLANE):
                    for q in range(layers):
                        slabs[unit, k, q] = (
                            slabs[unit, k, q].astype(F32) + pair_in[s, k, q].astype(F32)
                        ).astype(BF16)
            units = job_units(job, core)
            return push(
                "plane",
                lambda r: (
                    slabs.at[units, (place + r) % PLANE],
                    plane_in.at[r - 1, job_slots(job)],
                ),
            )

        def grads_layer(job, both=False):
            first, last = slots[job]
            for s in range(first, last):
                unit = first_unit(job, core) + (s - first)
                for q in range(layers):
                    total = slabs[unit, place, q].astype(F32)
                    for r in range(PLANE - 1):
                        total = total + plane_in[r, s, q].astype(F32)
                    layer_out[s, q] = total.astype(BF16)
            size = job_slots(job)
            there = lambda r: layer_out.at[size, (layer + r) % layers]
            copies = push("layer", lambda r: (there(r), layer_in.at[r - 1, size]))
            if both:
                copies += push("cross", lambda r: (there(r), layer_in2.at[pl.ds(r, 1)]))
                copies += push("core", lambda r: (layer_out.at[size, layer], layer_in2.at[pl.ds(0, 1)]))
            return copies

        def grads_share(job, both=False):
            first, last = slots[job]
            for s in range(first, last):
                total = layer_out[s, layer].astype(F32)
                for r in range(layers - 1):
                    total = total + layer_in[r, s].astype(F32)
                share_in[first_unit(job, core) + (s - first)] = total
            if both:
                total = layer_in2[0].astype(F32)
                for r in range(1, layers):
                    total = total + layer_in2[r].astype(F32)
                share_in[first_unit(job, 1 - core)] = total
                return []
            units = job_units(job, core)
            return push("core", lambda r: (share_in.at[units], share_in.at[units]))

        shares = []

    for n in range(2):
        grad = across(act[:, half * n : half * n + half], gol[...])
        if linked:
            for k in range(dp // 2):
                owner = n * dp // 2 + k
                for j in range(4):
                    first = 4 * SHARD * k + SHARD * j
                    slabs[8 + j, owner % PLANE, owner // PLANE] = grad[
                        first : first + SHARD
                    ].astype(BF16)
        else:
            g2_ref[half * n : half * n + half, :] = grad
    if linked:
        job0 = grads_pair(0)

    def middle_back(rows, block):
        grads = against(gel[rows, :], w1_ref[...])
        for k, i in enumerate(block):
            here = image_rows(i)
            grad = grads[padded * k : padded * k + padded]
            kept_middle = middle[here, :]
            unit, inverse = normalise(kept_middle)
            middle[here, :] = norm_back(grad, unit, inverse, row(5))
            middle[real_rows(i), :] += gins[i]
            gins[i] = kept_middle[:length]
            low = middle[here, :].astype(BF16)
            gml[here, :] = low
            sums[ROW_PROJ] += fold(low.astype(F32))

    each_block(middle_back, 0, 1)
    if linked:
        arrive(job0)
        job0 = grads_plane(0)
    each_block(middle_back, 1, blocks)

    for n in range(2):
        grad = across(nmid[...], gel[:, half * n : half * n + half])
        if linked:
            emit(4 + 2 * n, grad[:, 0:feat])
            emit(5 + 2 * n, grad[:, feat:])
        else:
            g1_ref[:, half * n : half * n + half] = grad
    if linked:
        job1 = grads_pair(1)

    grad = across(att[...], gml[...])
    if linked:
        emit(3, grad)
        arrive(job1)
        job1 = grads_plane(1)
    else:
        gp_ref[...] = grad

    def grad_attended(rows, _):
        att[rows, :] = against(gml[rows, :], wp_ref[...]).astype(BF16)

    each_block(grad_attended)

    def attend_back(h):
        first = feat * h
        part = slice(128 * h, 128 * h + 128)
        results = []
        for i in range(images):
            rows = image_rows(i)
            grad = stacked_halves(att[rows, part])
            share = probs[h, i].astype(F32)
            grad_share = against(grad, qkv[rows, first + 256 : first + 384])
            inner = jnp.sum(share * grad_share, -1, keepdims=True)
            grad_score = (share * (grad_share - inner)).astype(BF16)
            key = qkv[rows, first + 128 : first + 256]
            grad_query = (merged_halves(dot(grad_score, key)) * SCALE).astype(BF16)
            results.append((grad_score, grad_query))
        for i, (grad_score, _) in enumerate(results):
            dsc[i] = grad_score
        results = [grad_query for _, grad_query in results]
        for i in range(images):
            rows = image_rows(i)
            query = stacked_halves(qkv[rows, first : first + 128] * BF16(SCALE))
            grad = stacked_halves(att[rows, part])
            grad_key = across(dsc[i], query).astype(BF16)
            grad_value = across(probs[h, i], grad).astype(BF16)
            for n, moved in enumerate((results[i], grad_key, grad_value)):
                qkv[rows, first + 128 * n : first + 128 * n + 128] = moved
                sums[n, :, part] += fold(moved.astype(F32))

    def qkv_grad(first, last):
        cols = slice(feat * first, feat * last)
        grad = across(normed[...], qkv[:, cols])
        for h in range(first, last):
            part = grad[:, feat * (h - first) : feat * (h - first + 1)]
            if linked:
                emit(h, part)
            else:
                gq_ref[:, feat * h : feat * h + feat] = part

    attend_back(2)
    if linked:
        arrive(job0)
        job0 = grads_layer(0)
    qkv_grad(2, 3)
    if linked:
        job2 = grads_pair(2)
    attend_back(1)
    if linked:
        arrive(job1)
        job1 = grads_layer(1)
        arrive(job2)
        job2 = grads_plane(2)
    attend_back(0)
    qkv_grad(0, 2)

    def column_sums(out):
        out[...] = jnp.zeros(out.shape, F32)
        for n in range(ROW_FC1):
            out[n : n + 1, :] = jnp.sum(sums[n], 0, keepdims=True)
        for j in range(hidden_units):
            out[ROW_FC1 + j : ROW_FC1 + j + 1, :] = jnp.sum(
                sums1[:, feat * j : feat * j + feat], 0, keepdims=True
            )

    def sums_push(stage, kind):
        return push(kind, lambda r: (vsum.at[stage], vin.at[3 * stage + r - 1]))

    def sums_add(stage, count):
        total = vsum[stage]
        for r in range(count):
            total = total + vin[3 * stage + r]
        vsum[stage + 1] = total

    def contract(rows, block):
        total = dot(act[rows, :], w2_ref[...]) + row(7)
        for k, i in enumerate(block):
            outs[i] = (gins[i] + total[padded * k : padded * k + length]).astype(BF16)

    def input_back(rows, block):
        grads = against(qkv[rows, :], wq_ref[...])
        for k, i in enumerate(block):
            here = image_rows(i)
            unit, inverse = normalise(xs[here, :].astype(F32))
            back = norm_back(grads[padded * k : padded * k + padded], unit, inverse, row(0))
            gins[i] = (middle[here, :] + back)[:length]

    if linked:
        job3 = grads_pair(3)
        column_sums(vsum.at[0])
        vec_go = sums_push(0, "core")
        each_block(contract, 0, 1)
        arrive(job3)
        job3 = grads_plane(3)
        arrive(vec_go)
        sums_add(0, 1)
        vec_go = sums_push(1, "plane")
        arrive(job0)
        shares.append(grads_share(0))
        arrive(job2)
        job2 = grads_layer(2)
        each_block(contract, 1, blocks)
        out_copy.start()
        arrive(job1)
        shares.append(grads_share(1))
        arrive(job3)
        job3 = grads_layer(3, both=True)
        arrive(vec_go)
        sums_add(1, PLANE - 1)
        vec_go = sums_push(2, "layer")
        each_block(input_back)
        gin_copy.start()
        arrive(job2)
        shares.append(grads_share(2))
        arrive(job3)
        shares.append(grads_share(3, both=True))
        arrive(vec_go)
        sums_add(2, layers - 1)
        vsum_ref[...] = vsum[3]
        for copies in shares:
            arrive(copies)
        share_ref[...] = share_in[...]
        for copy in started:
            copy.wait_send()
    else:
        each_block(contract)
        out_copy.start()
        each_block(input_back)
        gin_copy.start()
        column_sums(vsum_ref)
    out_copy.wait()
    gin_copy.wait()


def layer_call(linked, dp, sources, tokens, cotangent, keep, *rest):
    images, length, feat = tokens.shape
    padded = -(-length // 16) * 16
    hidden = 4 * feat
    rows = images * padded
    vmem = pl.BlockSpec(memory_space=pltpu.VMEM)
    anywhere = pl.BlockSpec(memory_space=pl.ANY)
    smem = pl.BlockSpec(memory_space=pltpu.SMEM)
    shape = jax.ShapeDtypeStruct
    outs = [shape((images, length, feat), BF16), shape((images, length, feat), F32)]
    weights, links = [], []
    params = dict(vmem_limit_bytes=64 * 1024 * 1024)
    if linked:
        layers = dp // PLANE
        width = -(-sources // 128) * 128
        in_specs = [anywhere, anywhere, vmem, smem] + [vmem] * 5
        outs += [shape((UNITS, SHARD, feat), F32), shape((SUM_ROWS, feat), F32)]
        along, beside = layers - 1, PLANE - 1
        copies = 4 * (along + beside + 1) + (along + beside) + (along + beside + 1)
        copies += 4 * (1 + beside + along) + 3 + (along + 1) + (1 + beside + along)
        weights = [
            pltpu.VMEM((feat, PAIRS * feat), BF16),
            pltpu.VMEM((feat, feat), BF16),
            pltpu.VMEM((feat, hidden), BF16),
            pltpu.VMEM((hidden, feat), BF16),
            pltpu.VMEM((16, feat), F32),
        ]
        links = [
            pltpu.VMEM((UNITS, PLANE, layers, SHARD, feat), BF16),
            pltpu.VMEM((PLANE, layers, 16, 128), BF16),
            pltpu.VMEM((32, width), F32),
            pltpu.VMEM((9, 8, width), F32),
            pltpu.VMEM((UNITS // 2, PLANE, layers, SHARD, feat), BF16),
            pltpu.VMEM((beside, UNITS // 2, layers, SHARD, feat), BF16),
            pltpu.VMEM((UNITS // 2, layers, SHARD, feat), BF16),
            pltpu.VMEM((along, UNITS // 2, SHARD, feat), BF16),
            pltpu.VMEM((layers, SHARD, feat), BF16),
            pltpu.VMEM((4, SUM_ROWS, feat), F32),
            pltpu.VMEM((9, SUM_ROWS, feat), F32),
            pltpu.VMEM((UNITS, SHARD, feat), F32),
            pltpu.SemaphoreType.DMA((copies,)),
            pltpu.SemaphoreType.DMA((copies,)),
        ]
        params.update(collective_id=0, has_side_effects=True)
    else:
        in_specs = [anywhere, anywhere] + [vmem] * 7
        outs += [shape(w.shape, F32) for w in rest[1:5]] + [shape((SUM_ROWS, feat), F32)]
    return pl.pallas_call(
        functools.partial(layer_kernel, linked, dp, sources),
        out_shape=outs,
        in_specs=in_specs,
        out_specs=[anywhere, anywhere] + [vmem] * (len(outs) - 2),
        scratch_shapes=weights
        + links
        + [
            pltpu.VMEM((images, length, feat), BF16),
            pltpu.VMEM((rows, feat), BF16),
            pltpu.VMEM((rows, feat), BF16),
            pltpu.VMEM((rows, PAIRS * feat), BF16),
            pltpu.VMEM((PAIRS, images, 2 * padded, padded), BF16),
            pltpu.VMEM((rows, feat), BF16),
            pltpu.VMEM((rows, feat), F32),
            pltpu.VMEM((rows, feat), BF16),
            pltpu.VMEM((rows, hidden), BF16),
            pltpu.VMEM((rows, hidden), BF16),
            pltpu.VMEM((rows, feat), BF16),
            pltpu.VMEM((rows, feat), BF16),
            pltpu.VMEM((images, 2 * padded, padded), BF16),
            pltpu.VMEM((8, 8, feat), F32),
            pltpu.VMEM((8, hidden), F32),
            pltpu.VMEM((8, hidden), F32),
            pltpu.VMEM((images, length, feat), BF16),
            pltpu.VMEM((images, length, feat), F32),
            pltpu.VMEM((16, 256), F32),
            pltpu.VMEM((16, 256), F32),
            pltpu.SemaphoreType.DMA((4,)),
        ],
        compiler_params=pltpu.CompilerParams(**params),
        name="layer",
    )(tokens, cotangent, keep, *rest)


def adamw(master, first, second, gradient, step_rate, weight_decay):
    first_new = 0.9 * first + 0.1 * gradient
    second_new = 0.999 * second + 0.001 * gradient * gradient
    step_size = first_new / (1.0 - 0.9**STEP) / (jnp.sqrt(second_new / (1.0 - 0.999**STEP)) + 1e-08)
    return (first_new, second_new, master - step_rate * (step_size + weight_decay * master))


def norm_grads(products, weighted, gain, bias):
    return (products - bias * weighted) / gain, weighted


def step_kernel(out_tmp, gin_tmp, share_ref, vsum_ref, *refs):
    state, large, outs, held, (came, went) = refs[:15], refs[15:17], refs[17:32], refs[32:34], refs[34:]
    feat = share_ref.shape[2]
    images = out_tmp.shape[0]

    def moves(sources, targets, sems):
        return [
            pltpu.make_async_copy(sources[n].at[i], targets[n].at[i], sems.at[n, i])
            for i in range(images)
            for n in range(2)
        ]

    arrivals = moves((out_tmp, gin_tmp), held, came)
    departures = moves(held, large, went)
    for move in arrivals:
        move.start()

    def update(n, here, gradient):
        new = adamw(
            state[n][here], state[5 + n][here], state[10 + n][here], gradient, step_rates[n], decays[n]
        )
        for k in range(3):
            outs[3 * n + k][here] = new[k]

    def low(values):
        return values.astype(BF16).astype(F32)

    everything = slice(None)
    first_products = jnp.zeros((SHARD, 128), F32)
    first_weighted = jnp.zeros((SHARD, 128), F32)
    for u in range(PAIRS):
        for n in range(3):
            first = n * feat + 128 * u
            cols = slice(first, first + 128)
            grad = share_ref[u, :, 128 * n : 128 * n + 128]
            weight = low(state[0][:, cols])
            first_products += grad * weight
            first_weighted += weight * vsum_ref[n : n + 1, 128 * u : 128 * u + 128]
            update(0, (everything, cols), grad)
    update(1, (everything, everything), share_ref[3])
    second_products = jnp.zeros((SHARD, feat), F32)
    second_weighted = jnp.zeros((SHARD, feat), F32)
    for j in range(4):
        cols = slice(feat * j, feat * j + feat)
        weight = low(state[2][:, cols])
        second_products += share_ref[4 + j] * weight
        second_weighted += weight * vsum_ref[ROW_FC1 + j : ROW_FC1 + j + 1, :]
        update(2, (everything, cols), share_ref[4 + j])
        update(3, (slice(SHARD * j, SHARD * j + SHARD), everything), share_ref[8 + j])

    for arrival, departure in zip(arrivals, departures):
        arrival.wait()
        departure.start()

    me = lax.axis_index("dp")
    sums = vsum_ref[...]
    lanes = lax.broadcasted_iota(jnp.int32, (SUM_ROWS, 128), 1)
    mine = jnp.zeros((SUM_ROWS, 128), F32)
    for owner in range(16):
        shift = (SHARD * owner) % 128
        block = SHARD * owner // 128
        part = sums[:, 128 * block : 128 * block + 128]
        part = pltpu.roll(part, 128 - shift, 1) if shift else part
        if shift + SHARD > 128:
            rest = pltpu.roll(sums[:, 128 * block + 128 : 128 * block + 256], 128 - shift, 1)
            part = jnp.where(lanes < 128 - shift, part, rest)
        mine = jnp.where(me == owner, part, mine)
    mine = mine[:, 0:SHARD]
    eye = lax.broadcasted_iota(jnp.int32, (SHARD, SHARD), 0) == lax.broadcasted_iota(
        jnp.int32, (SHARD, SHARD), 1
    )

    def as_row(values):
        column = jnp.sum(values, 1, keepdims=True)
        return jnp.sum(jnp.where(eye, column, 0.0), 0, keepdims=True)

    vec = low(state[4][...])
    gain_first, shift_first = norm_grads(
        as_row(first_products), as_row(first_weighted), vec[0:1], vec[1:2]
    )
    gain_second, shift_second = norm_grads(
        as_row(second_products), as_row(second_weighted), vec[5:6], vec[6:7]
    )
    grads = [gain_first, shift_first, mine[0:1], mine[2:3], mine[ROW_PROJ : ROW_PROJ + 1]]
    grads += [gain_second, shift_second, mine[ROW_FC2 : ROW_FC2 + 1]]
    grads += [mine[ROW_FC1 + j : ROW_FC1 + j + 1] for j in range(4)]
    for n, grad in enumerate(grads):
        update(4, (slice(n, n + 1), everything), grad)
    for move in departures:
        move.wait()


def step_call(layer_out, input_grad, share, vsum, states):
    vmem = pl.BlockSpec(memory_space=pltpu.VMEM)
    anywhere = pl.BlockSpec(memory_space=pl.ANY)
    shape = jax.ShapeDtypeStruct
    large = [shape(a.shape, a.dtype) for a in (layer_out, input_grad)]
    return pl.pallas_call(
        step_kernel,
        out_shape=large + [shape(states[n].shape, F32) for n in range(5) for _ in range(3)],
        in_specs=[anywhere] * 2 + [vmem] * 17,
        out_specs=[anywhere] * 2 + [vmem] * 15,
        scratch_shapes=[pltpu.VMEM(a.shape, a.dtype) for a in (layer_out, input_grad)]
        + [pltpu.SemaphoreType.DMA((2, layer_out.shape[0]))] * 2,
        compiler_params=pltpu.CompilerParams(vmem_limit_bytes=64 * 1024 * 1024),
        name="step",
    )(layer_out, input_grad, share, vsum, *states)


def by_pair(weight):
    rows, cols = weight.shape
    return weight.reshape(rows, 3, PAIRS, 128).transpose(0, 2, 1, 3).reshape(rows, cols)


def from_pairs(grad):
    rows, cols = grad.shape
    return grad.reshape(rows, PAIRS, 3, 128).transpose(0, 2, 1, 3).reshape(rows, cols)


def on_device(tokens, cotangent, keep_mask, source, *states):
    masters = states[:5]
    dp = lax.axis_size("dp")
    images, length, feat = tokens.shape
    sources = images * lax.axis_size("head") * dp // 3
    if dp == 16:
        layer_out, input_grad, share, vsum = layer_call(
            True, dp, sources, tokens, cotangent, keep_mask, source, *masters
        )
        return tuple(step_call(layer_out, input_grad, share, vsum, states))
    gather = functools.partial(lax.all_gather, axis_name="dp", tiled=True)
    low = [master.astype(BF16) for master in masters]
    w_qkv, w_proj, w_fc1, w_fc2 = (gather(w, axis=0) for w in low[:4])
    vectors = gather(low[4], axis=1).astype(F32)
    live_mask = keep_mask.astype(F32)
    kept_rows = jnp.sum(live_mask, 1)
    onehot = (source[:, None] == jnp.arange(sources, dtype=jnp.int32)[None, :]).astype(F32)
    totals = lax.psum(jnp.sum(onehot * kept_rows[:, None], 0), ("dp", "head"))
    image_total = jnp.sum(onehot * totals[None, :], 1)
    token_weight = live_mask * (length / image_total)[:, None]
    layer_out, input_grad, gq, gp, g1, g2, vsum = layer_call(
        False, dp, sources, tokens, cotangent, keep_mask,
        token_weight, by_pair(w_qkv), w_proj, w_fc1, w_fc2, vectors,
    )
    shares = [
        lax.psum_scatter(
            lax.psum(g.astype(BF16), "head").astype(F32), "dp", scatter_dimension=0, tiled=True
        )
        for g in (from_pairs(gq), gp, g1, g2)
    ]
    vsum = lax.psum(vsum, ("dp", "head"))
    low = [w.astype(F32) for w in low]
    own = masters[4].shape[1]
    mine = lax.dynamic_slice_in_dim(vsum, lax.axis_index("dp") * own, own, 1)
    norms = []
    for share, weight, behind, n in (
        (shares[0], low[0], vsum[:3], 0),
        (shares[2], low[2], vsum[ROW_FC1 : ROW_FC1 + 4], 5),
    ):
        products = jnp.sum(share * weight, 1)
        weighted = jnp.sum(weight * behind.reshape(1, -1), 1)
        norms.append(norm_grads(products, weighted, low[4][n], low[4][n + 1]))
    rows = [*norms[0], mine[0], mine[2], mine[ROW_PROJ], *norms[1], mine[ROW_FC2]]
    shares.append(jnp.stack(rows + [mine[ROW_FC1 + j] for j in range(4)]))
    new = []
    for n in range(5):
        new.extend(
            adamw(masters[n], states[5 + n], states[10 + n], shares[n], step_rates[n], decays[n])
        )
    return (layer_out, input_grad, *new)


def solution(mesh):
    split = P(("dp", "head"), None, None)
    rows, cols = P("dp", None), P(None, "dp")
    weights = (rows, rows, rows, rows, cols)
    return jax.shard_map(
        on_device,
        mesh=mesh,
        in_specs=(split, split, P(("dp", "head"), None), P(("dp", "head"))) + weights * 3,
        out_specs=(split, split) + (rows,) * 12 + (cols,) * 3,
        check_vma=False,
    )
```

```python
import functools

import jax
import jax.numpy as jnp
from jax import lax
from jax.experimental import pallas as pl
from jax.experimental.pallas import tpu as pltpu
from jax.sharding import PartitionSpec as P

HEADS = 6
HEAD_DIM = 64
STEP = 10
PAIRS = HEADS // 2
SCALE = HEAD_DIM ** (-0.5)

norm_eps = 1e-06
step_rates = (0.1, 0.4, 0.1, 0.05, 0.5)
decays = (0.05, 0.05, 0.05, 0.05, 0.0)

UNITS = 12
PLANE = 4
SHARD = 24

ROW_PROJ, ROW_FC2, ROW_FC1, SUM_ROWS = 3, 4, 5, 16

F32 = jnp.float32
BF16 = jnp.bfloat16


def dot(left, right):
    return lax.dot_general(left, right, (((1,), (0,)), ((), ())), preferred_element_type=F32)


def across(left, right):
    return lax.dot_general(left, right, (((0,), (0,)), ((), ())), preferred_element_type=F32)


def against(left, right):
    return lax.dot_general(left, right, (((1,), (1,)), ((), ())), preferred_element_type=F32)


def normalise(values):
    average = jnp.mean(values, -1, keepdims=True)
    centred = values - average
    variance = jnp.mean(centred * centred, -1, keepdims=True)
    inverse = lax.rsqrt(variance + norm_eps)
    return centred * inverse, inverse


def norm_back(grad, unit, inverse, gain_row):
    scaled = grad * gain_row
    first = jnp.mean(scaled, -1, keepdims=True)
    second = jnp.mean(scaled * unit, -1, keepdims=True)
    return inverse * (scaled - first - unit * second)


def fold(values):
    rows, cols = values.shape
    return jnp.sum(values.reshape(rows // 8, 8, cols), 0)


LOG2E_HALF = 0.7213475204444817
INV_SQRT_2PI = 0.3989422804014327


def gelu_parts(x):
    cdf = 0.5 + 0.5 * lax.erf(x * 0.7071067811865476)
    bell = jnp.exp2(x * x * (-LOG2E_HALF)) * INV_SQRT_2PI
    return x * cdf, cdf + x * bell


def layer_kernel(linked, dp, sources, *refs):
    refs = list(refs)

    def take(count):
        taken = refs[:count]
        del refs[:count]
        return taken

    tok_hbm, cot_hbm, keep_ref = take(3)
    if linked:
        src_ref, qm_ref, pm_ref, f1_ref, f2_ref, vm_ref = take(6)
        out_hbm, gin_hbm, share_ref, vsum_ref = take(4)
        wq_ref, wp_ref, w1_ref, w2_ref, vec_ref = take(5)
        slabs, vslabs, tot_mine, tot_in, pair_in, plane_in, layer_out, layer_in, layer_in2 = take(9)
        vsum, vin, share_in, send, recv = take(5)
    else:
        tw_ref, wq_ref, wp_ref, w1_ref, w2_ref, vec_ref = take(6)
        out_hbm, gin_hbm, gq_ref, gp_ref, g1_ref, g2_ref, vsum_ref = take(7)
    cot, xs, normed, qkv, probs, att, middle, nmid, act, gel, gol, gml, dsc = take(13)
    sums, sums1, b1, outs, gins, keepf, tws, local = take(8)

    images, length, feat = cot.shape
    padded = xs.shape[0] // images
    hidden = act.shape[1]
    hidden_units = hidden // feat
    group = 3 if images % 3 == 0 else 1
    blocks = images // group
    chunk = 256
    half = hidden // 2
    lane = lax.broadcasted_iota(jnp.int32, (padded, 128), 1)
    low_half = lane < HEAD_DIM

    def image_rows(i):
        return pl.ds(pl.multiple_of(i * padded, padded), padded)

    def real_rows(i):
        return pl.ds(pl.multiple_of(i * padded, padded), length)

    def each_block(body, first=0, last=None):
        def step(t, carry):
            rows = pl.ds(pl.multiple_of(t * group * padded, padded), group * padded)
            body(rows, [t * group + k for k in range(group)])
            return carry

        lax.fori_loop(first, blocks if last is None else last, step, 0)

    def row(n):
        return vec_ref[n : n + 1, :]

    def stacked_halves(values):
        zero = jnp.zeros_like(values)
        return jnp.concatenate(
            [jnp.where(low_half, values, zero), jnp.where(low_half, zero, values)], 0
        )

    def merged_halves(values):
        return jnp.where(low_half, values[:padded], values[padded:])

    tok_in = pltpu.make_async_copy(tok_hbm, outs, local.at[0])
    cot_in = pltpu.make_async_copy(cot_hbm, cot, local.at[1])
    out_copy = pltpu.make_async_copy(outs, out_hbm, local.at[2])
    gin_copy = pltpu.make_async_copy(gins, gin_hbm, local.at[3])
    tok_in.start()
    cot_in.start()

    if linked:
        me = lax.axis_index("dp")
        core = lax.axis_index("head")
        layers = dp // PLANE
        layer, place = me // PLANE, me % PLANE
        next_layer = [(layer + r) % layers for r in range(layers)]
        next_place = [(place + r) % PLANE for r in range(PLANE)]
        counter = [0]
        started = []

        def peers(kind):
            if kind == "layer":
                return [(next_layer[r] * PLANE + place, core) for r in range(1, layers)]
            if kind == "cross":
                return [(next_layer[r] * PLANE + place, 1 - core) for r in range(1, layers)]
            if kind == "plane":
                return [(layer * PLANE + next_place[r], core) for r in range(1, PLANE)]
            return [(me, 1 - core)]

        places = {kind: peers(kind) for kind in ("layer", "cross", "plane", "core")}

        def copies_of(ticket):
            kind, pick, first = ticket
            for r, device in enumerate(places[kind], 1):
                src, dst = pick(r)
                yield pltpu.make_async_remote_copy(
                    src_ref=src,
                    dst_ref=dst,
                    send_sem=send.at[first + r - 1],
                    recv_sem=recv.at[first + r - 1],
                    device_id=device,
                    device_id_type=pl.DeviceIdType.MESH,
                )

        def push(kind, pick):
            ticket = (kind, pick, counter[0])
            counter[0] += len(places[kind])
            for copy in copies_of(ticket):
                copy.start()
            started.append(ticket)
            return [ticket]

        def arrive(tickets):
            for ticket in tickets:
                for copy in copies_of(ticket):
                    copy.wait_recv()

        def all_sent():
            for ticket in started:
                for copy in copies_of(ticket):
                    copy.wait_send()
            started.clear()

        barrier = pltpu.get_barrier_semaphore()
        everyone = [device for kind in places.values() for device in kind]
        for device in everyone:
            pl.semaphore_signal(
                barrier, inc=1, device_id=device, device_id_type=pl.DeviceIdType.MESH
            )

        def own_block(u):
            if u < PAIRS:
                parts = [qm_ref[:, n * feat + 128 * u : n * feat + 128 * u + 128] for n in range(3)]
                return jnp.concatenate(parts, 1)
            if u == 3:
                return pm_ref[...]
            if u < 8:
                return f1_ref[:, feat * (u - 4) : feat * (u - 3)]
            return f2_ref[SHARD * (u - 8) : SHARD * (u - 7), :]

        def own_slab(u, other):
            slabs[u + (other - u) * core, place, layer] = jnp.where(
                core == 0, own_block(u), own_block(other)
            ).astype(BF16)

        def vec_push(kind):
            if kind == "layer":
                return push(kind, lambda r: (vslabs.at[place, layer],) * 2)
            return push(kind, lambda r: (vslabs.at[place],) * 2)

        def tot_push(kind, stage):
            part = pl.ds(8 * stage, 8)
            return push(kind, lambda r: (tot_mine.at[part], tot_in.at[3 * stage + r - 1]))

        def tot_sum(stage, count):
            total = tot_mine[8 * stage : 8 * stage + 8]
            for r in range(count):
                total = total + tot_in[3 * stage + r]
            tot_mine[8 * stage + 8 : 8 * stage + 16] = total

        step_units = (
            pl.ds(core, 1), pl.ds(2 + core, 1), pl.ds(4 + 2 * core, 2), pl.ds(8 + 2 * core, 2)
        )
        other = 1 - core
        their_units = (
            pl.ds(other, 1), pl.ds(2 + other, 1), pl.ds(4 + 2 * other, 2), pl.ds(8 + 2 * other, 2)
        )

        def weights_push(step, kind):
            units = step_units[step]
            if kind == "layer":
                return push(kind, lambda r: (slabs.at[units, place, layer],) * 2)
            if kind == "plane":
                return push(kind, lambda r: (slabs.at[units, place],) * 2)
            return push(kind, lambda r: (slabs.at[units],) * 2)

        def two_shards(first, second):
            return jnp.concatenate([first.astype(F32), second.astype(F32)], 0).astype(BF16)

        def assemble(u):
            for q in range(layers):
                for k in range(0, PLANE, 2):
                    both = two_shards(slabs[u, k, q], slabs[u, k + 1, q])
                    first = SHARD * (PLANE * q + k)
                    rows = slice(first, first + 2 * SHARD)
                    if u < PAIRS:
                        wq_ref[rows, feat * u : feat * u + feat] = both
                    elif u == 3:
                        wp_ref[rows, :] = both
                    else:
                        w1_ref[rows, feat * (u - 4) : feat * (u - 3)] = both

        def assemble_w2():
            for q in range(layers):
                for k in range(PLANE):
                    for j in range(0, 4, 2):
                        first = 4 * SHARD * (PLANE * q + k) + SHARD * j
                        w2_ref[first : first + 2 * SHARD, :] = two_shards(
                            slabs[8 + j, k, q], slabs[9 + j, k, q]
                        )

        def spread(values, owner):
            lanes = lax.broadcasted_iota(jnp.int32, (16, 128), 1)
            shift = (SHARD * owner) % 128
            moved = pltpu.roll(values, shift, 1) if shift else values
            block = SHARD * owner // 128
            here = jnp.where(lanes >= shift, moved, 0.0)
            vec_ref[:, 128 * block : 128 * block + 128] += here
            if shift + SHARD > 128:
                rest = jnp.where(lanes < shift, moved, 0.0)
                vec_ref[:, 128 * block + 128 : 128 * block + 256] += rest

        vslabs[place, layer] = jnp.zeros((16, 128), BF16)
        vslabs[place, layer, 0:12, 0:SHARD] = vm_ref[...].astype(BF16)
        own_slab(0, 1)
        kept = jnp.sum(keep_ref[...].astype(F32), 1, keepdims=True)
        width = tot_mine.shape[1]
        source_lane = lax.broadcasted_iota(jnp.int32, (1, width), 1)
        mine = jnp.zeros((1, width), F32)
        for i in range(images):
            mine = mine + jnp.where(source_lane == src_ref[i], kept[i : i + 1], 0.0)
        tot_mine[0:8] = jnp.broadcast_to(mine, (8, width))
        pl.semaphore_wait(barrier, len(everyone))
        vec_go = vec_push("layer")
        go0 = weights_push(0, "layer")
        tot_go = tot_push("layer", 0)
        own_slab(2, 3)
        go1 = weights_push(1, "layer")
        for pair in ((4, 6), (5, 7), (8, 10), (9, 11)):
            own_slab(*pair)
        go2 = weights_push(2, "layer")
        go3 = weights_push(3, "layer")

    for i in range(images):
        tail = slice(padded * (i + 1) - 16, padded * (i + 1))
        xs[tail, :] = jnp.zeros((16, feat), BF16)
        gol[tail, :] = jnp.zeros((16, feat), BF16)
    sums[...] = jnp.zeros_like(sums)
    sums1[...] = jnp.zeros_like(sums1)
    keepf[...] = jnp.zeros_like(keepf)
    keepf[0:images, 0:length] = keep_ref[...].astype(F32)

    def first_norm(_, block):
        for i in block:
            xs[real_rows(i), :] = outs[i]
            unit, _ = normalise(xs[image_rows(i), :].astype(F32))
            middle[image_rows(i), :] = unit

    def first_scale(rows, _):
        normed[rows, :] = (middle[rows, :] * row(0) + row(1)).astype(BF16)

    tok_in.wait()
    each_block(first_norm)

    if linked:
        arrive(vec_go)
        vec_go = vec_push("plane")
        arrive(go0)
        go0 = weights_push(0, "plane")
        arrive(tot_go)
        tot_sum(0, layers - 1)
        tot_go = tot_push("plane", 1)
        arrive(vec_go)
        vec_ref[...] = jnp.zeros_like(vec_ref)
        for owner in range(dp):
            spread(vslabs[owner % PLANE, owner // PLANE].astype(F32), owner)

    for j in range(hidden_units):
        b1[0:1, feat * j : feat * j + feat] = row(8 + j)
    each_block(first_scale)

    if linked:
        arrive(go1)
        arrive(go0)
        go0 = weights_push(0, "core")
        go1 = weights_push(1, "plane")
        arrive(tot_go)
        tot_sum(1, PLANE - 1)
        tot_go = tot_push("core", 2)
        arrive(go2)
        go2 = weights_push(2, "plane")
        arrive(go0)
        assemble(0)
        assemble(1)

    def project(first, last):
        cols = slice(feat * first, feat * last)
        parts = []
        for h in range(first, last):
            part = pl.ds(128 * h, 128)
            parts += [vec_ref[2:3, part], jnp.zeros((1, 128), F32), vec_ref[3:4, part]]
        bias = jnp.concatenate(parts, 1)

        def body(rows, _):
            qkv[rows, cols] = (dot(normed[rows, :], wq_ref[:, cols]) + bias).astype(BF16)

        each_block(body)

    def pair_lanes(h):
        if isinstance(h, int):
            return slice(128 * h, 128 * h + 128)
        return pl.ds(pl.multiple_of(128 * h, 128), 128)

    def head_part(h, n):
        first = feat * h + 128 * n
        if isinstance(h, int):
            return slice(first, first + 128)
        return pl.ds(pl.multiple_of(first, 128), 128)

    def attend(h):
        results = []
        for i in range(images):
            rows = image_rows(i)
            alive = keepf[i : i + 1, 0:padded] > 0
            query = stacked_halves(qkv[rows, head_part(h, 0)] * BF16(SCALE))
            scores = against(query, qkv[rows, head_part(h, 1)])
            scores = jnp.where(alive, scores, -1e9)
            top = jnp.max(scores, -1, keepdims=True)
            raised = jnp.exp(scores - top)
            share = raised * (1.0 / jnp.sum(raised, -1, keepdims=True))
            share = share.astype(BF16)
            mixed = dot(share, qkv[rows, head_part(h, 2)])
            results.append((share, merged_halves(mixed).astype(BF16)))
        out = pair_lanes(h)
        for i, (share, mixed) in enumerate(results):
            probs[h, i] = share
            att[image_rows(i), out] = mixed

    project(0, 2)
    tickets = {}

    def attend_step(h, carry):
        @pl.when(h == 1)
        def _():
            if linked:
                arrive(go1)
                tickets[1] = weights_push(1, "core")
                arrive(go3)
                tickets[3] = weights_push(3, "plane")

        @pl.when(h == 2)
        def _():
            if linked:
                arrive(tickets[1])
                assemble(2)
                assemble(3)
            project(2, 3)

        attend(h)
        return carry

    lax.fori_loop(0, PAIRS, attend_step, 0)

    def second_norm(rows, block):
        middle[rows, :] = xs[rows, :].astype(F32) + (dot(att[rows, :], wp_ref[...]) + row(4))
        for i in block:
            unit, _ = normalise(middle[image_rows(i), :])
            nmid[image_rows(i), :] = (unit * row(5) + row(6)).astype(BF16)

    each_block(second_norm)
    if linked:
        arrive(go2)
        go2 = weights_push(2, "core")

    if linked:
        arrive(tot_go)
        tot_sum(2, 1)
        totals = tot_mine[24:25]
        for i in range(images):
            total = jnp.sum(
                jnp.where(source_lane == src_ref[i], totals, 0.0), 1, keepdims=True
            )
            tws[i : i + 1] = keepf[i : i + 1] * (length / total)
    else:
        tws[...] = jnp.zeros_like(tws)
        tws[0:images, 0:length] = tw_ref[...]
    eye = lax.broadcasted_iota(jnp.int32, (padded, padded), 0) == lax.broadcasted_iota(
        jnp.int32, (padded, padded), 1
    )

    def weigh(_, block):
        for i in block:
            weight_row = tws[pl.ds(i, 1), 0:padded]
            column = jnp.sum(jnp.where(eye, weight_row, 0.0), 1, keepdims=True)
            grad = cot[i].astype(F32) * column[:length]
            gins[i] = grad
            gol[real_rows(i), :] = grad.astype(BF16)

    cot_in.wait()
    each_block(weigh)

    if linked:
        arrive(go2)
        for u in range(4, 8):
            assemble(u)

    def expand(rows, _):
        values = nmid[rows, :]
        for j in range(hidden // chunk):
            cols = slice(chunk * j, chunk * j + chunk)
            active, slope = gelu_parts(dot(values, w1_ref[:, cols]) + b1[0:1, cols])
            act[rows, cols] = active.astype(BF16)
            gel[rows, cols] = slope.astype(BF16)

    each_block(expand, 0, blocks - 1)
    if linked:
        arrive(tickets[3])
        go3 = weights_push(3, "core")
    each_block(expand, blocks - 1, blocks)
    if linked:
        arrive(go3)
        assemble_w2()
        all_sent()

    def hidden_back(rows, _):
        grad = gol[rows, :]
        sums[ROW_FC2] += fold(grad.astype(F32))
        for j in range(hidden // chunk):
            cols = slice(chunk * j, chunk * j + chunk)
            back = against(grad, w2_ref[cols, :]) * gel[rows, cols].astype(F32)
            back = back.astype(BF16)
            gel[rows, cols] = back
            sums1[:, cols] += fold(back.astype(F32))

    each_block(hidden_back)

    if linked:
        slots = ((0, 2), (2, 4), (4, 5), (5, 6))

        first_unit = (8 + 2 * core, 4 + 2 * core, 2 + core, core)
        first_unit_there = (8 + 2 * other, 4 + 2 * other, 2 + other, other)

        def job_slots(job):
            first, last = slots[job]
            return pl.ds(first, last - first)

        def emit(u, grad):
            for owner in range(dp):
                slabs[u, owner % PLANE, owner // PLANE] = grad[
                    SHARD * owner : SHARD * owner + SHARD
                ].astype(BF16)

        def grads_pair(job):
            theirs = their_units[3 - job]
            return push("core", lambda r: (slabs.at[theirs], pair_in.at[job_slots(job)]))

        def grads_plane(job):
            first, last = slots[job]
            for s in range(first, last):
                unit = first_unit[job] + (s - first)
                for k in range(PLANE):
                    for q in range(layers):
                        slabs[unit, k, q] = (
                            slabs[unit, k, q].astype(F32) + pair_in[s, k, q].astype(F32)
                        ).astype(BF16)
            units = step_units[3 - job]
            return push(
                "plane",
                lambda r: (
                    slabs.at[units, next_place[r]],
                    plane_in.at[r - 1, job_slots(job)],
                ),
            )

        def grads_layer(job, both=False):
            first, last = slots[job]
            for s in range(first, last):
                unit = first_unit[job] + (s - first)
                for q in range(layers):
                    total = slabs[unit, place, q].astype(F32)
                    for r in range(PLANE - 1):
                        total = total + plane_in[r, s, q].astype(F32)
                    layer_out[s, q] = total.astype(BF16)
            size = job_slots(job)
            there = lambda r: layer_out.at[size, next_layer[r]]
            copies = push("layer", lambda r: (there(r), layer_in.at[r - 1, size]))
            if both:
                copies += push("cross", lambda r: (there(r), layer_in2.at[pl.ds(r, 1)]))
                copies += push("core", lambda r: (layer_out.at[size, layer], layer_in2.at[pl.ds(0, 1)]))
            return copies

        def grads_share(job, both=False):
            first, last = slots[job]
            for s in range(first, last):
                total = layer_out[s, layer].astype(F32)
                for r in range(layers - 1):
                    total = total + layer_in[r, s].astype(F32)
                share_in[first_unit[job] + (s - first)] = total
            if both:
                total = layer_in2[0].astype(F32)
                for r in range(1, layers):
                    total = total + layer_in2[r].astype(F32)
                share_in[first_unit_there[job]] = total
                return []
            units = step_units[3 - job]
            return push("core", lambda r: (share_in.at[units], share_in.at[units]))

        shares = []

    for n in range(2):
        grad = across(act[:, half * n : half * n + half], gol[...])
        if linked:
            for k in range(dp // 2):
                owner = n * dp // 2 + k
                for j in range(4):
                    first = 4 * SHARD * k + SHARD * j
                    slabs[8 + j, owner % PLANE, owner // PLANE] = grad[
                        first : first + SHARD
                    ].astype(BF16)
        else:
            g2_ref[half * n : half * n + half, :] = grad
    if linked:
        job0 = grads_pair(0)

    def middle_back(rows, block):
        grads = against(gel[rows, :], w1_ref[...])
        for k, i in enumerate(block):
            here = image_rows(i)
            grad = grads[padded * k : padded * k + padded]
            kept_middle = middle[here, :]
            unit, inverse = normalise(kept_middle)
            middle[here, :] = norm_back(grad, unit, inverse, row(5))
            middle[real_rows(i), :] += gins[i]
            gins[i] = kept_middle[:length]
            low = middle[here, :].astype(BF16)
            gml[here, :] = low
            sums[ROW_PROJ] += fold(low.astype(F32))

    each_block(middle_back, 0, 1)
    if linked:
        arrive(job0)
        job0 = grads_plane(0)
    each_block(middle_back, 1, blocks)

    for n in range(2):
        grad = across(nmid[...], gel[:, half * n : half * n + half])
        if linked:
            emit(4 + 2 * n, grad[:, 0:feat])
            emit(5 + 2 * n, grad[:, feat:])
        else:
            g1_ref[:, half * n : half * n + half] = grad
    if linked:
        job1 = grads_pair(1)

    grad = across(att[...], gml[...])
    if linked:
        emit(3, grad)
        arrive(job1)
        job1 = grads_plane(1)
    else:
        gp_ref[...] = grad

    def grad_attended(rows, _):
        att[rows, :] = against(gml[rows, :], wp_ref[...]).astype(BF16)

    each_block(grad_attended)

    def attend_back(h):
        part = pair_lanes(h)
        results = []
        for i in range(images):
            rows = image_rows(i)
            grad = stacked_halves(att[rows, part])
            share = probs[h, i].astype(F32)
            grad_share = against(grad, qkv[rows, head_part(h, 2)])
            inner = jnp.sum(share * grad_share, -1, keepdims=True)
            grad_score = (share * (grad_share - inner)).astype(BF16)
            key = qkv[rows, head_part(h, 1)]
            grad_query = (merged_halves(dot(grad_score, key)) * SCALE).astype(BF16)
            results.append((grad_score, grad_query))
        for i, (grad_score, _) in enumerate(results):
            dsc[i] = grad_score
        moved = []
        for i, (_, grad_query) in enumerate(results):
            rows = image_rows(i)
            query = stacked_halves(qkv[rows, head_part(h, 0)] * BF16(SCALE))
            grad = stacked_halves(att[rows, part])
            grad_key = across(dsc[i], query).astype(BF16)
            grad_value = across(probs[h, i], grad).astype(BF16)
            moved.append((grad_query, grad_key, grad_value))
        for n in range(3):
            for i in range(images):
                qkv[image_rows(i), head_part(h, n)] = moved[i][n]
            sums[n, :, part] = sum(fold(parts[n].astype(F32)) for parts in moved)

    def qkv_grad(first, last):
        cols = slice(feat * first, feat * last)
        grad = across(normed[...], qkv[:, cols])
        for h in range(first, last):
            part = grad[:, feat * (h - first) : feat * (h - first + 1)]
            if linked:
                emit(h, part)
            else:
                gq_ref[:, feat * h : feat * h + feat] = part

    def back_step(t, carry):
        attend_back(PAIRS - 1 - t)

        if t == 0:
            if linked:
                arrive(job0)
                tickets["job0"] = grads_layer(0)
            qkv_grad(2, 3)
            if linked:
                tickets["job2"] = grads_pair(2)

        if t == 1:
            if linked:
                arrive(job1)
                tickets["job1"] = grads_layer(1)
                arrive(tickets["job2"])
                tickets["job2"] = grads_plane(2)

        return carry

    for t in range(PAIRS):
        back_step(t, 0)
    qkv_grad(0, 2)

    def column_sums(out):
        out[...] = jnp.zeros(out.shape, F32)
        for n in range(ROW_FC1):
            out[n : n + 1, :] = jnp.sum(sums[n], 0, keepdims=True)
        for j in range(hidden_units):
            out[ROW_FC1 + j : ROW_FC1 + j + 1, :] = jnp.sum(
                sums1[:, feat * j : feat * j + feat], 0, keepdims=True
            )

    def sums_push(stage, kind):
        return push(kind, lambda r: (vsum.at[stage], vin.at[3 * stage + r - 1]))

    def sums_add(stage, count):
        total = vsum[stage]
        for r in range(count):
            total = total + vin[3 * stage + r]
        vsum[stage + 1] = total

    def contract(rows, block):
        total = dot(act[rows, :], w2_ref[...]) + row(7)
        for k, i in enumerate(block):
            outs[i] = (gins[i] + total[padded * k : padded * k + length]).astype(BF16)

    def input_back(rows, block):
        grads = against(qkv[rows, :], wq_ref[...])
        for k, i in enumerate(block):
            here = image_rows(i)
            unit, inverse = normalise(xs[here, :].astype(F32))
            back = norm_back(grads[padded * k : padded * k + padded], unit, inverse, row(0))
            gins[i] = (middle[here, :] + back)[:length]

    if linked:
        job3 = grads_pair(3)
        column_sums(vsum.at[0])
        vec_go = sums_push(0, "core")
        each_block(contract, 0, 1)
        arrive(job3)
        job3 = grads_plane(3)
        arrive(vec_go)
        sums_add(0, 1)
        vec_go = sums_push(1, "plane")
        arrive(tickets["job0"])
        shares.append(grads_share(0))
        arrive(tickets["job2"])
        job2 = grads_layer(2)
        each_block(contract, 1, blocks)
        out_copy.start()
        arrive(tickets["job1"])
        shares.append(grads_share(1))
        arrive(job3)
        job3 = grads_layer(3, both=True)
        arrive(vec_go)
        sums_add(1, PLANE - 1)
        vec_go = sums_push(2, "layer")
        each_block(input_back)
        gin_copy.start()
        arrive(job2)
        shares.append(grads_share(2))
        arrive(job3)
        shares.append(grads_share(3, both=True))
        arrive(vec_go)
        sums_add(2, layers - 1)
        vsum_ref[...] = vsum[3]
        for copies in shares:
            arrive(copies)
        share_ref[...] = share_in[...]
        all_sent()
    else:
        each_block(contract)
        out_copy.start()
        each_block(input_back)
        gin_copy.start()
        column_sums(vsum_ref)
    out_copy.wait()
    gin_copy.wait()


def layer_call(linked, dp, sources, tokens, cotangent, keep, *rest):
    images, length, feat = tokens.shape
    padded = -(-length // 16) * 16
    hidden = 4 * feat
    rows = images * padded
    vmem = pl.BlockSpec(memory_space=pltpu.VMEM)
    anywhere = pl.BlockSpec(memory_space=pl.ANY)
    smem = pl.BlockSpec(memory_space=pltpu.SMEM)
    shape = jax.ShapeDtypeStruct
    outs = [shape((images, length, feat), BF16), shape((images, length, feat), F32)]
    weights, links = [], []
    params = dict(vmem_limit_bytes=64 * 1024 * 1024)
    if linked:
        layers = dp // PLANE
        width = -(-sources // 128) * 128
        in_specs = [anywhere, anywhere, vmem, smem] + [vmem] * 5
        outs += [shape((UNITS, SHARD, feat), F32), shape((SUM_ROWS, feat), F32)]
        along, beside = layers - 1, PLANE - 1
        copies = 4 * (along + beside + 1) + (along + beside) + (along + beside + 1)
        copies += 4 * (1 + beside + along) + 3 + (along + 1) + (1 + beside + along)
        weights = [
            pltpu.VMEM((feat, PAIRS * feat), BF16),
            pltpu.VMEM((feat, feat), BF16),
            pltpu.VMEM((feat, hidden), BF16),
            pltpu.VMEM((hidden, feat), BF16),
            pltpu.VMEM((16, feat), F32),
        ]
        links = [
            pltpu.VMEM((UNITS, PLANE, layers, SHARD, feat), BF16),
            pltpu.VMEM((PLANE, layers, 16, 128), BF16),
            pltpu.VMEM((32, width), F32),
            pltpu.VMEM((9, 8, width), F32),
            pltpu.VMEM((UNITS // 2, PLANE, layers, SHARD, feat), BF16),
            pltpu.VMEM((beside, UNITS // 2, layers, SHARD, feat), BF16),
            pltpu.VMEM((UNITS // 2, layers, SHARD, feat), BF16),
            pltpu.VMEM((along, UNITS // 2, SHARD, feat), BF16),
            pltpu.VMEM((layers, SHARD, feat), BF16),
            pltpu.VMEM((4, SUM_ROWS, feat), F32),
            pltpu.VMEM((9, SUM_ROWS, feat), F32),
            pltpu.VMEM((UNITS, SHARD, feat), F32),
            pltpu.SemaphoreType.DMA((copies,)),
            pltpu.SemaphoreType.DMA((copies,)),
        ]
        params.update(collective_id=0, has_side_effects=True)
    else:
        in_specs = [anywhere, anywhere] + [vmem] * 7
        outs += [shape(w.shape, F32) for w in rest[1:5]] + [shape((SUM_ROWS, feat), F32)]
    return pl.pallas_call(
        functools.partial(layer_kernel, linked, dp, sources),
        out_shape=outs,
        in_specs=in_specs,
        out_specs=[anywhere, anywhere] + [vmem] * (len(outs) - 2),
        scratch_shapes=weights
        + links
        + [
            pltpu.VMEM((images, length, feat), BF16),
            pltpu.VMEM((rows, feat), BF16),
            pltpu.VMEM((rows, feat), BF16),
            pltpu.VMEM((rows, PAIRS * feat), BF16),
            pltpu.VMEM((PAIRS, images, 2 * padded, padded), BF16),
            pltpu.VMEM((rows, feat), BF16),
            pltpu.VMEM((rows, feat), F32),
            pltpu.VMEM((rows, feat), BF16),
            pltpu.VMEM((rows, hidden), BF16),
            pltpu.VMEM((rows, hidden), BF16),
            pltpu.VMEM((rows, feat), BF16),
            pltpu.VMEM((rows, feat), BF16),
            pltpu.VMEM((images, 2 * padded, padded), BF16),
            pltpu.VMEM((8, 8, feat), F32),
            pltpu.VMEM((8, hidden), F32),
            pltpu.VMEM((8, hidden), F32),
            pltpu.VMEM((images, length, feat), BF16),
            pltpu.VMEM((images, length, feat), F32),
            pltpu.VMEM((16, 256), F32),
            pltpu.VMEM((16, 256), F32),
            pltpu.SemaphoreType.DMA((4,)),
        ],
        compiler_params=pltpu.CompilerParams(**params),
        name="layer",
    )(tokens, cotangent, keep, *rest)


def adamw(master, first, second, gradient, step_rate, weight_decay):
    first_new = 0.9 * first + 0.1 * gradient
    second_new = 0.999 * second + 0.001 * gradient * gradient
    step_size = first_new / (1.0 - 0.9**STEP) / (jnp.sqrt(second_new / (1.0 - 0.999**STEP)) + 1e-08)
    return (first_new, second_new, master - step_rate * (step_size + weight_decay * master))


def norm_grads(products, weighted, gain, bias):
    return (products - bias * weighted) / gain, weighted


def step_kernel(out_tmp, gin_tmp, share_ref, vsum_ref, *refs):
    state, large, outs, held, (came, went) = refs[:15], refs[15:17], refs[17:32], refs[32:34], refs[34:]
    feat = share_ref.shape[2]
    images = out_tmp.shape[0]

    def moves(sources, targets, sems):
        return [
            pltpu.make_async_copy(sources[n].at[i], targets[n].at[i], sems.at[n, i])
            for i in range(images)
            for n in range(2)
        ]

    arrivals = moves((out_tmp, gin_tmp), held, came)
    departures = moves(held, large, went)
    for move in arrivals:
        move.start()

    def update(n, here, gradient):
        new = adamw(
            state[n][here], state[5 + n][here], state[10 + n][here], gradient, step_rates[n], decays[n]
        )
        for k in range(3):
            outs[3 * n + k][here] = new[k]

    def low(values):
        return values.astype(BF16).astype(F32)

    everything = slice(None)
    first_products = jnp.zeros((SHARD, 128), F32)
    first_weighted = jnp.zeros((SHARD, 128), F32)
    for u in range(PAIRS):
        for n in range(3):
            first = n * feat + 128 * u
            cols = slice(first, first + 128)
            grad = share_ref[u, :, 128 * n : 128 * n + 128]
            weight = low(state[0][:, cols])
            first_products += grad * weight
            first_weighted += weight * vsum_ref[n : n + 1, 128 * u : 128 * u + 128]
            update(0, (everything, cols), grad)
    update(1, (everything, everything), share_ref[3])
    second_products = jnp.zeros((SHARD, feat), F32)
    second_weighted = jnp.zeros((SHARD, feat), F32)
    for j in range(4):
        cols = slice(feat * j, feat * j + feat)
        weight = low(state[2][:, cols])
        second_products += share_ref[4 + j] * weight
        second_weighted += weight * vsum_ref[ROW_FC1 + j : ROW_FC1 + j + 1, :]
        update(2, (everything, cols), share_ref[4 + j])
        update(3, (slice(SHARD * j, SHARD * j + SHARD), everything), share_ref[8 + j])

    for arrival, departure in zip(arrivals, departures):
        arrival.wait()
        departure.start()

    me = lax.axis_index("dp")
    sums = vsum_ref[...]
    lanes = lax.broadcasted_iota(jnp.int32, (SUM_ROWS, 128), 1)
    mine = jnp.zeros((SUM_ROWS, 128), F32)
    for owner in range(16):
        shift = (SHARD * owner) % 128
        block = SHARD * owner // 128
        part = sums[:, 128 * block : 128 * block + 128]
        part = pltpu.roll(part, 128 - shift, 1) if shift else part
        if shift + SHARD > 128:
            rest = pltpu.roll(sums[:, 128 * block + 128 : 128 * block + 256], 128 - shift, 1)
            part = jnp.where(lanes < 128 - shift, part, rest)
        mine = jnp.where(me == owner, part, mine)
    mine = mine[:, 0:SHARD]
    eye = lax.broadcasted_iota(jnp.int32, (SHARD, SHARD), 0) == lax.broadcasted_iota(
        jnp.int32, (SHARD, SHARD), 1
    )

    def as_row(values):
        column = jnp.sum(values, 1, keepdims=True)
        return jnp.sum(jnp.where(eye, column, 0.0), 0, keepdims=True)

    vec = low(state[4][...])
    gain_first, shift_first = norm_grads(
        as_row(first_products), as_row(first_weighted), vec[0:1], vec[1:2]
    )
    gain_second, shift_second = norm_grads(
        as_row(second_products), as_row(second_weighted), vec[5:6], vec[6:7]
    )
    grads = [gain_first, shift_first, mine[0:1], mine[2:3], mine[ROW_PROJ : ROW_PROJ + 1]]
    grads += [gain_second, shift_second, mine[ROW_FC2 : ROW_FC2 + 1]]
    grads += [mine[ROW_FC1 + j : ROW_FC1 + j + 1] for j in range(4)]
    for n, grad in enumerate(grads):
        update(4, (slice(n, n + 1), everything), grad)
    for move in departures:
        move.wait()


def step_call(layer_out, input_grad, share, vsum, states):
    vmem = pl.BlockSpec(memory_space=pltpu.VMEM)
    anywhere = pl.BlockSpec(memory_space=pl.ANY)
    shape = jax.ShapeDtypeStruct
    large = [shape(a.shape, a.dtype) for a in (layer_out, input_grad)]
    return pl.pallas_call(
        step_kernel,
        out_shape=large + [shape(states[n].shape, F32) for n in range(5) for _ in range(3)],
        in_specs=[anywhere] * 2 + [vmem] * 17,
        out_specs=[anywhere] * 2 + [vmem] * 15,
        scratch_shapes=[pltpu.VMEM(a.shape, a.dtype) for a in (layer_out, input_grad)]
        + [pltpu.SemaphoreType.DMA((2, layer_out.shape[0]))] * 2,
        compiler_params=pltpu.CompilerParams(vmem_limit_bytes=64 * 1024 * 1024),
        name="step",
    )(layer_out, input_grad, share, vsum, *states)


def by_pair(weight):
    rows, cols = weight.shape
    return weight.reshape(rows, 3, PAIRS, 128).transpose(0, 2, 1, 3).reshape(rows, cols)


def from_pairs(grad):
    rows, cols = grad.shape
    return grad.reshape(rows, PAIRS, 3, 128).transpose(0, 2, 1, 3).reshape(rows, cols)


def on_device(tokens, cotangent, keep_mask, source, *states):
    masters = states[:5]
    dp = lax.axis_size("dp")
    images, length, feat = tokens.shape
    sources = images * lax.axis_size("head") * dp // 3
    if dp == 16:
        layer_out, input_grad, share, vsum = layer_call(
            True, dp, sources, tokens, cotangent, keep_mask, source, *masters
        )
        return tuple(step_call(layer_out, input_grad, share, vsum, states))
    gather = functools.partial(lax.all_gather, axis_name="dp", tiled=True)
    low = [master.astype(BF16) for master in masters]
    w_qkv, w_proj, w_fc1, w_fc2 = (gather(w, axis=0) for w in low[:4])
    vectors = gather(low[4], axis=1).astype(F32)
    live_mask = keep_mask.astype(F32)
    kept_rows = jnp.sum(live_mask, 1)
    onehot = (source[:, None] == jnp.arange(sources, dtype=jnp.int32)[None, :]).astype(F32)
    totals = lax.psum(jnp.sum(onehot * kept_rows[:, None], 0), ("dp", "head"))
    image_total = jnp.sum(onehot * totals[None, :], 1)
    token_weight = live_mask * (length / image_total)[:, None]
    layer_out, input_grad, gq, gp, g1, g2, vsum = layer_call(
        False, dp, sources, tokens, cotangent, keep_mask,
        token_weight, by_pair(w_qkv), w_proj, w_fc1, w_fc2, vectors,
    )
    shares = [
        lax.psum_scatter(
            lax.psum(g.astype(BF16), "head").astype(F32), "dp", scatter_dimension=0, tiled=True
        )
        for g in (from_pairs(gq), gp, g1, g2)
    ]
    vsum = lax.psum(vsum, ("dp", "head"))
    low = [w.astype(F32) for w in low]
    own = masters[4].shape[1]
    mine = lax.dynamic_slice_in_dim(vsum, lax.axis_index("dp") * own, own, 1)
    norms = []
    for share, weight, behind, n in (
        (shares[0], low[0], vsum[:3], 0),
        (shares[2], low[2], vsum[ROW_FC1 : ROW_FC1 + 4], 5),
    ):
        products = jnp.sum(share * weight, 1)
        weighted = jnp.sum(weight * behind.reshape(1, -1), 1)
        norms.append(norm_grads(products, weighted, low[4][n], low[4][n + 1]))
    rows = [*norms[0], mine[0], mine[2], mine[ROW_PROJ], *norms[1], mine[ROW_FC2]]
    shares.append(jnp.stack(rows + [mine[ROW_FC1 + j] for j in range(4)]))
    new = []
    for n in range(5):
        new.extend(
            adamw(masters[n], states[5 + n], states[10 + n], shares[n], step_rates[n], decays[n])
        )
    return (layer_out, input_grad, *new)


def solution(mesh):
    split = P(("dp", "head"), None, None)
    rows, cols = P("dp", None), P(None, "dp")
    weights = (rows, rows, rows, rows, cols)
    return jax.shard_map(
        on_device,
        mesh=mesh,
        in_specs=(split, split, P(("dp", "head"), None), P(("dp", "head"))) + weights * 3,
        out_specs=(split, split) + (rows,) * 12 + (cols,) * 3,
        check_vma=False,
    )
```

```python
import functools

import jax
import jax.numpy as jnp
from jax import lax
from jax.experimental import pallas as pl
from jax.experimental.pallas import tpu as pltpu
from jax.sharding import PartitionSpec as P

HEADS = 6
HEAD_DIM = 64
STEP = 10
PAIRS = HEADS // 2
SCALE = HEAD_DIM ** (-0.5)

norm_eps = 1e-06
step_rates = (0.1, 0.4, 0.1, 0.05, 0.5)
decays = (0.05, 0.05, 0.05, 0.05, 0.0)

UNITS = 12
PLANE = 4
SHARD = 24

ROW_PROJ, ROW_FC2, ROW_FC1, SUM_ROWS = 3, 4, 5, 16

F32 = jnp.float32
BF16 = jnp.bfloat16


def dot(left, right):
    return lax.dot_general(left, right, (((1,), (0,)), ((), ())), preferred_element_type=F32)


def across(left, right):
    return lax.dot_general(left, right, (((0,), (0,)), ((), ())), preferred_element_type=F32)


def against(left, right):
    return lax.dot_general(left, right, (((1,), (1,)), ((), ())), preferred_element_type=F32)


def normalise(values):
    average = jnp.mean(values, -1, keepdims=True)
    centred = values - average
    variance = jnp.mean(centred * centred, -1, keepdims=True)
    inverse = lax.rsqrt(variance + norm_eps)
    return centred * inverse, inverse


def norm_back(grad, unit, inverse, gain_row):
    scaled = grad * gain_row
    first = jnp.mean(scaled, -1, keepdims=True)
    second = jnp.mean(scaled * unit, -1, keepdims=True)
    return inverse * (scaled - first - unit * second)


def fold(values):
    rows, cols = values.shape
    return jnp.sum(values.reshape(rows // 8, 8, cols), 0)


LOG2E_HALF = 0.7213475204444817
INV_SQRT_2PI = 0.3989422804014327


def gelu_parts(x):
    cdf = 0.5 + 0.5 * lax.erf(x * 0.7071067811865476)
    bell = jnp.exp2(x * x * (-LOG2E_HALF)) * INV_SQRT_2PI
    return x * cdf, cdf + x * bell


def layer_kernel(linked, dp, sources, *refs):
    refs = list(refs)

    def take(count):
        taken = refs[:count]
        del refs[:count]
        return taken

    tok_hbm, cot_hbm, keep_ref = take(3)
    if linked:
        src_ref, qm_ref, pm_ref, f1_ref, f2_ref, vm_ref = take(6)
        out_hbm, gin_hbm, share_ref, vsum_ref = take(4)
        wq_ref, wp_ref, w1_ref, w2_ref, vec_ref = take(5)
        slabs, vslabs, tot_mine, tot_in, pair_in, plane_in, layer_out, layer_in, layer_in2 = take(9)
        vsum, vin, share_in, send, recv = take(5)
    else:
        tw_ref, wq_ref, wp_ref, w1_ref, w2_ref, vec_ref = take(6)
        out_hbm, gin_hbm, gq_ref, gp_ref, g1_ref, g2_ref, vsum_ref = take(7)
    cot, xs, normed, qkv, probs, att, middle, nmid, act, gel, gol, gml, dsc = take(13)
    sums, sums1, b1, outs, gins, keepf, tws, local = take(8)

    images, length, feat = cot.shape
    padded = xs.shape[0] // images
    hidden = act.shape[1]
    hidden_units = hidden // feat
    group = 3 if images % 3 == 0 else 1
    blocks = images // group
    chunk = 256
    half = hidden // 2
    lane = lax.broadcasted_iota(jnp.int32, (padded, 128), 1)
    low_half = lane < HEAD_DIM

    def image_rows(i):
        return pl.ds(pl.multiple_of(i * padded, padded), padded)

    def real_rows(i):
        return pl.ds(pl.multiple_of(i * padded, padded), length)

    def each_block(body, first=0, last=None):
        def step(t, carry):
            rows = pl.ds(pl.multiple_of(t * group * padded, padded), group * padded)
            body(rows, [t * group + k for k in range(group)])
            return carry

        lax.fori_loop(first, blocks if last is None else last, step, 0)

    def row(n):
        return vec_ref[n : n + 1, :]

    def stacked_halves(values):
        zero = jnp.zeros_like(values)
        return jnp.concatenate(
            [jnp.where(low_half, values, zero), jnp.where(low_half, zero, values)], 0
        )

    def merged_halves(values):
        return jnp.where(low_half, values[:padded], values[padded:])

    tok_in = pltpu.make_async_copy(tok_hbm, outs, local.at[0])
    cot_in = pltpu.make_async_copy(cot_hbm, cot, local.at[1])
    out_copy = pltpu.make_async_copy(outs, out_hbm, local.at[2])
    gin_copy = pltpu.make_async_copy(gins, gin_hbm, local.at[3])
    tok_in.start()
    cot_in.start()

    if linked:
        me = lax.axis_index("dp")
        core = lax.axis_index("head")
        layers = dp // PLANE
        layer, place = me // PLANE, me % PLANE
        next_layer = [(layer + r) % layers for r in range(layers)]
        next_place = [(place + r) % PLANE for r in range(PLANE)]
        counter = [0]
        started = []

        def peers(kind):
            if kind == "layer":
                return [(next_layer[r] * PLANE + place, core) for r in range(1, layers)]
            if kind == "cross":
                return [(next_layer[r] * PLANE + place, 1 - core) for r in range(1, layers)]
            if kind == "plane":
                return [(layer * PLANE + next_place[r], core) for r in range(1, PLANE)]
            return [(me, 1 - core)]

        places = {kind: peers(kind) for kind in ("layer", "cross", "plane", "core")}

        def copies_of(ticket):
            kind, pick, first = ticket
            for r, device in enumerate(places[kind], 1):
                src, dst = pick(r)
                yield pltpu.make_async_remote_copy(
                    src_ref=src,
                    dst_ref=dst,
                    send_sem=send.at[first + r - 1],
                    recv_sem=recv.at[first + r - 1],
                    device_id=device,
                    device_id_type=pl.DeviceIdType.MESH,
                )

        def push(kind, pick):
            ticket = (kind, pick, counter[0])
            counter[0] += len(places[kind])
            for copy in copies_of(ticket):
                copy.start()
            started.append(ticket)
            return [ticket]

        def arrive(tickets):
            for ticket in tickets:
                for copy in copies_of(ticket):
                    copy.wait_recv()

        def all_sent():
            for ticket in started:
                for copy in copies_of(ticket):
                    copy.wait_send()
            started.clear()

        barrier = pltpu.get_barrier_semaphore()
        everyone = [device for kind in places.values() for device in kind]
        for device in everyone:
            pl.semaphore_signal(
                barrier, inc=1, device_id=device, device_id_type=pl.DeviceIdType.MESH
            )

        def own_block(u):
            if u < PAIRS:
                parts = [qm_ref[:, n * feat + 128 * u : n * feat + 128 * u + 128] for n in range(3)]
                return jnp.concatenate(parts, 1)
            if u == 3:
                return pm_ref[...]
            if u < 8:
                return f1_ref[:, feat * (u - 4) : feat * (u - 3)]
            return f2_ref[SHARD * (u - 8) : SHARD * (u - 7), :]

        def own_slab(u, other):
            slabs[u + (other - u) * core, place, layer] = jnp.where(
                core == 0, own_block(u), own_block(other)
            ).astype(BF16)

        def vec_push(kind):
            if kind == "layer":
                return push(kind, lambda r: (vslabs.at[place, layer],) * 2)
            return push(kind, lambda r: (vslabs.at[place],) * 2)

        def tot_push(kind, stage):
            part = pl.ds(8 * stage, 8)
            return push(kind, lambda r: (tot_mine.at[part], tot_in.at[3 * stage + r - 1]))

        def tot_sum(stage, count):
            total = tot_mine[8 * stage : 8 * stage + 8]
            for r in range(count):
                total = total + tot_in[3 * stage + r]
            tot_mine[8 * stage + 8 : 8 * stage + 16] = total

        step_units = (
            pl.ds(core, 1), pl.ds(2 + core, 1), pl.ds(4 + 2 * core, 2), pl.ds(8 + 2 * core, 2)
        )
        other = 1 - core
        their_units = (
            pl.ds(other, 1), pl.ds(2 + other, 1), pl.ds(4 + 2 * other, 2), pl.ds(8 + 2 * other, 2)
        )

        def weights_push(step, kind):
            units = step_units[step]
            if kind == "layer":
                return push(kind, lambda r: (slabs.at[units, place, layer],) * 2)
            if kind == "plane":
                return push(kind, lambda r: (slabs.at[units, place],) * 2)
            return push(kind, lambda r: (slabs.at[units],) * 2)

        def two_shards(first, second):
            return jnp.concatenate([first.astype(F32), second.astype(F32)], 0).astype(BF16)

        def each_layer(body):
            lax.fori_loop(0, layers, lambda q, c: (body(q), c)[1], 0)

        def assemble(u):
            def body(q):
                for k in range(0, PLANE, 2):
                    both = two_shards(slabs[u, k, q], slabs[u, k + 1, q])
                    first = pl.multiple_of(SHARD * PLANE * q + SHARD * k, 16)
                    rows = pl.ds(first, 2 * SHARD)
                    if u < PAIRS:
                        wq_ref[rows, feat * u : feat * u + feat] = both
                    elif u == 3:
                        wp_ref[rows, :] = both
                    else:
                        w1_ref[rows, feat * (u - 4) : feat * (u - 3)] = both

            each_layer(body)

        def assemble_w2():
            def body(q):
                for k in range(PLANE):
                    for j in range(0, 4, 2):
                        first = pl.multiple_of(4 * SHARD * (PLANE * q + k) + SHARD * j, 16)
                        w2_ref[pl.ds(first, 2 * SHARD), :] = two_shards(
                            slabs[8 + j, k, q], slabs[9 + j, k, q]
                        )

            each_layer(body)

        def spread(values, owner):
            lanes = lax.broadcasted_iota(jnp.int32, (16, 128), 1)
            shift = (SHARD * owner) % 128
            moved = pltpu.roll(values, shift, 1) if shift else values
            block = SHARD * owner // 128
            here = jnp.where(lanes >= shift, moved, 0.0)
            vec_ref[:, 128 * block : 128 * block + 128] += here
            if shift + SHARD > 128:
                rest = jnp.where(lanes < shift, moved, 0.0)
                vec_ref[:, 128 * block + 128 : 128 * block + 256] += rest

        vslabs[place, layer] = jnp.zeros((16, 128), BF16)
        vslabs[place, layer, 0:12, 0:SHARD] = vm_ref[...].astype(BF16)
        own_slab(0, 1)
        kept = jnp.sum(keep_ref[...].astype(F32), 1, keepdims=True)
        width = tot_mine.shape[1]
        source_lane = lax.broadcasted_iota(jnp.int32, (1, width), 1)
        mine = jnp.zeros((1, width), F32)
        for i in range(images):
            mine = mine + jnp.where(source_lane == src_ref[i], kept[i : i + 1], 0.0)
        tot_mine[0:8] = jnp.broadcast_to(mine, (8, width))
        pl.semaphore_wait(barrier, len(everyone))
        vec_go = vec_push("layer")
        go0 = weights_push(0, "layer")
        tot_go = tot_push("layer", 0)
        own_slab(2, 3)
        go1 = weights_push(1, "layer")
        for pair in ((4, 6), (5, 7), (8, 10), (9, 11)):
            own_slab(*pair)
        go2 = weights_push(2, "layer")
        go3 = weights_push(3, "layer")

    for i in range(images):
        tail = slice(padded * (i + 1) - 16, padded * (i + 1))
        xs[tail, :] = jnp.zeros((16, feat), BF16)
        gol[tail, :] = jnp.zeros((16, feat), BF16)
    sums[...] = jnp.zeros_like(sums)
    sums1[...] = jnp.zeros_like(sums1)
    keepf[...] = jnp.zeros_like(keepf)
    keepf[0:images, 0:length] = keep_ref[...].astype(F32)

    def first_norm(_, block):
        for i in block:
            xs[real_rows(i), :] = outs[i]
            unit, _ = normalise(xs[image_rows(i), :].astype(F32))
            middle[image_rows(i), :] = unit

    def first_scale(rows, _):
        normed[rows, :] = (middle[rows, :] * row(0) + row(1)).astype(BF16)

    tok_in.wait()
    each_block(first_norm)

    if linked:
        arrive(vec_go)
        vec_go = vec_push("plane")
        arrive(go0)
        go0 = weights_push(0, "plane")
        arrive(tot_go)
        tot_sum(0, layers - 1)
        tot_go = tot_push("plane", 1)
        arrive(vec_go)
        vec_ref[...] = jnp.zeros_like(vec_ref)
        for owner in range(dp):
            spread(vslabs[owner % PLANE, owner // PLANE].astype(F32), owner)

    for j in range(hidden_units):
        b1[0:1, feat * j : feat * j + feat] = row(8 + j)
    each_block(first_scale)

    if linked:
        arrive(go1)
        arrive(go0)
        go0 = weights_push(0, "core")
        go1 = weights_push(1, "plane")
        arrive(tot_go)
        tot_sum(1, PLANE - 1)
        tot_go = tot_push("core", 2)
        arrive(go2)
        go2 = weights_push(2, "plane")
        arrive(go0)
        assemble(0)
        assemble(1)

    def project(first, last):
        cols = slice(feat * first, feat * last)
        parts = []
        for h in range(first, last):
            part = pl.ds(128 * h, 128)
            parts += [vec_ref[2:3, part], jnp.zeros((1, 128), F32), vec_ref[3:4, part]]
        bias = jnp.concatenate(parts, 1)

        def body(rows, _):
            qkv[rows, cols] = (dot(normed[rows, :], wq_ref[:, cols]) + bias).astype(BF16)

        each_block(body)

    def pair_lanes(h):
        if isinstance(h, int):
            return slice(128 * h, 128 * h + 128)
        return pl.ds(pl.multiple_of(128 * h, 128), 128)

    def head_part(h, n):
        first = feat * h + 128 * n
        if isinstance(h, int):
            return slice(first, first + 128)
        return pl.ds(pl.multiple_of(first, 128), 128)

    def attend(h):
        results = []
        for i in range(images):
            rows = image_rows(i)
            alive = keepf[i : i + 1, 0:padded] > 0
            query = stacked_halves(qkv[rows, head_part(h, 0)] * BF16(SCALE))
            scores = against(query, qkv[rows, head_part(h, 1)])
            scores = jnp.where(alive, scores, -1e9)
            top = jnp.max(scores, -1, keepdims=True)
            raised = jnp.exp(scores - top)
            share = raised * (1.0 / jnp.sum(raised, -1, keepdims=True))
            share = share.astype(BF16)
            mixed = dot(share, qkv[rows, head_part(h, 2)])
            results.append((share, merged_halves(mixed).astype(BF16)))
        out = pair_lanes(h)
        for i, (share, mixed) in enumerate(results):
            probs[h, i] = share
            att[image_rows(i), out] = mixed

    project(0, 2)
    tickets = {}

    def attend_step(h, carry):
        @pl.when(h == 1)
        def _():
            if linked:
                arrive(go1)
                tickets[1] = weights_push(1, "core")
                arrive(go3)
                tickets[3] = weights_push(3, "plane")

        @pl.when(h == 2)
        def _():
            if linked:
                arrive(tickets[1])
                assemble(2)
                assemble(3)
            project(2, 3)

        attend(h)
        return carry

    lax.fori_loop(0, PAIRS, attend_step, 0)

    def second_norm(rows, block):
        middle[rows, :] = xs[rows, :].astype(F32) + (dot(att[rows, :], wp_ref[...]) + row(4))
        for i in block:
            unit, _ = normalise(middle[image_rows(i), :])
            nmid[image_rows(i), :] = (unit * row(5) + row(6)).astype(BF16)

    each_block(second_norm)
    if linked:
        arrive(go2)
        go2 = weights_push(2, "core")

    if linked:
        arrive(tot_go)
        tot_sum(2, 1)
        totals = tot_mine[24:25]
        for i in range(images):
            total = jnp.sum(
                jnp.where(source_lane == src_ref[i], totals, 0.0), 1, keepdims=True
            )
            tws[i : i + 1] = keepf[i : i + 1] * (length / total)
    else:
        tws[...] = jnp.zeros_like(tws)
        tws[0:images, 0:length] = tw_ref[...]
    eye = lax.broadcasted_iota(jnp.int32, (padded, padded), 0) == lax.broadcasted_iota(
        jnp.int32, (padded, padded), 1
    )

    def weigh(_, block):
        for i in block:
            weight_row = tws[pl.ds(i, 1), 0:padded]
            column = jnp.sum(jnp.where(eye, weight_row, 0.0), 1, keepdims=True)
            grad = cot[i].astype(F32) * column[:length]
            gins[i] = grad
            gol[real_rows(i), :] = grad.astype(BF16)

    cot_in.wait()
    each_block(weigh)

    if linked:
        arrive(go2)
        for u in range(4, 8):
            assemble(u)

    def expand(rows, _):
        values = nmid[rows, :]
        for j in range(hidden // chunk):
            cols = slice(chunk * j, chunk * j + chunk)
            active, slope = gelu_parts(dot(values, w1_ref[:, cols]) + b1[0:1, cols])
            act[rows, cols] = active.astype(BF16)
            gel[rows, cols] = slope.astype(BF16)

    each_block(expand, 0, blocks - 1)
    if linked:
        arrive(tickets[3])
        go3 = weights_push(3, "core")
    each_block(expand, blocks - 1, blocks)
    if linked:
        arrive(go3)
        assemble_w2()
        all_sent()

    def hidden_back(rows, _):
        grad = gol[rows, :]
        sums[ROW_FC2] += fold(grad.astype(F32))
        for j in range(hidden // chunk):
            cols = slice(chunk * j, chunk * j + chunk)
            back = against(grad, w2_ref[cols, :]) * gel[rows, cols].astype(F32)
            back = back.astype(BF16)
            gel[rows, cols] = back
            sums1[:, cols] += fold(back.astype(F32))

    each_block(hidden_back)

    if linked:
        slots = ((0, 2), (2, 4), (4, 5), (5, 6))

        first_unit = (8 + 2 * core, 4 + 2 * core, 2 + core, core)
        first_unit_there = (8 + 2 * other, 4 + 2 * other, 2 + other, other)

        def job_slots(job):
            first, last = slots[job]
            return pl.ds(first, last - first)

        def emit(u, grad):
            for owner in range(dp):
                slabs[u, owner % PLANE, owner // PLANE] = grad[
                    SHARD * owner : SHARD * owner + SHARD
                ].astype(BF16)

        def grads_pair(job):
            theirs = their_units[3 - job]
            return push("core", lambda r: (slabs.at[theirs], pair_in.at[job_slots(job)]))

        def grads_plane(job):
            first, last = slots[job]
            for s in range(first, last):
                unit = first_unit[job] + (s - first)

                def body(q):
                    for k in range(PLANE):
                        slabs[unit, k, q] = (
                            slabs[unit, k, q].astype(F32) + pair_in[s, k, q].astype(F32)
                        ).astype(BF16)

                each_layer(body)
            units = step_units[3 - job]
            return push(
                "plane",
                lambda r: (
                    slabs.at[units, next_place[r]],
                    plane_in.at[r - 1, job_slots(job)],
                ),
            )

        def grads_layer(job, both=False):
            first, last = slots[job]
            for s in range(first, last):
                unit = first_unit[job] + (s - first)
                for q in range(layers):
                    total = slabs[unit, place, q].astype(F32)
                    for r in range(PLANE - 1):
                        total = total + plane_in[r, s, q].astype(F32)
                    layer_out[s, q] = total.astype(BF16)
            size = job_slots(job)
            there = lambda r: layer_out.at[size, next_layer[r]]
            copies = push("layer", lambda r: (there(r), layer_in.at[r - 1, size]))
            if both:
                copies += push("cross", lambda r: (there(r), layer_in2.at[pl.ds(r, 1)]))
                copies += push("core", lambda r: (layer_out.at[size, layer], layer_in2.at[pl.ds(0, 1)]))
            return copies

        def grads_share(job, both=False):
            first, last = slots[job]
            for s in range(first, last):
                total = layer_out[s, layer].astype(F32)
                for r in range(layers - 1):
                    total = total + layer_in[r, s].astype(F32)
                share_in[first_unit[job] + (s - first)] = total
            if both:
                total = layer_in2[0].astype(F32)
                for r in range(1, layers):
                    total = total + layer_in2[r].astype(F32)
                share_in[first_unit_there[job]] = total
                return []
            units = step_units[3 - job]
            return push("core", lambda r: (share_in.at[units], share_in.at[units]))

        shares = []

    for n in range(2):
        grad = across(act[:, half * n : half * n + half], gol[...])
        if linked:
            for k in range(dp // 2):
                owner = n * dp // 2 + k
                for j in range(4):
                    first = 4 * SHARD * k + SHARD * j
                    slabs[8 + j, owner % PLANE, owner // PLANE] = grad[
                        first : first + SHARD
                    ].astype(BF16)
        else:
            g2_ref[half * n : half * n + half, :] = grad
    if linked:
        job0 = grads_pair(0)

    def middle_back(rows, block):
        grads = against(gel[rows, :], w1_ref[...])
        for k, i in enumerate(block):
            here = image_rows(i)
            grad = grads[padded * k : padded * k + padded]
            kept_middle = middle[here, :]
            unit, inverse = normalise(kept_middle)
            middle[here, :] = norm_back(grad, unit, inverse, row(5))
            middle[real_rows(i), :] += gins[i]
            gins[i] = kept_middle[:length]
            low = middle[here, :].astype(BF16)
            gml[here, :] = low
            sums[ROW_PROJ] += fold(low.astype(F32))

    each_block(middle_back, 0, 1)
    if linked:
        arrive(job0)
        job0 = grads_plane(0)
    each_block(middle_back, 1, blocks)

    for n in range(2):
        grad = across(nmid[...], gel[:, half * n : half * n + half])
        if linked:
            emit(4 + 2 * n, grad[:, 0:feat])
            emit(5 + 2 * n, grad[:, feat:])
        else:
            g1_ref[:, half * n : half * n + half] = grad
    if linked:
        job1 = grads_pair(1)

    grad = across(att[...], gml[...])
    if linked:
        emit(3, grad)
        arrive(job1)
        job1 = grads_plane(1)
    else:
        gp_ref[...] = grad

    def grad_attended(rows, _):
        att[rows, :] = against(gml[rows, :], wp_ref[...]).astype(BF16)

    each_block(grad_attended)

    def attend_back(h):
        part = pair_lanes(h)
        results = []
        for i in range(images):
            rows = image_rows(i)
            grad = stacked_halves(att[rows, part])
            share = probs[h, i].astype(F32)
            grad_share = against(grad, qkv[rows, head_part(h, 2)])
            inner = jnp.sum(share * grad_share, -1, keepdims=True)
            grad_score = (share * (grad_share - inner)).astype(BF16)
            key = qkv[rows, head_part(h, 1)]
            grad_query = (merged_halves(dot(grad_score, key)) * SCALE).astype(BF16)
            results.append((grad_score, grad_query))
        for i, (grad_score, _) in enumerate(results):
            dsc[i] = grad_score
        moved = []
        for i, (_, grad_query) in enumerate(results):
            rows = image_rows(i)
            query = stacked_halves(qkv[rows, head_part(h, 0)] * BF16(SCALE))
            grad = stacked_halves(att[rows, part])
            grad_key = across(dsc[i], query).astype(BF16)
            grad_value = across(probs[h, i], grad).astype(BF16)
            moved.append((grad_query, grad_key, grad_value))
        for n in range(3):
            for i in range(images):
                qkv[image_rows(i), head_part(h, n)] = moved[i][n]
            sums[n, :, part] = sum(fold(parts[n].astype(F32)) for parts in moved)

    def qkv_grad(first, last):
        cols = slice(feat * first, feat * last)
        grad = across(normed[...], qkv[:, cols])
        for h in range(first, last):
            part = grad[:, feat * (h - first) : feat * (h - first + 1)]
            if linked:
                emit(h, part)
            else:
                gq_ref[:, feat * h : feat * h + feat] = part

    def back_step(t, carry):
        attend_back(PAIRS - 1 - t)

        if t == 0:
            if linked:
                arrive(job0)
                tickets["job0"] = grads_layer(0)
            qkv_grad(2, 3)
            if linked:
                tickets["job2"] = grads_pair(2)

        if t == 1:
            if linked:
                arrive(job1)
                tickets["job1"] = grads_layer(1)
                arrive(tickets["job2"])
                tickets["job2"] = grads_plane(2)

        return carry

    for t in range(PAIRS):
        back_step(t, 0)
    qkv_grad(0, 2)

    def column_sums(out):
        out[...] = jnp.zeros(out.shape, F32)
        for n in range(ROW_FC1):
            out[n : n + 1, :] = jnp.sum(sums[n], 0, keepdims=True)
        for j in range(hidden_units):
            out[ROW_FC1 + j : ROW_FC1 + j + 1, :] = jnp.sum(
                sums1[:, feat * j : feat * j + feat], 0, keepdims=True
            )

    def sums_push(stage, kind):
        return push(kind, lambda r: (vsum.at[stage], vin.at[3 * stage + r - 1]))

    def sums_add(stage, count):
        total = vsum[stage]
        for r in range(count):
            total = total + vin[3 * stage + r]
        vsum[stage + 1] = total

    def contract(rows, block):
        total = dot(act[rows, :], w2_ref[...]) + row(7)
        for k, i in enumerate(block):
            outs[i] = (gins[i] + total[padded * k : padded * k + length]).astype(BF16)

    def input_back(rows, block):
        grads = against(qkv[rows, :], wq_ref[...])
        for k, i in enumerate(block):
            here = image_rows(i)
            unit, inverse = normalise(xs[here, :].astype(F32))
            back = norm_back(grads[padded * k : padded * k + padded], unit, inverse, row(0))
            gins[i] = (middle[here, :] + back)[:length]

    if linked:
        job3 = grads_pair(3)
        column_sums(vsum.at[0])
        vec_go = sums_push(0, "core")
        each_block(contract, 0, 1)
        arrive(job3)
        job3 = grads_plane(3)
        arrive(vec_go)
        sums_add(0, 1)
        vec_go = sums_push(1, "plane")
        arrive(tickets["job0"])
        shares.append(grads_share(0))
        arrive(tickets["job2"])
        job2 = grads_layer(2)
        each_block(contract, 1, blocks)
        out_copy.start()
        arrive(tickets["job1"])
        shares.append(grads_share(1))
        arrive(job3)
        job3 = grads_layer(3, both=True)
        arrive(vec_go)
        sums_add(1, PLANE - 1)
        vec_go = sums_push(2, "layer")
        each_block(input_back)
        gin_copy.start()
        arrive(job2)
        shares.append(grads_share(2))
        arrive(job3)
        shares.append(grads_share(3, both=True))
        arrive(vec_go)
        sums_add(2, layers - 1)
        vsum_ref[...] = vsum[3]
        for copies in shares:
            arrive(copies)
        share_ref[...] = share_in[...]
        all_sent()
    else:
        each_block(contract)
        out_copy.start()
        each_block(input_back)
        gin_copy.start()
        column_sums(vsum_ref)
    out_copy.wait()
    gin_copy.wait()


def layer_call(linked, dp, sources, tokens, cotangent, keep, *rest):
    images, length, feat = tokens.shape
    padded = -(-length // 16) * 16
    hidden = 4 * feat
    rows = images * padded
    vmem = pl.BlockSpec(memory_space=pltpu.VMEM)
    anywhere = pl.BlockSpec(memory_space=pl.ANY)
    smem = pl.BlockSpec(memory_space=pltpu.SMEM)
    shape = jax.ShapeDtypeStruct
    outs = [shape((images, length, feat), BF16), shape((images, length, feat), F32)]
    weights, links = [], []
    params = dict(vmem_limit_bytes=64 * 1024 * 1024)
    if linked:
        layers = dp // PLANE
        width = -(-sources // 128) * 128
        in_specs = [anywhere, anywhere, vmem, smem] + [vmem] * 5
        outs += [shape((UNITS, SHARD, feat), F32), shape((SUM_ROWS, feat), F32)]
        along, beside = layers - 1, PLANE - 1
        copies = 4 * (along + beside + 1) + (along + beside) + (along + beside + 1)
        copies += 4 * (1 + beside + along) + 3 + (along + 1) + (1 + beside + along)
        weights = [
            pltpu.VMEM((feat, PAIRS * feat), BF16),
            pltpu.VMEM((feat, feat), BF16),
            pltpu.VMEM((feat, hidden), BF16),
            pltpu.VMEM((hidden, feat), BF16),
            pltpu.VMEM((16, feat), F32),
        ]
        links = [
            pltpu.VMEM((UNITS, PLANE, layers, SHARD, feat), BF16),
            pltpu.VMEM((PLANE, layers, 16, 128), BF16),
            pltpu.VMEM((32, width), F32),
            pltpu.VMEM((9, 8, width), F32),
            pltpu.VMEM((UNITS // 2, PLANE, layers, SHARD, feat), BF16),
            pltpu.VMEM((beside, UNITS // 2, layers, SHARD, feat), BF16),
            pltpu.VMEM((UNITS // 2, layers, SHARD, feat), BF16),
            pltpu.VMEM((along, UNITS // 2, SHARD, feat), BF16),
            pltpu.VMEM((layers, SHARD, feat), BF16),
            pltpu.VMEM((4, SUM_ROWS, feat), F32),
            pltpu.VMEM((9, SUM_ROWS, feat), F32),
            pltpu.VMEM((UNITS, SHARD, feat), F32),
            pltpu.SemaphoreType.DMA((copies,)),
            pltpu.SemaphoreType.DMA((copies,)),
        ]
        params.update(collective_id=0, has_side_effects=True)
    else:
        in_specs = [anywhere, anywhere] + [vmem] * 7
        outs += [shape(w.shape, F32) for w in rest[1:5]] + [shape((SUM_ROWS, feat), F32)]
    return pl.pallas_call(
        functools.partial(layer_kernel, linked, dp, sources),
        out_shape=outs,
        in_specs=in_specs,
        out_specs=[anywhere, anywhere] + [vmem] * (len(outs) - 2),
        scratch_shapes=weights
        + links
        + [
            pltpu.VMEM((images, length, feat), BF16),
            pltpu.VMEM((rows, feat), BF16),
            pltpu.VMEM((rows, feat), BF16),
            pltpu.VMEM((rows, PAIRS * feat), BF16),
            pltpu.VMEM((PAIRS, images, 2 * padded, padded), BF16),
            pltpu.VMEM((rows, feat), BF16),
            pltpu.VMEM((rows, feat), F32),
            pltpu.VMEM((rows, feat), BF16),
            pltpu.VMEM((rows, hidden), BF16),
            pltpu.VMEM((rows, hidden), BF16),
            pltpu.VMEM((rows, feat), BF16),
            pltpu.VMEM((rows, feat), BF16),
            pltpu.VMEM((images, 2 * padded, padded), BF16),
            pltpu.VMEM((8, 8, feat), F32),
            pltpu.VMEM((8, hidden), F32),
            pltpu.VMEM((8, hidden), F32),
            pltpu.VMEM((images, length, feat), BF16),
            pltpu.VMEM((images, length, feat), F32),
            pltpu.VMEM((16, 256), F32),
            pltpu.VMEM((16, 256), F32),
            pltpu.SemaphoreType.DMA((4,)),
        ],
        compiler_params=pltpu.CompilerParams(**params),
        name="layer",
    )(tokens, cotangent, keep, *rest)


def adamw(master, first, second, gradient, step_rate, weight_decay):
    first_new = 0.9 * first + 0.1 * gradient
    second_new = 0.999 * second + 0.001 * gradient * gradient
    step_size = first_new / (1.0 - 0.9**STEP) / (jnp.sqrt(second_new / (1.0 - 0.999**STEP)) + 1e-08)
    return (first_new, second_new, master - step_rate * (step_size + weight_decay * master))


def norm_grads(products, weighted, gain, bias):
    return (products - bias * weighted) / gain, weighted


def step_kernel(*refs):
    refs = list(refs)

    def take(count):
        taken = refs[:count]
        del refs[:count]
        return taken

    large_in, small_in, large_out, state_out = take(2), take(17), take(2), take(15)
    large, small, outs = take(2), take(17), take(15)
    came, went, small_came, small_went = take(4)
    share_ref, vsum_ref, *state = small
    feat = share_ref.shape[2]
    images = large[0].shape[0]
    parts = came.shape[1]
    size = images // parts

    def moves(sources, targets, sems):
        return [
            pltpu.make_async_copy(
                sources[n].at[pl.ds(size * i, size)], targets[n].at[pl.ds(size * i, size)], sems.at[n, i]
            )
            for i in range(parts)
            for n in range(2)
        ]

    def copies(sources, targets, sems):
        return [
            pltpu.make_async_copy(src, dst, sems.at[n])
            for n, (src, dst) in enumerate(zip(sources, targets))
        ]

    arrivals, departures = moves(large_in, large, came), moves(large, large_out, went)
    small_arrivals = copies(small_in, small, small_came)
    small_departures = copies(outs, state_out, small_went)

    def fetch(n):
        return [small_arrivals[2 + 5 * k + n] for k in range(3)]

    order = [small_arrivals[0], *fetch(0), *fetch(2), *fetch(3)]
    order += [small_arrivals[1], *fetch(1), *fetch(4)]
    for move in order[:4] + arrivals + order[4:]:
        move.start()

    def ready(n):
        for move in fetch(n):
            move.wait()

    def store(n):
        for k in range(3):
            small_departures[3 * n + k].start()

    def pass_on(count):
        for _ in range(count):
            arrivals[0].wait()
            departures[0].start()
            del arrivals[0]
            left.append(departures.pop(0))

    left = []

    def update(n, here, gradient):
        new = adamw(
            state[n][here], state[5 + n][here], state[10 + n][here], gradient, step_rates[n], decays[n]
        )
        for k in range(3):
            outs[3 * n + k][here] = new[k]

    def low(values):
        return values.astype(BF16).astype(F32)

    everything = slice(None)
    small_arrivals[0].wait()
    small_arrivals[1].wait()
    first_products = jnp.zeros((SHARD, 128), F32)
    first_weighted = jnp.zeros((SHARD, 128), F32)
    ready(0)
    for u in range(PAIRS):
        for n in range(3):
            first = n * feat + 128 * u
            cols = slice(first, first + 128)
            grad = share_ref[u, :, 128 * n : 128 * n + 128]
            weight = low(state[0][:, cols])
            first_products += grad * weight
            first_weighted += weight * vsum_ref[n : n + 1, 128 * u : 128 * u + 128]
            update(0, (everything, cols), grad)
    store(0)
    pass_on(2)
    second_products = jnp.zeros((SHARD, feat), F32)
    second_weighted = jnp.zeros((SHARD, feat), F32)
    ready(2)
    for j in range(4):
        cols = slice(feat * j, feat * j + feat)
        weight = low(state[2][:, cols])
        second_products += share_ref[4 + j] * weight
        second_weighted += weight * vsum_ref[ROW_FC1 + j : ROW_FC1 + j + 1, :]
        update(2, (everything, cols), share_ref[4 + j])
    store(2)
    pass_on(2)
    ready(3)
    for j in range(4):
        update(3, (slice(SHARD * j, SHARD * j + SHARD), everything), share_ref[8 + j])
    store(3)
    ready(1)
    update(1, (everything, everything), share_ref[3])
    store(1)
    ready(4)
    pass_on(len(arrivals))

    me = lax.axis_index("dp")
    sums = vsum_ref[...]
    lanes = lax.broadcasted_iota(jnp.int32, (SUM_ROWS, 128), 1)
    mine = jnp.zeros((SUM_ROWS, 128), F32)
    for owner in range(16):
        shift = (SHARD * owner) % 128
        block = SHARD * owner // 128
        part = sums[:, 128 * block : 128 * block + 128]
        part = pltpu.roll(part, 128 - shift, 1) if shift else part
        if shift + SHARD > 128:
            rest = pltpu.roll(sums[:, 128 * block + 128 : 128 * block + 256], 128 - shift, 1)
            part = jnp.where(lanes < 128 - shift, part, rest)
        mine = jnp.where(me == owner, part, mine)
    mine = mine[:, 0:SHARD]
    eye = lax.broadcasted_iota(jnp.int32, (SHARD, SHARD), 0) == lax.broadcasted_iota(
        jnp.int32, (SHARD, SHARD), 1
    )

    def as_row(values):
        column = jnp.sum(values, 1, keepdims=True)
        return jnp.sum(jnp.where(eye, column, 0.0), 0, keepdims=True)

    vec = low(state[4][...])
    gain_first, shift_first = norm_grads(
        as_row(first_products), as_row(first_weighted), vec[0:1], vec[1:2]
    )
    gain_second, shift_second = norm_grads(
        as_row(second_products), as_row(second_weighted), vec[5:6], vec[6:7]
    )
    grads = [gain_first, shift_first, mine[0:1], mine[2:3], mine[ROW_PROJ : ROW_PROJ + 1]]
    grads += [gain_second, shift_second, mine[ROW_FC2 : ROW_FC2 + 1]]
    grads += [mine[ROW_FC1 + j : ROW_FC1 + j + 1] for j in range(4)]
    for n, grad in enumerate(grads):
        update(4, (slice(n, n + 1), everything), grad)
    store(4)
    for move in left + small_departures:
        move.wait()


def step_call(layer_out, input_grad, share, vsum, states):
    anywhere = pl.BlockSpec(memory_space=pl.ANY)
    shape = jax.ShapeDtypeStruct
    large = [shape(a.shape, a.dtype) for a in (layer_out, input_grad)]
    new = [shape(states[n].shape, F32) for n in range(5) for _ in range(3)]
    operands = (layer_out, input_grad, share, vsum, *states)
    parts = 3 if layer_out.shape[0] % 3 == 0 else 1
    dma = pltpu.SemaphoreType.DMA
    return pl.pallas_call(
        step_kernel,
        out_shape=large + new,
        in_specs=[anywhere] * len(operands),
        out_specs=[anywhere] * 17,
        scratch_shapes=[pltpu.VMEM(a.shape, a.dtype) for a in (*operands, *new)]
        + [dma((2, parts)), dma((2, parts)), dma((17,)), dma((15,))],
        compiler_params=pltpu.CompilerParams(vmem_limit_bytes=64 * 1024 * 1024),
        name="step",
    )(*operands)


def by_pair(weight):
    rows, cols = weight.shape
    return weight.reshape(rows, 3, PAIRS, 128).transpose(0, 2, 1, 3).reshape(rows, cols)


def from_pairs(grad):
    rows, cols = grad.shape
    return grad.reshape(rows, PAIRS, 3, 128).transpose(0, 2, 1, 3).reshape(rows, cols)


def on_device(tokens, cotangent, keep_mask, source, *states):
    masters = states[:5]
    dp = lax.axis_size("dp")
    images, length, feat = tokens.shape
    sources = images * lax.axis_size("head") * dp // 3
    if dp == 16:
        layer_out, input_grad, share, vsum = layer_call(
            True, dp, sources, tokens, cotangent, keep_mask, source, *masters
        )
        return tuple(step_call(layer_out, input_grad, share, vsum, states))
    gather = functools.partial(lax.all_gather, axis_name="dp", tiled=True)
    low = [master.astype(BF16) for master in masters]
    w_qkv, w_proj, w_fc1, w_fc2 = (gather(w, axis=0) for w in low[:4])
    vectors = gather(low[4], axis=1).astype(F32)
    live_mask = keep_mask.astype(F32)
    kept_rows = jnp.sum(live_mask, 1)
    onehot = (source[:, None] == jnp.arange(sources, dtype=jnp.int32)[None, :]).astype(F32)
    totals = lax.psum(jnp.sum(onehot * kept_rows[:, None], 0), ("dp", "head"))
    image_total = jnp.sum(onehot * totals[None, :], 1)
    token_weight = live_mask * (length / image_total)[:, None]
    layer_out, input_grad, gq, gp, g1, g2, vsum = layer_call(
        False, dp, sources, tokens, cotangent, keep_mask,
        token_weight, by_pair(w_qkv), w_proj, w_fc1, w_fc2, vectors,
    )
    shares = [
        lax.psum_scatter(
            lax.psum(g.astype(BF16), "head").astype(F32), "dp", scatter_dimension=0, tiled=True
        )
        for g in (from_pairs(gq), gp, g1, g2)
    ]
    vsum = lax.psum(vsum, ("dp", "head"))
    low = [w.astype(F32) for w in low]
    own = masters[4].shape[1]
    mine = lax.dynamic_slice_in_dim(vsum, lax.axis_index("dp") * own, own, 1)
    norms = []
    for share, weight, behind, n in (
        (shares[0], low[0], vsum[:3], 0),
        (shares[2], low[2], vsum[ROW_FC1 : ROW_FC1 + 4], 5),
    ):
        products = jnp.sum(share * weight, 1)
        weighted = jnp.sum(weight * behind.reshape(1, -1), 1)
        norms.append(norm_grads(products, weighted, low[4][n], low[4][n + 1]))
    rows = [*norms[0], mine[0], mine[2], mine[ROW_PROJ], *norms[1], mine[ROW_FC2]]
    shares.append(jnp.stack(rows + [mine[ROW_FC1 + j] for j in range(4)]))
    new = []
    for n in range(5):
        new.extend(
            adamw(masters[n], states[5 + n], states[10 + n], shares[n], step_rates[n], decays[n])
        )
    return (layer_out, input_grad, *new)


def solution(mesh):
    split = P(("dp", "head"), None, None)
    rows, cols = P("dp", None), P(None, "dp")
    weights = (rows, rows, rows, rows, cols)
    return jax.shard_map(
        on_device,
        mesh=mesh,
        in_specs=(split, split, P(("dp", "head"), None), P(("dp", "head"))) + weights * 3,
        out_specs=(split, split) + (rows,) * 12 + (cols,) * 3,
        check_vma=False,
    )
```

```python
import functools

import jax
import jax.numpy as jnp
from jax import lax
from jax.experimental import pallas as pl
from jax.experimental.pallas import tpu as pltpu
from jax.sharding import PartitionSpec as P

HEADS = 6
HEAD_DIM = 64
STEP = 10
PAIRS = HEADS // 2
SCALE = HEAD_DIM ** (-0.5)

norm_eps = 1e-06
step_rates = (0.1, 0.4, 0.1, 0.05, 0.5)
decays = (0.05, 0.05, 0.05, 0.05, 0.0)

UNITS = 12
PLANE = 4
SHARD = 24

ROW_PROJ, ROW_FC2, ROW_FC1, SUM_ROWS = 3, 4, 5, 16

F32 = jnp.float32
BF16 = jnp.bfloat16


def dot(left, right):
    return lax.dot_general(left, right, (((1,), (0,)), ((), ())), preferred_element_type=F32)


def across(left, right):
    return lax.dot_general(left, right, (((0,), (0,)), ((), ())), preferred_element_type=F32)


def against(left, right):
    return lax.dot_general(left, right, (((1,), (1,)), ((), ())), preferred_element_type=F32)


def normalise(values):
    average = jnp.mean(values, -1, keepdims=True)
    centred = values - average
    variance = jnp.mean(centred * centred, -1, keepdims=True)
    inverse = lax.rsqrt(variance + norm_eps)
    return centred * inverse, inverse


def norm_back(grad, unit, inverse, gain_row):
    scaled = grad * gain_row
    first = jnp.mean(scaled, -1, keepdims=True)
    second = jnp.mean(scaled * unit, -1, keepdims=True)
    return inverse * (scaled - first - unit * second)


def fold(values):
    rows, cols = values.shape
    return jnp.sum(values.reshape(rows // 8, 8, cols), 0)


LOG2E_HALF = 0.7213475204444817
INV_SQRT_2PI = 0.3989422804014327


def gelu_parts(x):
    cdf = 0.5 + 0.5 * lax.erf(x * 0.7071067811865476)
    bell = jnp.exp2(x * x * (-LOG2E_HALF)) * INV_SQRT_2PI
    return x * cdf, cdf + x * bell


def layer_kernel(linked, dp, sources, *refs):
    refs = list(refs)

    def take(count):
        taken = refs[:count]
        del refs[:count]
        return taken

    tok_hbm, cot_hbm, keep_ref = take(3)
    if linked:
        src_ref, qm_ref, pm_ref, f1_ref, f2_ref, vm_ref = take(6)
        out_hbm, gin_hbm, share_ref, vsum_ref = take(4)
        wq_ref, wp_ref, w1_ref, w2_ref, vec_ref = take(5)
        slabs, vslabs, tot_mine, tot_in, pair_in, plane_in, layer_out, layer_in, layer_in2 = take(9)
        vsum, vin, late, late_in, share_in, send, recv = take(7)
    else:
        tw_ref, wq_ref, wp_ref, w1_ref, w2_ref, vec_ref = take(6)
        out_hbm, gin_hbm, gq_ref, gp_ref, g1_ref, g2_ref, vsum_ref = take(7)
    cot, xs, normed, qkv, probs, att, middle, nmid, act, gel, gol, gml, dsc = take(13)
    sums, sums1, b1, outs, gins, keepf, tws, local = take(8)

    images, length, feat = cot.shape
    padded = xs.shape[0] // images
    hidden = act.shape[1]
    hidden_units = hidden // feat
    group = 3 if images % 3 == 0 else 1
    blocks = images // group
    chunk = 256
    half = hidden // 2
    lane = lax.broadcasted_iota(jnp.int32, (padded, 128), 1)
    low_half = lane < HEAD_DIM

    def image_rows(i):
        return pl.ds(pl.multiple_of(i * padded, padded), padded)

    def real_rows(i):
        return pl.ds(pl.multiple_of(i * padded, padded), length)

    def each_block(body, first=0, last=None):
        def step(t, carry):
            rows = pl.ds(pl.multiple_of(t * group * padded, padded), group * padded)
            body(rows, [t * group + k for k in range(group)])
            return carry

        lax.fori_loop(first, blocks if last is None else last, step, 0)

    def row(n):
        return vec_ref[n : n + 1, :]

    def stacked_halves(values):
        zero = jnp.zeros_like(values)
        return jnp.concatenate(
            [jnp.where(low_half, values, zero), jnp.where(low_half, zero, values)], 0
        )

    def merged_halves(values):
        return jnp.where(low_half, values[:padded], values[padded:])

    tok_in = pltpu.make_async_copy(tok_hbm, outs, local.at[0])
    cot_in = pltpu.make_async_copy(cot_hbm, cot, local.at[1])
    out_copy = pltpu.make_async_copy(outs, out_hbm, local.at[2])
    gin_copy = pltpu.make_async_copy(gins, gin_hbm, local.at[3])
    tok_in.start()
    cot_in.start()

    if linked:
        me = lax.axis_index("dp")
        core = lax.axis_index("head")
        layers = dp // PLANE
        layer, place = me // PLANE, me % PLANE
        next_layer = [(layer + r) % layers for r in range(layers)]
        next_place = [(place + r) % PLANE for r in range(PLANE)]
        counter = [0]
        started = []

        def peers(kind):
            if kind == "layer":
                return [(next_layer[r] * PLANE + place, core) for r in range(1, layers)]
            if kind == "cross":
                return [(next_layer[r] * PLANE + place, 1 - core) for r in range(1, layers)]
            if kind == "plane":
                return [(layer * PLANE + next_place[r], core) for r in range(1, PLANE)]
            return [(me, 1 - core)]

        places = {kind: peers(kind) for kind in ("layer", "cross", "plane", "core")}

        def copies_of(ticket):
            kind, pick, first = ticket
            for r, device in enumerate(places[kind], 1):
                src, dst = pick(r)
                yield pltpu.make_async_remote_copy(
                    src_ref=src,
                    dst_ref=dst,
                    send_sem=send.at[first + r - 1],
                    recv_sem=recv.at[first + r - 1],
                    device_id=device,
                    device_id_type=pl.DeviceIdType.MESH,
                )

        def push(kind, pick):
            ticket = (kind, pick, counter[0])
            counter[0] += len(places[kind])
            for copy in copies_of(ticket):
                copy.start()
            started.append(ticket)
            return [ticket]

        def arrive(tickets):
            for ticket in tickets:
                for copy in copies_of(ticket):
                    copy.wait_recv()

        def all_sent():
            for ticket in started:
                for copy in copies_of(ticket):
                    copy.wait_send()
            started.clear()

        barrier = pltpu.get_barrier_semaphore()
        everyone = [device for kind in places.values() for device in kind]
        for device in everyone:
            pl.semaphore_signal(
                barrier, inc=1, device_id=device, device_id_type=pl.DeviceIdType.MESH
            )

        def own_block(u):
            if u < PAIRS:
                parts = [qm_ref[:, n * feat + 128 * u : n * feat + 128 * u + 128] for n in range(3)]
                return jnp.concatenate(parts, 1)
            if u == 3:
                return pm_ref[...]
            if u < 8:
                return f1_ref[:, feat * (u - 4) : feat * (u - 3)]
            return f2_ref[SHARD * (u - 8) : SHARD * (u - 7), :]

        def own_slab(u, other):
            slabs[u + (other - u) * core, place, layer] = jnp.where(
                core == 0, own_block(u), own_block(other)
            ).astype(BF16)

        def vec_push(kind):
            if kind == "layer":
                return push(kind, lambda r: (vslabs.at[place, layer],) * 2)
            return push(kind, lambda r: (vslabs.at[place],) * 2)

        def tot_push(kind, stage):
            part = pl.ds(8 * stage, 8)
            return push(kind, lambda r: (tot_mine.at[part], tot_in.at[3 * stage + r - 1]))

        def tot_sum(stage, count):
            total = tot_mine[8 * stage : 8 * stage + 8]
            for r in range(count):
                total = total + tot_in[3 * stage + r]
            tot_mine[8 * stage + 8 : 8 * stage + 16] = total

        step_units = (
            pl.ds(core, 1), pl.ds(2 + core, 1), pl.ds(4 + 2 * core, 2), pl.ds(8 + 2 * core, 2)
        )
        other = 1 - core
        their_units = (
            pl.ds(other, 1), pl.ds(2 + other, 1), pl.ds(4 + 2 * other, 2), pl.ds(8 + 2 * other, 2)
        )

        def weights_push(step, kind):
            units = step_units[step]
            if kind == "layer":
                return push(kind, lambda r: (slabs.at[units, place, layer],) * 2)
            if kind == "plane":
                return push(kind, lambda r: (slabs.at[units, place],) * 2)
            return push(kind, lambda r: (slabs.at[units],) * 2)

        def two_shards(first, second):
            return jnp.concatenate([first.astype(F32), second.astype(F32)], 0).astype(BF16)

        def each_layer(body):
            lax.fori_loop(0, layers, lambda q, c: (body(q), c)[1], 0)

        def assemble(u):
            def body(q):
                for k in range(0, PLANE, 2):
                    both = two_shards(slabs[u, k, q], slabs[u, k + 1, q])
                    first = pl.multiple_of(SHARD * PLANE * q + SHARD * k, 16)
                    rows = pl.ds(first, 2 * SHARD)
                    if u < PAIRS:
                        wq_ref[rows, feat * u : feat * u + feat] = both
                    elif u == 3:
                        wp_ref[rows, :] = both
                    else:
                        w1_ref[rows, feat * (u - 4) : feat * (u - 3)] = both

            each_layer(body)

        def assemble_w2():
            def body(q):
                for k in range(PLANE):
                    for j in range(0, 4, 2):
                        first = pl.multiple_of(4 * SHARD * (PLANE * q + k) + SHARD * j, 16)
                        w2_ref[pl.ds(first, 2 * SHARD), :] = two_shards(
                            slabs[8 + j, k, q], slabs[9 + j, k, q]
                        )

            each_layer(body)

        def spread(values, owner):
            lanes = lax.broadcasted_iota(jnp.int32, (16, 128), 1)
            shift = (SHARD * owner) % 128
            moved = pltpu.roll(values, shift, 1) if shift else values
            block = SHARD * owner // 128
            here = jnp.where(lanes >= shift, moved, 0.0)
            vec_ref[:, 128 * block : 128 * block + 128] += here
            if shift + SHARD > 128:
                rest = jnp.where(lanes < shift, moved, 0.0)
                vec_ref[:, 128 * block + 128 : 128 * block + 256] += rest

        vslabs[place, layer] = jnp.zeros((16, 128), BF16)
        vslabs[place, layer, 0:12, 0:SHARD] = vm_ref[...].astype(BF16)
        own_slab(0, 1)
        kept = jnp.sum(keep_ref[...].astype(F32), 1, keepdims=True)
        width = tot_mine.shape[1]
        source_lane = lax.broadcasted_iota(jnp.int32, (1, width), 1)
        mine = jnp.zeros((1, width), F32)
        for i in range(images):
            mine = mine + jnp.where(source_lane == src_ref[i], kept[i : i + 1], 0.0)
        tot_mine[0:8] = jnp.broadcast_to(mine, (8, width))
        pl.semaphore_wait(barrier, len(everyone))
        vec_go = vec_push("layer")
        go0 = weights_push(0, "layer")
        tot_go = tot_push("layer", 0)
        own_slab(2, 3)
        go1 = weights_push(1, "layer")
        for pair in ((4, 6), (5, 7), (8, 10), (9, 11)):
            own_slab(*pair)
        go2 = weights_push(2, "layer")
        go3 = weights_push(3, "layer")

    for i in range(images):
        tail = slice(padded * (i + 1) - 16, padded * (i + 1))
        xs[tail, :] = jnp.zeros((16, feat), BF16)
        gol[tail, :] = jnp.zeros((16, feat), BF16)
    sums[...] = jnp.zeros_like(sums)
    sums1[...] = jnp.zeros_like(sums1)
    keepf[...] = jnp.zeros_like(keepf)
    keepf[0:images, 0:length] = keep_ref[...].astype(F32)

    def first_norm(_, block):
        for i in block:
            xs[real_rows(i), :] = outs[i]
            unit, _ = normalise(xs[image_rows(i), :].astype(F32))
            middle[image_rows(i), :] = unit

    def first_scale(rows, _):
        normed[rows, :] = (middle[rows, :] * row(0) + row(1)).astype(BF16)

    tok_in.wait()
    each_block(first_norm)

    if linked:
        arrive(vec_go)
        vec_go = vec_push("plane")
        arrive(go0)
        go0 = weights_push(0, "plane")
        arrive(tot_go)
        tot_sum(0, layers - 1)
        tot_go = tot_push("plane", 1)
        arrive(vec_go)
        vec_ref[...] = jnp.zeros_like(vec_ref)
        for owner in range(dp):
            spread(vslabs[owner % PLANE, owner // PLANE].astype(F32), owner)

    for j in range(hidden_units):
        b1[0:1, feat * j : feat * j + feat] = row(8 + j)
    each_block(first_scale)

    if linked:
        arrive(go1)
        arrive(go0)
        go0 = weights_push(0, "core")
        go1 = weights_push(1, "plane")
        arrive(tot_go)
        tot_sum(1, PLANE - 1)
        tot_go = tot_push("core", 2)
        arrive(go2)
        go2 = weights_push(2, "plane")
        arrive(go0)
        assemble(0)
        assemble(1)

    def project(first, last):
        cols = slice(feat * first, feat * last)
        parts = []
        for h in range(first, last):
            part = pl.ds(128 * h, 128)
            parts += [vec_ref[2:3, part], jnp.zeros((1, 128), F32), vec_ref[3:4, part]]
        bias = jnp.concatenate(parts, 1)

        def body(rows, _):
            qkv[rows, cols] = (dot(normed[rows, :], wq_ref[:, cols]) + bias).astype(BF16)

        each_block(body)

    def pair_lanes(h):
        if isinstance(h, int):
            return slice(128 * h, 128 * h + 128)
        return pl.ds(pl.multiple_of(128 * h, 128), 128)

    def head_part(h, n):
        first = feat * h + 128 * n
        if isinstance(h, int):
            return slice(first, first + 128)
        return pl.ds(pl.multiple_of(first, 128), 128)

    def attend(h):
        results = []
        for i in range(images):
            rows = image_rows(i)
            alive = keepf[i : i + 1, 0:padded] > 0
            query = stacked_halves(qkv[rows, head_part(h, 0)] * BF16(SCALE))
            scores = against(query, qkv[rows, head_part(h, 1)])
            scores = jnp.where(alive, scores, -1e9)
            top = jnp.max(scores, -1, keepdims=True)
            raised = jnp.exp(scores - top)
            share = raised * (1.0 / jnp.sum(raised, -1, keepdims=True))
            share = share.astype(BF16)
            mixed = dot(share, qkv[rows, head_part(h, 2)])
            results.append((share, merged_halves(mixed).astype(BF16)))
        out = pair_lanes(h)
        for i, (share, mixed) in enumerate(results):
            probs[h, i] = share
            att[image_rows(i), out] = mixed

    project(0, 2)
    tickets = {}

    def attend_step(h, carry):
        @pl.when(h == 1)
        def _():
            if linked:
                arrive(go1)
                tickets[1] = weights_push(1, "core")
                arrive(go3)
                tickets[3] = weights_push(3, "plane")

        @pl.when(h == 2)
        def _():
            if linked:
                arrive(tickets[1])
                assemble(2)
                assemble(3)
            project(2, 3)

        attend(h)
        return carry

    lax.fori_loop(0, PAIRS, attend_step, 0)

    def second_norm(rows, block):
        middle[rows, :] = xs[rows, :].astype(F32) + (dot(att[rows, :], wp_ref[...]) + row(4))
        for i in block:
            unit, _ = normalise(middle[image_rows(i), :])
            nmid[image_rows(i), :] = (unit * row(5) + row(6)).astype(BF16)

    each_block(second_norm)
    if linked:
        arrive(go2)
        go2 = weights_push(2, "core")

    if linked:
        arrive(tot_go)
        tot_sum(2, 1)
        totals = tot_mine[24:25]
        for i in range(images):
            total = jnp.sum(
                jnp.where(source_lane == src_ref[i], totals, 0.0), 1, keepdims=True
            )
            tws[i : i + 1] = keepf[i : i + 1] * (length / total)
    else:
        tws[...] = jnp.zeros_like(tws)
        tws[0:images, 0:length] = tw_ref[...]
    eye = lax.broadcasted_iota(jnp.int32, (padded, padded), 0) == lax.broadcasted_iota(
        jnp.int32, (padded, padded), 1
    )

    def weigh(_, block):
        for i in block:
            weight_row = tws[pl.ds(i, 1), 0:padded]
            column = jnp.sum(jnp.where(eye, weight_row, 0.0), 1, keepdims=True)
            grad = cot[i].astype(F32) * column[:length]
            gins[i] = grad
            gol[real_rows(i), :] = grad.astype(BF16)

    cot_in.wait()
    each_block(weigh)

    if linked:
        arrive(go2)
        for u in range(4, 8):
            assemble(u)

    def expand(rows, _):
        values = nmid[rows, :]
        for j in range(hidden // chunk):
            cols = slice(chunk * j, chunk * j + chunk)
            active, slope = gelu_parts(dot(values, w1_ref[:, cols]) + b1[0:1, cols])
            act[rows, cols] = active.astype(BF16)
            gel[rows, cols] = slope.astype(BF16)

    each_block(expand, 0, blocks - 1)
    if linked:
        arrive(tickets[3])
        go3 = weights_push(3, "core")
    each_block(expand, blocks - 1, blocks)
    if linked:
        arrive(go3)
        assemble_w2()
        all_sent()

    def hidden_back(rows, _):
        grad = gol[rows, :]
        sums[ROW_FC2] += fold(grad.astype(F32))
        for j in range(hidden // chunk):
            cols = slice(chunk * j, chunk * j + chunk)
            back = against(grad, w2_ref[cols, :]) * gel[rows, cols].astype(F32)
            back = back.astype(BF16)
            gel[rows, cols] = back
            sums1[:, cols] += fold(back.astype(F32))

    each_block(hidden_back)

    if linked:
        slots = ((0, 2), (2, 4), (4, 5), (5, 6))

        first_unit = (8 + 2 * core, 4 + 2 * core, 2 + core, core)
        first_unit_there = (8 + 2 * other, 4 + 2 * other, 2 + other, other)

        def job_slots(job):
            first, last = slots[job]
            return pl.ds(first, last - first)

        def emit(u, grad):
            for owner in range(dp):
                slabs[u, owner % PLANE, owner // PLANE] = grad[
                    SHARD * owner : SHARD * owner + SHARD
                ].astype(BF16)

        def grads_pair(job):
            theirs = their_units[3 - job]
            return push("core", lambda r: (slabs.at[theirs], pair_in.at[job_slots(job)]))

        def grads_plane(job):
            first, last = slots[job]
            for s in range(first, last):
                unit = first_unit[job] + (s - first)

                def body(q):
                    for k in range(PLANE):
                        slabs[unit, k, q] = (
                            slabs[unit, k, q].astype(F32) + pair_in[s, k, q].astype(F32)
                        ).astype(BF16)

                each_layer(body)
            units = step_units[3 - job]
            return push(
                "plane",
                lambda r: (
                    slabs.at[units, next_place[r]],
                    plane_in.at[r - 1, job_slots(job)],
                ),
            )

        def grads_layer(job, both=False):
            first, last = slots[job]
            for s in range(first, last):
                unit = first_unit[job] + (s - first)
                for q in range(layers):
                    total = slabs[unit, place, q].astype(F32)
                    for r in range(PLANE - 1):
                        total = total + plane_in[r, s, q].astype(F32)
                    layer_out[s, q] = total.astype(BF16)
            size = job_slots(job)
            there = lambda r: layer_out.at[size, next_layer[r]]
            copies = push("layer", lambda r: (there(r), layer_in.at[r - 1, size]))
            if both:
                copies += push("cross", lambda r: (there(r), layer_in2.at[pl.ds(r, 1)]))
                copies += push("core", lambda r: (layer_out.at[size, layer], layer_in2.at[pl.ds(0, 1)]))
            return copies

        def grads_share(job, both=False):
            first, last = slots[job]
            for s in range(first, last):
                total = layer_out[s, layer].astype(F32)
                for r in range(layers - 1):
                    total = total + layer_in[r, s].astype(F32)
                share_in[first_unit[job] + (s - first)] = total
            if both:
                total = layer_in2[0].astype(F32)
                for r in range(1, layers):
                    total = total + layer_in2[r].astype(F32)
                share_in[first_unit_there[job]] = total
                return []
            units = step_units[3 - job]
            return push("core", lambda r: (share_in.at[units], share_in.at[units]))

        shares = []

    for n in range(2):
        grad = across(act[:, half * n : half * n + half], gol[...])
        if linked:
            for k in range(dp // 2):
                owner = n * dp // 2 + k
                for j in range(4):
                    first = 4 * SHARD * k + SHARD * j
                    slabs[8 + j, owner % PLANE, owner // PLANE] = grad[
                        first : first + SHARD
                    ].astype(BF16)
        else:
            g2_ref[half * n : half * n + half, :] = grad
    if linked:
        job0 = grads_pair(0)

    def middle_back(rows, block):
        grads = against(gel[rows, :], w1_ref[...])
        for k, i in enumerate(block):
            here = image_rows(i)
            grad = grads[padded * k : padded * k + padded]
            kept_middle = middle[here, :]
            unit, inverse = normalise(kept_middle)
            middle[here, :] = norm_back(grad, unit, inverse, row(5))
            middle[real_rows(i), :] += gins[i]
            gins[i] = kept_middle[:length]
            low = middle[here, :].astype(BF16)
            gml[here, :] = low
            sums[ROW_PROJ] += fold(low.astype(F32))

    each_block(middle_back, 0, 1)
    if linked:
        arrive(job0)
        job0 = grads_plane(0)
    each_block(middle_back, 1, blocks)

    for n in range(2):
        grad = across(nmid[...], gel[:, half * n : half * n + half])
        if linked:
            emit(4 + 2 * n, grad[:, 0:feat])
            emit(5 + 2 * n, grad[:, feat:])
        else:
            g1_ref[:, half * n : half * n + half] = grad
    if linked:
        job1 = grads_pair(1)

    grad = across(att[...], gml[...])
    if linked:
        emit(3, grad)
        arrive(job1)
        job1 = grads_plane(1)
    else:
        gp_ref[...] = grad

    def grad_attended(rows, _):
        att[rows, :] = against(gml[rows, :], wp_ref[...]).astype(BF16)

    each_block(grad_attended)

    def attend_back(h):
        part = pair_lanes(h)
        results = []
        for i in range(images):
            rows = image_rows(i)
            grad = stacked_halves(att[rows, part])
            share = probs[h, i].astype(F32)
            grad_share = against(grad, qkv[rows, head_part(h, 2)])
            inner = jnp.sum(share * grad_share, -1, keepdims=True)
            grad_score = (share * (grad_share - inner)).astype(BF16)
            key = qkv[rows, head_part(h, 1)]
            grad_query = (merged_halves(dot(grad_score, key)) * SCALE).astype(BF16)
            results.append((grad_score, grad_query))
        for i, (grad_score, _) in enumerate(results):
            dsc[i] = grad_score
        moved = []
        for i, (_, grad_query) in enumerate(results):
            rows = image_rows(i)
            query = stacked_halves(qkv[rows, head_part(h, 0)] * BF16(SCALE))
            grad = stacked_halves(att[rows, part])
            grad_key = across(dsc[i], query).astype(BF16)
            grad_value = across(probs[h, i], grad).astype(BF16)
            moved.append((grad_query, grad_key, grad_value))
        for n in range(3):
            for i in range(images):
                qkv[image_rows(i), head_part(h, n)] = moved[i][n]
            sums[n, :, part] = sum(fold(parts[n].astype(F32)) for parts in moved)

    def qkv_grad(first, last):
        cols = slice(feat * first, feat * last)
        grad = across(normed[...], qkv[:, cols])
        for h in range(first, last):
            part = grad[:, feat * (h - first) : feat * (h - first + 1)]
            if linked:
                emit(h, part)
            else:
                gq_ref[:, feat * h : feat * h + feat] = part

    def column_sums(out):
        out[...] = jnp.zeros(out.shape, F32)
        for n in range(ROW_FC1):
            out[n : n + 1, :] = jnp.sum(sums[n], 0, keepdims=True)
        for j in range(hidden_units):
            out[ROW_FC1 + j : ROW_FC1 + j + 1, :] = jnp.sum(
                sums1[:, feat * j : feat * j + feat], 0, keepdims=True
            )

    def sums_push(stage, kind):
        return push(kind, lambda r: (vsum.at[stage], vin.at[3 * stage + r - 1]))

    def late_push(stage, kind):
        return push(kind, lambda r: (late.at[stage], late_in.at[3 * stage + r - 1]))

    def sums_add(stage, count, own, came):
        total = own[stage]
        for r in range(count):
            total = total + came[3 * stage + r]
        own[stage + 1] = total

    def back_step(t, carry):
        attend_back(PAIRS - 1 - t)

        if t == 0:
            if linked:
                arrive(job0)
                tickets["job0"] = grads_layer(0)
            qkv_grad(2, 3)
            if linked:
                tickets["job2"] = grads_pair(2)

        if t == 1:
            if linked:
                arrive(job1)
                tickets["job1"] = grads_layer(1)
                arrive(tickets["job2"])
                tickets["job2"] = grads_plane(2)
                column_sums(vsum.at[0])
                tickets["vec"] = sums_push(0, "core")

        return carry

    for t in range(PAIRS):
        back_step(t, 0)
    if linked:
        arrive(tickets["vec"])
        sums_add(0, 1, vsum, vin)
        vec_go = sums_push(1, "plane")
        late[0] = jnp.zeros((8, 128), F32)
        for n in range(3):
            late[0, n : n + 1, :] = jnp.sum(sums[n, :, 0:128], 0, keepdims=True)
        late_go = late_push(0, "core")
    qkv_grad(0, 2)

    def contract(rows, block):
        total = dot(act[rows, :], w2_ref[...]) + row(7)
        for k, i in enumerate(block):
            outs[i] = (gins[i] + total[padded * k : padded * k + length]).astype(BF16)

    def input_back(rows, block):
        grads = against(qkv[rows, :], wq_ref[...])
        for k, i in enumerate(block):
            here = image_rows(i)
            unit, inverse = normalise(xs[here, :].astype(F32))
            back = norm_back(grads[padded * k : padded * k + padded], unit, inverse, row(0))
            gins[i] = (middle[here, :] + back)[:length]

    if linked:
        job3 = grads_pair(3)
        arrive(late_go)
        sums_add(0, 1, late, late_in)
        each_block(contract, 0, 1)
        arrive(job3)
        job3 = grads_plane(3)
        late_go = late_push(1, "plane")
        arrive(tickets["job2"])
        job2 = grads_layer(2)
        arrive(tickets["job0"])
        shares.append(grads_share(0))
        arrive(vec_go)
        sums_add(1, PLANE - 1, vsum, vin)
        vec_go = sums_push(2, "layer")
        each_block(contract, 1, blocks)
        out_copy.start()
        arrive(tickets["job1"])
        shares.append(grads_share(1))
        each_block(input_back, 0, 1)
        arrive(job3)
        job3 = grads_layer(3, both=True)
        arrive(late_go)
        sums_add(1, PLANE - 1, late, late_in)
        late_go = late_push(2, "layer")
        each_block(input_back, 1, blocks)
        gin_copy.start()
        arrive(job2)
        shares.append(grads_share(2))
        arrive(vec_go)
        sums_add(2, layers - 1, vsum, vin)
        arrive(late_go)
        sums_add(2, layers - 1, late, late_in)
        vsum[3, 0:3, 0:128] = late[3, 0:3, :]
        arrive(job3)
        shares.append(grads_share(3, both=True))
        vsum_ref[...] = vsum[3]
        for copies in shares:
            arrive(copies)
        share_ref[...] = share_in[...]
        all_sent()
    else:
        each_block(contract)
        out_copy.start()
        each_block(input_back)
        gin_copy.start()
        column_sums(vsum_ref)
    out_copy.wait()
    gin_copy.wait()


def layer_call(linked, dp, sources, tokens, cotangent, keep, *rest):
    images, length, feat = tokens.shape
    padded = -(-length // 16) * 16
    hidden = 4 * feat
    rows = images * padded
    vmem = pl.BlockSpec(memory_space=pltpu.VMEM)
    anywhere = pl.BlockSpec(memory_space=pl.ANY)
    smem = pl.BlockSpec(memory_space=pltpu.SMEM)
    shape = jax.ShapeDtypeStruct
    outs = [shape((images, length, feat), BF16), shape((images, length, feat), F32)]
    weights, links = [], []
    params = dict(vmem_limit_bytes=64 * 1024 * 1024)
    if linked:
        layers = dp // PLANE
        width = -(-sources // 128) * 128
        in_specs = [anywhere, anywhere, vmem, smem] + [vmem] * 5
        outs += [shape((UNITS, SHARD, feat), F32), shape((SUM_ROWS, feat), F32)]
        along, beside = layers - 1, PLANE - 1
        copies = 4 * (along + beside + 1) + (along + beside) + (along + beside + 1)
        copies += 4 * (1 + beside + along) + 3 + (along + 1) + 2 * (1 + beside + along)
        weights = [
            pltpu.VMEM((feat, PAIRS * feat), BF16),
            pltpu.VMEM((feat, feat), BF16),
            pltpu.VMEM((feat, hidden), BF16),
            pltpu.VMEM((hidden, feat), BF16),
            pltpu.VMEM((16, feat), F32),
        ]
        links = [
            pltpu.VMEM((UNITS, PLANE, layers, SHARD, feat), BF16),
            pltpu.VMEM((PLANE, layers, 16, 128), BF16),
            pltpu.VMEM((32, width), F32),
            pltpu.VMEM((9, 8, width), F32),
            pltpu.VMEM((UNITS // 2, PLANE, layers, SHARD, feat), BF16),
            pltpu.VMEM((beside, UNITS // 2, layers, SHARD, feat), BF16),
            pltpu.VMEM((UNITS // 2, layers, SHARD, feat), BF16),
            pltpu.VMEM((along, UNITS // 2, SHARD, feat), BF16),
            pltpu.VMEM((layers, SHARD, feat), BF16),
            pltpu.VMEM((4, SUM_ROWS, feat), F32),
            pltpu.VMEM((9, SUM_ROWS, feat), F32),
            pltpu.VMEM((4, 8, 128), F32),
            pltpu.VMEM((9, 8, 128), F32),
            pltpu.VMEM((UNITS, SHARD, feat), F32),
            pltpu.SemaphoreType.DMA((copies,)),
            pltpu.SemaphoreType.DMA((copies,)),
        ]
        params.update(collective_id=0, has_side_effects=True)
    else:
        in_specs = [anywhere, anywhere] + [vmem] * 7
        outs += [shape(w.shape, F32) for w in rest[1:5]] + [shape((SUM_ROWS, feat), F32)]
    return pl.pallas_call(
        functools.partial(layer_kernel, linked, dp, sources),
        out_shape=outs,
        in_specs=in_specs,
        out_specs=[anywhere, anywhere] + [vmem] * (len(outs) - 2),
        scratch_shapes=weights
        + links
        + [
            pltpu.VMEM((images, length, feat), BF16),
            pltpu.VMEM((rows, feat), BF16),
            pltpu.VMEM((rows, feat), BF16),
            pltpu.VMEM((rows, PAIRS * feat), BF16),
            pltpu.VMEM((PAIRS, images, 2 * padded, padded), BF16),
            pltpu.VMEM((rows, feat), BF16),
            pltpu.VMEM((rows, feat), F32),
            pltpu.VMEM((rows, feat), BF16),
            pltpu.VMEM((rows, hidden), BF16),
            pltpu.VMEM((rows, hidden), BF16),
            pltpu.VMEM((rows, feat), BF16),
            pltpu.VMEM((rows, feat), BF16),
            pltpu.VMEM((images, 2 * padded, padded), BF16),
            pltpu.VMEM((8, 8, feat), F32),
            pltpu.VMEM((8, hidden), F32),
            pltpu.VMEM((8, hidden), F32),
            pltpu.VMEM((images, length, feat), BF16),
            pltpu.VMEM((images, length, feat), F32),
            pltpu.VMEM((16, 256), F32),
            pltpu.VMEM((16, 256), F32),
            pltpu.SemaphoreType.DMA((4,)),
        ],
        compiler_params=pltpu.CompilerParams(**params),
        name="layer",
    )(tokens, cotangent, keep, *rest)


def adamw(master, first, second, gradient, step_rate, weight_decay):
    first_new = 0.9 * first + 0.1 * gradient
    second_new = 0.999 * second + 0.001 * gradient * gradient
    step_size = first_new / (1.0 - 0.9**STEP) / (jnp.sqrt(second_new / (1.0 - 0.999**STEP)) + 1e-08)
    return (first_new, second_new, master - step_rate * (step_size + weight_decay * master))


def norm_grads(products, weighted, gain, bias):
    return (products - bias * weighted) / gain, weighted


def step_kernel(*refs):
    refs = list(refs)

    def take(count):
        taken = refs[:count]
        del refs[:count]
        return taken

    large_in, small_in, large_out, state_out = take(2), take(17), take(2), take(15)
    large, small, outs = take(2), take(17), take(15)
    came, went, small_came, small_went = take(4)
    share_ref, vsum_ref, *state = small
    feat = share_ref.shape[2]
    images = large[0].shape[0]
    parts = came.shape[1]
    size = images // parts

    def moves(sources, targets, sems):
        return [
            pltpu.make_async_copy(
                sources[n].at[pl.ds(size * i, size)], targets[n].at[pl.ds(size * i, size)], sems.at[n, i]
            )
            for i in range(parts)
            for n in range(2)
        ]

    def copies(sources, targets, sems):
        return [
            pltpu.make_async_copy(src, dst, sems.at[n])
            for n, (src, dst) in enumerate(zip(sources, targets))
        ]

    arrivals, departures = moves(large_in, large, came), moves(large, large_out, went)
    small_arrivals = copies(small_in, small, small_came)
    small_departures = copies(outs, state_out, small_went)

    def fetch(n):
        return [small_arrivals[2 + 5 * k + n] for k in range(3)]

    order = [small_arrivals[0], *fetch(0), *fetch(2), *fetch(3)]
    order += [small_arrivals[1], *fetch(1), *fetch(4)]
    for move in order[:4] + arrivals + order[4:]:
        move.start()

    def ready(n):
        for move in fetch(n):
            move.wait()

    def store(n):
        for k in range(3):
            small_departures[3 * n + k].start()

    def pass_on(count):
        for _ in range(count):
            arrivals[0].wait()
            departures[0].start()
            del arrivals[0]
            left.append(departures.pop(0))

    left = []

    def update(n, here, gradient):
        new = adamw(
            state[n][here], state[5 + n][here], state[10 + n][here], gradient, step_rates[n], decays[n]
        )
        for k in range(3):
            outs[3 * n + k][here] = new[k]

    def low(values):
        return values.astype(BF16).astype(F32)

    everything = slice(None)
    small_arrivals[0].wait()
    small_arrivals[1].wait()
    first_products = jnp.zeros((SHARD, 128), F32)
    first_weighted = jnp.zeros((SHARD, 128), F32)
    ready(0)
    for u in range(PAIRS):
        for n in range(3):
            first = n * feat + 128 * u
            cols = slice(first, first + 128)
            grad = share_ref[u, :, 128 * n : 128 * n + 128]
            weight = low(state[0][:, cols])
            first_products += grad * weight
            first_weighted += weight * vsum_ref[n : n + 1, 128 * u : 128 * u + 128]
            update(0, (everything, cols), grad)
    store(0)
    pass_on(2)
    second_products = jnp.zeros((SHARD, feat), F32)
    second_weighted = jnp.zeros((SHARD, feat), F32)
    ready(2)
    for j in range(4):
        cols = slice(feat * j, feat * j + feat)
        weight = low(state[2][:, cols])
        second_products += share_ref[4 + j] * weight
        second_weighted += weight * vsum_ref[ROW_FC1 + j : ROW_FC1 + j + 1, :]
        update(2, (everything, cols), share_ref[4 + j])
    store(2)
    pass_on(2)
    ready(3)
    for j in range(4):
        update(3, (slice(SHARD * j, SHARD * j + SHARD), everything), share_ref[8 + j])
    store(3)
    ready(1)
    update(1, (everything, everything), share_ref[3])
    store(1)
    ready(4)
    pass_on(len(arrivals))

    me = lax.axis_index("dp")
    sums = vsum_ref[...]
    lanes = lax.broadcasted_iota(jnp.int32, (SUM_ROWS, 128), 1)
    mine = jnp.zeros((SUM_ROWS, 128), F32)
    for owner in range(16):
        shift = (SHARD * owner) % 128
        block = SHARD * owner // 128
        part = sums[:, 128 * block : 128 * block + 128]
        part = pltpu.roll(part, 128 - shift, 1) if shift else part
        if shift + SHARD > 128:
            rest = pltpu.roll(sums[:, 128 * block + 128 : 128 * block + 256], 128 - shift, 1)
            part = jnp.where(lanes < 128 - shift, part, rest)
        mine = jnp.where(me == owner, part, mine)
    mine = mine[:, 0:SHARD]
    eye = lax.broadcasted_iota(jnp.int32, (SHARD, SHARD), 0) == lax.broadcasted_iota(
        jnp.int32, (SHARD, SHARD), 1
    )

    def as_row(values):
        column = jnp.sum(values, 1, keepdims=True)
        return jnp.sum(jnp.where(eye, column, 0.0), 0, keepdims=True)

    vec = low(state[4][...])
    gain_first, shift_first = norm_grads(
        as_row(first_products), as_row(first_weighted), vec[0:1], vec[1:2]
    )
    gain_second, shift_second = norm_grads(
        as_row(second_products), as_row(second_weighted), vec[5:6], vec[6:7]
    )
    grads = [gain_first, shift_first, mine[0:1], mine[2:3], mine[ROW_PROJ : ROW_PROJ + 1]]
    grads += [gain_second, shift_second, mine[ROW_FC2 : ROW_FC2 + 1]]
    grads += [mine[ROW_FC1 + j : ROW_FC1 + j + 1] for j in range(4)]
    for n, grad in enumerate(grads):
        update(4, (slice(n, n + 1), everything), grad)
    store(4)
    for move in left + small_departures:
        move.wait()


def step_call(layer_out, input_grad, share, vsum, states):
    anywhere = pl.BlockSpec(memory_space=pl.ANY)
    shape = jax.ShapeDtypeStruct
    large = [shape(a.shape, a.dtype) for a in (layer_out, input_grad)]
    new = [shape(states[n].shape, F32) for n in range(5) for _ in range(3)]
    operands = (layer_out, input_grad, share, vsum, *states)
    parts = 3 if layer_out.shape[0] % 3 == 0 else 1
    dma = pltpu.SemaphoreType.DMA
    return pl.pallas_call(
        step_kernel,
        out_shape=large + new,
        in_specs=[anywhere] * len(operands),
        out_specs=[anywhere] * 17,
        scratch_shapes=[pltpu.VMEM(a.shape, a.dtype) for a in (*operands, *new)]
        + [dma((2, parts)), dma((2, parts)), dma((17,)), dma((15,))],
        compiler_params=pltpu.CompilerParams(vmem_limit_bytes=64 * 1024 * 1024),
        name="step",
    )(*operands)


def by_pair(weight):
    rows, cols = weight.shape
    return weight.reshape(rows, 3, PAIRS, 128).transpose(0, 2, 1, 3).reshape(rows, cols)


def from_pairs(grad):
    rows, cols = grad.shape
    return grad.reshape(rows, PAIRS, 3, 128).transpose(0, 2, 1, 3).reshape(rows, cols)


def on_device(tokens, cotangent, keep_mask, source, *states):
    masters = states[:5]
    dp = lax.axis_size("dp")
    images, length, feat = tokens.shape
    sources = images * lax.axis_size("head") * dp // 3
    if dp == 16:
        layer_out, input_grad, share, vsum = layer_call(
            True, dp, sources, tokens, cotangent, keep_mask, source, *masters
        )
        return tuple(step_call(layer_out, input_grad, share, vsum, states))
    gather = functools.partial(lax.all_gather, axis_name="dp", tiled=True)
    low = [master.astype(BF16) for master in masters]
    w_qkv, w_proj, w_fc1, w_fc2 = (gather(w, axis=0) for w in low[:4])
    vectors = gather(low[4], axis=1).astype(F32)
    live_mask = keep_mask.astype(F32)
    kept_rows = jnp.sum(live_mask, 1)
    onehot = (source[:, None] == jnp.arange(sources, dtype=jnp.int32)[None, :]).astype(F32)
    totals = lax.psum(jnp.sum(onehot * kept_rows[:, None], 0), ("dp", "head"))
    image_total = jnp.sum(onehot * totals[None, :], 1)
    token_weight = live_mask * (length / image_total)[:, None]
    layer_out, input_grad, gq, gp, g1, g2, vsum = layer_call(
        False, dp, sources, tokens, cotangent, keep_mask,
        token_weight, by_pair(w_qkv), w_proj, w_fc1, w_fc2, vectors,
    )
    shares = [
        lax.psum_scatter(
            lax.psum(g.astype(BF16), "head").astype(F32), "dp", scatter_dimension=0, tiled=True
        )
        for g in (from_pairs(gq), gp, g1, g2)
    ]
    vsum = lax.psum(vsum, ("dp", "head"))
    low = [w.astype(F32) for w in low]
    own = masters[4].shape[1]
    mine = lax.dynamic_slice_in_dim(vsum, lax.axis_index("dp") * own, own, 1)
    norms = []
    for share, weight, behind, n in (
        (shares[0], low[0], vsum[:3], 0),
        (shares[2], low[2], vsum[ROW_FC1 : ROW_FC1 + 4], 5),
    ):
        products = jnp.sum(share * weight, 1)
        weighted = jnp.sum(weight * behind.reshape(1, -1), 1)
        norms.append(norm_grads(products, weighted, low[4][n], low[4][n + 1]))
    rows = [*norms[0], mine[0], mine[2], mine[ROW_PROJ], *norms[1], mine[ROW_FC2]]
    shares.append(jnp.stack(rows + [mine[ROW_FC1 + j] for j in range(4)]))
    new = []
    for n in range(5):
        new.extend(
            adamw(masters[n], states[5 + n], states[10 + n], shares[n], step_rates[n], decays[n])
        )
    return (layer_out, input_grad, *new)


def solution(mesh):
    split = P(("dp", "head"), None, None)
    rows, cols = P("dp", None), P(None, "dp")
    weights = (rows, rows, rows, rows, cols)
    return jax.shard_map(
        on_device,
        mesh=mesh,
        in_specs=(split, split, P(("dp", "head"), None), P(("dp", "head"))) + weights * 3,
        out_specs=(split, split) + (rows,) * 12 + (cols,) * 3,
        check_vma=False,
    )
```

```python
import functools

import jax
import jax.numpy as jnp
from jax import lax
from jax.experimental import pallas as pl
from jax.experimental.pallas import tpu as pltpu
from jax.sharding import PartitionSpec as P

HEADS = 6
HEAD_DIM = 64
STEP = 10
PAIRS = HEADS // 2
SCALE = HEAD_DIM ** (-0.5)

norm_eps = 1e-06
step_rates = (0.1, 0.4, 0.1, 0.05, 0.5)
decays = (0.05, 0.05, 0.05, 0.05, 0.0)

UNITS = 12
PLANE = 4
SHARD = 24

ROW_PROJ, ROW_FC2, ROW_FC1, SUM_ROWS = 3, 4, 5, 16

F32 = jnp.float32
BF16 = jnp.bfloat16


def dot(left, right):
    return lax.dot_general(left, right, (((1,), (0,)), ((), ())), preferred_element_type=F32)


def across(left, right):
    return lax.dot_general(left, right, (((0,), (0,)), ((), ())), preferred_element_type=F32)


def against(left, right):
    return lax.dot_general(left, right, (((1,), (1,)), ((), ())), preferred_element_type=F32)


def normalise(values):
    average = jnp.mean(values, -1, keepdims=True)
    centred = values - average
    variance = jnp.mean(centred * centred, -1, keepdims=True)
    inverse = lax.rsqrt(variance + norm_eps)
    return centred * inverse, inverse


def norm_back(grad, unit, inverse, gain_row):
    scaled = grad * gain_row
    first = jnp.mean(scaled, -1, keepdims=True)
    second = jnp.mean(scaled * unit, -1, keepdims=True)
    return inverse * (scaled - first - unit * second)


def fold(values):
    rows, cols = values.shape
    return jnp.sum(values.reshape(rows // 8, 8, cols), 0)


LOG2E_HALF = 0.7213475204444817
INV_SQRT_2PI = 0.3989422804014327


def gelu_parts(x):
    cdf = 0.5 + 0.5 * lax.erf(x * 0.7071067811865476)
    bell = jnp.exp2(x * x * (-LOG2E_HALF)) * INV_SQRT_2PI
    return x * cdf, cdf + x * bell


def layer_kernel(linked, dp, sources, *refs):
    refs = list(refs)

    def take(count):
        taken = refs[:count]
        del refs[:count]
        return taken

    tok_hbm, cot_hbm, keep_ref = take(3)
    if linked:
        src_ref, qm_ref, pm_ref, f1_ref, f2_ref, vm_ref = take(6)
        out_hbm, gin_hbm, share_ref, vsum_ref = take(4)
        wq_ref, wp_ref, w1_ref, w2_ref, vec_ref = take(5)
        slabs, vslabs, tot_mine, tot_in, pair_in, plane_in, layer_out, layer_in, layer_in2 = take(9)
        vsum, vin, late, late_in, share_in, send, recv = take(7)
    else:
        tw_ref, wq_ref, wp_ref, w1_ref, w2_ref, vec_ref = take(6)
        out_hbm, gin_hbm, gq_ref, gp_ref, g1_ref, g2_ref, vsum_ref = take(7)
    cot, xs, normed, qkv, probs, att, middle, nmid, act, gel, gol, gml, dsc = take(13)
    sums, sums1, b1, outs, gins, keepf, tws, local = take(8)

    images, length, feat = cot.shape
    padded = xs.shape[0] // images
    hidden = act.shape[1]
    hidden_units = hidden // feat
    group = 3 if images % 3 == 0 else 1
    blocks = images // group
    chunk = 256
    half = hidden // 2
    lane = lax.broadcasted_iota(jnp.int32, (padded, 128), 1)
    low_half = lane < HEAD_DIM

    def image_rows(i):
        return pl.ds(pl.multiple_of(i * padded, padded), padded)

    def real_rows(i):
        return pl.ds(pl.multiple_of(i * padded, padded), length)

    def each_block(body, first=0, last=None):
        def step(t, carry):
            rows = pl.ds(pl.multiple_of(t * group * padded, padded), group * padded)
            body(rows, [t * group + k for k in range(group)])
            return carry

        lax.fori_loop(first, blocks if last is None else last, step, 0)

    def row(n):
        return vec_ref[n : n + 1, :]

    def stacked_halves(values):
        zero = jnp.zeros_like(values)
        return jnp.concatenate(
            [jnp.where(low_half, values, zero), jnp.where(low_half, zero, values)], 0
        )

    def merged_halves(values):
        return jnp.where(low_half, values[:padded], values[padded:])

    tok_in = pltpu.make_async_copy(tok_hbm, outs, local.at[0])
    cot_in = pltpu.make_async_copy(cot_hbm, cot, local.at[1])
    out_copy = pltpu.make_async_copy(outs, out_hbm, local.at[2])
    gin_copy = pltpu.make_async_copy(gins, gin_hbm, local.at[3])
    tok_in.start()
    cot_in.start()

    if linked:
        me = lax.axis_index("dp")
        core = lax.axis_index("head")
        layers = dp // PLANE
        layer, place = me // PLANE, me % PLANE
        next_layer = [(layer + r) % layers for r in range(layers)]
        next_place = [(place + r) % PLANE for r in range(PLANE)]
        counter = [0]
        started = []

        def peers(kind):
            if kind == "layer":
                return [(next_layer[r] * PLANE + place, core) for r in range(1, layers)]
            if kind == "cross":
                return [(next_layer[r] * PLANE + place, 1 - core) for r in range(1, layers)]
            if kind == "plane":
                return [(layer * PLANE + next_place[r], core) for r in range(1, PLANE)]
            return [(me, 1 - core)]

        places = {kind: peers(kind) for kind in ("layer", "cross", "plane", "core")}

        def copies_of(ticket):
            kind, pick, first = ticket
            for r, device in enumerate(places[kind], 1):
                src, dst = pick(r)
                yield pltpu.make_async_remote_copy(
                    src_ref=src,
                    dst_ref=dst,
                    send_sem=send.at[first + r - 1],
                    recv_sem=recv.at[first + r - 1],
                    device_id=device,
                    device_id_type=pl.DeviceIdType.MESH,
                )

        def push(kind, pick):
            ticket = (kind, pick, counter[0])
            counter[0] += len(places[kind])
            for copy in copies_of(ticket):
                copy.start()
            started.append(ticket)
            return [ticket]

        def arrive(tickets):
            for ticket in tickets:
                for copy in copies_of(ticket):
                    copy.wait_recv()

        def all_sent():
            for ticket in started:
                for copy in copies_of(ticket):
                    copy.wait_send()
            started.clear()

        barrier = pltpu.get_barrier_semaphore()
        everyone = [device for kind in places.values() for device in kind]
        for device in everyone:
            pl.semaphore_signal(
                barrier, inc=1, device_id=device, device_id_type=pl.DeviceIdType.MESH
            )

        def own_block(u):
            if u < PAIRS:
                parts = [qm_ref[:, n * feat + 128 * u : n * feat + 128 * u + 128] for n in range(3)]
                return jnp.concatenate(parts, 1)
            if u == 3:
                return pm_ref[...]
            if u < 8:
                return f1_ref[:, feat * (u - 4) : feat * (u - 3)]
            return f2_ref[SHARD * (u - 8) : SHARD * (u - 7), :]

        def own_slab(u, other):
            slabs[u + (other - u) * core, place, layer] = jnp.where(
                core == 0, own_block(u), own_block(other)
            ).astype(BF16)

        def vec_push(kind):
            if kind == "layer":
                return push(kind, lambda r: (vslabs.at[place, layer],) * 2)
            return push(kind, lambda r: (vslabs.at[place],) * 2)

        def tot_push(kind, stage):
            part = pl.ds(8 * stage, 8)
            return push(kind, lambda r: (tot_mine.at[part], tot_in.at[3 * stage + r - 1]))

        def tot_sum(stage, count):
            total = tot_mine[8 * stage : 8 * stage + 8]
            for r in range(count):
                total = total + tot_in[3 * stage + r]
            tot_mine[8 * stage + 8 : 8 * stage + 16] = total

        step_units = (
            pl.ds(core, 1), pl.ds(2 + core, 1), pl.ds(4 + 2 * core, 2), pl.ds(8 + 2 * core, 2)
        )
        other = 1 - core
        their_units = (
            pl.ds(other, 1), pl.ds(2 + other, 1), pl.ds(4 + 2 * other, 2), pl.ds(8 + 2 * other, 2)
        )

        def weights_push(step, kind):
            units = step_units[step]
            if kind == "layer":
                return push(kind, lambda r: (slabs.at[units, place, layer],) * 2)
            if kind == "plane":
                return push(kind, lambda r: (slabs.at[units, place],) * 2)
            return push(kind, lambda r: (slabs.at[units],) * 2)

        def two_shards(first, second):
            return jnp.concatenate([first.astype(F32), second.astype(F32)], 0).astype(BF16)

        def each_layer(body):
            lax.fori_loop(0, layers, lambda q, c: (body(q), c)[1], 0)

        def assemble(u):
            def body(q):
                for k in range(0, PLANE, 2):
                    both = two_shards(slabs[u, k, q], slabs[u, k + 1, q])
                    first = pl.multiple_of(SHARD * PLANE * q + SHARD * k, 16)
                    rows = pl.ds(first, 2 * SHARD)
                    if u < PAIRS:
                        wq_ref[rows, feat * u : feat * u + feat] = both
                    elif u == 3:
                        wp_ref[rows, :] = both
                    else:
                        w1_ref[rows, feat * (u - 4) : feat * (u - 3)] = both

            each_layer(body)

        def assemble_w2():
            def body(q):
                for k in range(PLANE):
                    for j in range(0, 4, 2):
                        first = pl.multiple_of(4 * SHARD * (PLANE * q + k) + SHARD * j, 16)
                        w2_ref[pl.ds(first, 2 * SHARD), :] = two_shards(
                            slabs[8 + j, k, q], slabs[9 + j, k, q]
                        )

            each_layer(body)

        def spread(values, owner):
            lanes = lax.broadcasted_iota(jnp.int32, (16, 128), 1)
            shift = (SHARD * owner) % 128
            moved = pltpu.roll(values, shift, 1) if shift else values
            block = SHARD * owner // 128
            here = jnp.where(lanes >= shift, moved, 0.0)
            vec_ref[:, 128 * block : 128 * block + 128] += here
            if shift + SHARD > 128:
                rest = jnp.where(lanes < shift, moved, 0.0)
                vec_ref[:, 128 * block + 128 : 128 * block + 256] += rest

        vslabs[place, layer] = jnp.zeros((16, 128), BF16)
        vslabs[place, layer, 0:12, 0:SHARD] = vm_ref[...].astype(BF16)
        own_slab(0, 1)
        kept = jnp.sum(keep_ref[...].astype(F32), 1, keepdims=True)
        width = tot_mine.shape[1]
        source_lane = lax.broadcasted_iota(jnp.int32, (1, width), 1)
        mine = jnp.zeros((1, width), F32)
        for i in range(images):
            mine = mine + jnp.where(source_lane == src_ref[i], kept[i : i + 1], 0.0)
        tot_mine[0:8] = jnp.broadcast_to(mine, (8, width))
        pl.semaphore_wait(barrier, len(everyone))
        vec_go = vec_push("layer")
        go0 = weights_push(0, "layer")
        tot_go = tot_push("layer", 0)
        own_slab(2, 3)
        go1 = weights_push(1, "layer")
        for pair in ((4, 6), (5, 7), (8, 10), (9, 11)):
            own_slab(*pair)
        go2 = weights_push(2, "layer")
        go3 = weights_push(3, "layer")

    for i in range(images):
        tail = slice(padded * (i + 1) - 16, padded * (i + 1))
        xs[tail, :] = jnp.zeros((16, feat), BF16)
        gol[tail, :] = jnp.zeros((16, feat), BF16)
    sums[...] = jnp.zeros_like(sums)
    sums1[...] = jnp.zeros_like(sums1)
    keepf[...] = jnp.zeros_like(keepf)
    keepf[0:images, 0:length] = keep_ref[...].astype(F32)

    def first_norm(_, block):
        for i in block:
            xs[real_rows(i), :] = outs[i]
            unit, _ = normalise(xs[image_rows(i), :].astype(F32))
            middle[image_rows(i), :] = unit

    def first_scale(rows, _):
        normed[rows, :] = (middle[rows, :] * row(0) + row(1)).astype(BF16)

    tok_in.wait()
    each_block(first_norm)

    if linked:
        arrive(vec_go)
        vec_go = vec_push("plane")
        arrive(go0)
        go0 = weights_push(0, "plane")
        arrive(tot_go)
        tot_sum(0, layers - 1)
        tot_go = tot_push("plane", 1)
        arrive(vec_go)
        vec_ref[...] = jnp.zeros_like(vec_ref)
        for owner in range(dp):
            spread(vslabs[owner % PLANE, owner // PLANE].astype(F32), owner)

    for j in range(hidden_units):
        b1[0:1, feat * j : feat * j + feat] = row(8 + j)
    each_block(first_scale)

    if linked:
        arrive(go1)
        arrive(go0)
        go0 = weights_push(0, "core")
        go1 = weights_push(1, "plane")
        arrive(tot_go)
        tot_sum(1, PLANE - 1)
        tot_go = tot_push("core", 2)
        arrive(go2)
        go2 = weights_push(2, "plane")
        arrive(go0)
        assemble(0)
        assemble(1)

    def project(first, last):
        cols = slice(feat * first, feat * last)
        parts = []
        for h in range(first, last):
            part = pl.ds(128 * h, 128)
            parts += [vec_ref[2:3, part], jnp.zeros((1, 128), F32), vec_ref[3:4, part]]
        bias = jnp.concatenate(parts, 1)

        def body(rows, _):
            qkv[rows, cols] = (dot(normed[rows, :], wq_ref[:, cols]) + bias).astype(BF16)

        each_block(body)

    def pair_lanes(h):
        if isinstance(h, int):
            return slice(128 * h, 128 * h + 128)
        return pl.ds(pl.multiple_of(128 * h, 128), 128)

    def head_part(h, n):
        first = feat * h + 128 * n
        if isinstance(h, int):
            return slice(first, first + 128)
        return pl.ds(pl.multiple_of(first, 128), 128)

    def attend(h):
        results = []
        for i in range(images):
            rows = image_rows(i)
            alive = keepf[i : i + 1, 0:padded] > 0
            query = stacked_halves(qkv[rows, head_part(h, 0)] * BF16(SCALE))
            scores = against(query, qkv[rows, head_part(h, 1)])
            scores = jnp.where(alive, scores, -1e9)
            top = jnp.max(scores, -1, keepdims=True)
            raised = jnp.exp(scores - top)
            share = raised * (1.0 / jnp.sum(raised, -1, keepdims=True))
            share = share.astype(BF16)
            mixed = dot(share, qkv[rows, head_part(h, 2)])
            results.append((share, merged_halves(mixed).astype(BF16)))
        out = pair_lanes(h)
        for i, (share, mixed) in enumerate(results):
            probs[h, i] = share
            att[image_rows(i), out] = mixed

    project(0, 2)
    tickets = {}

    def attend_step(h, carry):
        @pl.when(h == 1)
        def _():
            if linked:
                arrive(go1)
                tickets[1] = weights_push(1, "core")
                arrive(go3)
                tickets[3] = weights_push(3, "plane")

        @pl.when(h == 2)
        def _():
            if linked:
                arrive(tickets[1])
                assemble(2)
                assemble(3)
            project(2, 3)

        attend(h)
        return carry

    lax.fori_loop(0, PAIRS, attend_step, 0)

    def second_norm(rows, block):
        middle[rows, :] = xs[rows, :].astype(F32) + (dot(att[rows, :], wp_ref[...]) + row(4))
        for i in block:
            unit, _ = normalise(middle[image_rows(i), :])
            nmid[image_rows(i), :] = (unit * row(5) + row(6)).astype(BF16)

    each_block(second_norm)
    if linked:
        arrive(go2)
        go2 = weights_push(2, "core")

    if linked:
        arrive(tot_go)
        tot_sum(2, 1)
        totals = tot_mine[24:25]
        for i in range(images):
            total = jnp.sum(
                jnp.where(source_lane == src_ref[i], totals, 0.0), 1, keepdims=True
            )
            tws[i : i + 1] = keepf[i : i + 1] * (length / total)
    else:
        tws[...] = jnp.zeros_like(tws)
        tws[0:images, 0:length] = tw_ref[...]
    eye = lax.broadcasted_iota(jnp.int32, (padded, padded), 0) == lax.broadcasted_iota(
        jnp.int32, (padded, padded), 1
    )

    def weigh(_, block):
        for i in block:
            weight_row = tws[pl.ds(i, 1), 0:padded]
            column = jnp.sum(jnp.where(eye, weight_row, 0.0), 1, keepdims=True)
            grad = cot[i].astype(F32) * column[:length]
            gins[i] = grad
            gol[real_rows(i), :] = grad.astype(BF16)

    cot_in.wait()
    each_block(weigh)

    if linked:
        arrive(go2)
        for u in range(4, 8):
            assemble(u)

    def expand(rows, _):
        values = nmid[rows, :]
        for j in range(hidden // chunk):
            cols = slice(chunk * j, chunk * j + chunk)
            active, slope = gelu_parts(dot(values, w1_ref[:, cols]) + b1[0:1, cols])
            act[rows, cols] = active.astype(BF16)
            gel[rows, cols] = slope.astype(BF16)

    each_block(expand, 0, blocks - 1)
    if linked:
        arrive(tickets[3])
        go3 = weights_push(3, "core")
    each_block(expand, blocks - 1, blocks)
    if linked:
        all_sent()
        arrive(go3)
        assemble_w2()

    def hidden_back(rows, _):
        grad = gol[rows, :]
        sums[ROW_FC2] += fold(grad.astype(F32))
        for j in range(hidden // chunk):
            cols = slice(chunk * j, chunk * j + chunk)
            back = against(grad, w2_ref[cols, :]) * gel[rows, cols].astype(F32)
            back = back.astype(BF16)
            gel[rows, cols] = back
            sums1[:, cols] += fold(back.astype(F32))

    each_block(hidden_back)

    if linked:
        slots = ((0, 2), (2, 4), (4, 5), (5, 6))

        first_unit = (8 + 2 * core, 4 + 2 * core, 2 + core, core)
        first_unit_there = (8 + 2 * other, 4 + 2 * other, 2 + other, other)

        def job_slots(job):
            first, last = slots[job]
            return pl.ds(first, last - first)

        def emit(u, grad):
            for owner in range(dp):
                slabs[u, owner % PLANE, owner // PLANE] = grad[
                    SHARD * owner : SHARD * owner + SHARD
                ].astype(BF16)

        def grads_pair(job):
            theirs = their_units[3 - job]
            return push("core", lambda r: (slabs.at[theirs], pair_in.at[job_slots(job)]))

        def grads_plane(job):
            first, last = slots[job]
            for s in range(first, last):
                unit = first_unit[job] + (s - first)

                def body(q):
                    for k in range(PLANE):
                        slabs[unit, k, q] = (
                            slabs[unit, k, q].astype(F32) + pair_in[s, k, q].astype(F32)
                        ).astype(BF16)

                each_layer(body)
            units = step_units[3 - job]
            return push(
                "plane",
                lambda r: (
                    slabs.at[units, next_place[r]],
                    plane_in.at[r - 1, job_slots(job)],
                ),
            )

        def grads_layer(job, both=False):
            first, last = slots[job]
            for s in range(first, last):
                unit = first_unit[job] + (s - first)
                for q in range(layers):
                    total = slabs[unit, place, q].astype(F32)
                    for r in range(PLANE - 1):
                        total = total + plane_in[r, s, q].astype(F32)
                    layer_out[s, q] = total.astype(BF16)
            size = job_slots(job)
            there = lambda r: layer_out.at[size, next_layer[r]]
            copies = push("layer", lambda r: (there(r), layer_in.at[r - 1, size]))
            if both:
                copies += push("cross", lambda r: (there(r), layer_in2.at[pl.ds(r, 1)]))
                copies += push("core", lambda r: (layer_out.at[size, layer], layer_in2.at[pl.ds(0, 1)]))
            return copies

        def grads_share(job, both=False):
            first, last = slots[job]
            for s in range(first, last):
                total = layer_out[s, layer].astype(F32)
                for r in range(layers - 1):
                    total = total + layer_in[r, s].astype(F32)
                share_in[first_unit[job] + (s - first)] = total
            if both:
                total = layer_in2[0].astype(F32)
                for r in range(1, layers):
                    total = total + layer_in2[r].astype(F32)
                share_in[first_unit_there[job]] = total
                return []
            units = step_units[3 - job]
            return push("core", lambda r: (share_in.at[units], share_in.at[units]))

        shares = []

    for n in range(2):
        grad = across(act[:, half * n : half * n + half], gol[...])
        if linked:
            for k in range(dp // 2):
                owner = n * dp // 2 + k
                for j in range(4):
                    first = 4 * SHARD * k + SHARD * j
                    slabs[8 + j, owner % PLANE, owner // PLANE] = grad[
                        first : first + SHARD
                    ].astype(BF16)
        else:
            g2_ref[half * n : half * n + half, :] = grad
    if linked:
        job0 = grads_pair(0)

    def middle_back(rows, block):
        grads = against(gel[rows, :], w1_ref[...])
        for k, i in enumerate(block):
            here = image_rows(i)
            grad = grads[padded * k : padded * k + padded]
            kept_middle = middle[here, :]
            unit, inverse = normalise(kept_middle)
            middle[here, :] = norm_back(grad, unit, inverse, row(5))
            middle[real_rows(i), :] += gins[i]
            gins[i] = kept_middle[:length]
            low = middle[here, :].astype(BF16)
            gml[here, :] = low
            sums[ROW_PROJ] += fold(low.astype(F32))

    each_block(middle_back, 0, 1)
    if linked:
        arrive(job0)
        job0 = grads_plane(0)
    each_block(middle_back, 1, blocks)

    for n in range(2):
        grad = across(nmid[...], gel[:, half * n : half * n + half])
        if linked:
            emit(4 + 2 * n, grad[:, 0:feat])
            emit(5 + 2 * n, grad[:, feat:])
        else:
            g1_ref[:, half * n : half * n + half] = grad
    if linked:
        job1 = grads_pair(1)

    grad = across(att[...], gml[...])
    if linked:
        emit(3, grad)
        arrive(job1)
        job1 = grads_plane(1)
    else:
        gp_ref[...] = grad

    def grad_attended(rows, _):
        att[rows, :] = against(gml[rows, :], wp_ref[...]).astype(BF16)

    each_block(grad_attended)

    def attend_back(h):
        part = pair_lanes(h)
        results = []
        for i in range(images):
            rows = image_rows(i)
            grad = stacked_halves(att[rows, part])
            share = probs[h, i].astype(F32)
            grad_share = against(grad, qkv[rows, head_part(h, 2)])
            inner = jnp.sum(share * grad_share, -1, keepdims=True)
            grad_score = (share * (grad_share - inner)).astype(BF16)
            key = qkv[rows, head_part(h, 1)]
            grad_query = (merged_halves(dot(grad_score, key)) * SCALE).astype(BF16)
            results.append((grad_score, grad_query))
        for i, (grad_score, _) in enumerate(results):
            dsc[i] = grad_score
        moved = []
        for i, (_, grad_query) in enumerate(results):
            rows = image_rows(i)
            query = stacked_halves(qkv[rows, head_part(h, 0)] * BF16(SCALE))
            grad = stacked_halves(att[rows, part])
            grad_key = across(dsc[i], query).astype(BF16)
            grad_value = across(probs[h, i], grad).astype(BF16)
            moved.append((grad_query, grad_key, grad_value))
        for n in range(3):
            for i in range(images):
                qkv[image_rows(i), head_part(h, n)] = moved[i][n]
            sums[n, :, part] = sum(fold(parts[n].astype(F32)) for parts in moved)

    def qkv_grad(first, last):
        cols = slice(feat * first, feat * last)
        grad = across(normed[...], qkv[:, cols])
        for h in range(first, last):
            part = grad[:, feat * (h - first) : feat * (h - first + 1)]
            if linked:
                emit(h, part)
            else:
                gq_ref[:, feat * h : feat * h + feat] = part

    def column_sums(out):
        out[...] = jnp.zeros(out.shape, F32)
        for n in range(ROW_FC1):
            out[n : n + 1, :] = jnp.sum(sums[n], 0, keepdims=True)
        for j in range(hidden_units):
            out[ROW_FC1 + j : ROW_FC1 + j + 1, :] = jnp.sum(
                sums1[:, feat * j : feat * j + feat], 0, keepdims=True
            )

    def sums_push(stage, kind):
        return push(kind, lambda r: (vsum.at[stage], vin.at[3 * stage + r - 1]))

    def late_push(stage, kind):
        return push(kind, lambda r: (late.at[stage], late_in.at[3 * stage + r - 1]))

    def sums_add(stage, count, own, came):
        total = own[stage]
        for r in range(count):
            total = total + came[3 * stage + r]
        own[stage + 1] = total

    def back_step(t, carry):
        attend_back(PAIRS - 1 - t)

        if t == 0:
            if linked:
                arrive(job0)
                tickets["job0"] = grads_layer(0)
            qkv_grad(2, 3)
            if linked:
                tickets["job2"] = grads_pair(2)

        if t == 1:
            if linked:
                arrive(job1)
                tickets["job1"] = grads_layer(1)
                arrive(tickets["job2"])
                tickets["job2"] = grads_plane(2)
                column_sums(vsum.at[0])
                tickets["vec"] = sums_push(0, "core")

        return carry

    for t in range(PAIRS):
        back_step(t, 0)
    if linked:
        arrive(tickets["vec"])
        sums_add(0, 1, vsum, vin)
        vec_go = sums_push(1, "plane")
        late[0] = jnp.zeros((8, 128), F32)
        for n in range(3):
            late[0, n : n + 1, :] = jnp.sum(sums[n, :, 0:128], 0, keepdims=True)
        late_go = late_push(0, "core")
    qkv_grad(0, 2)

    def contract(rows, block):
        total = dot(act[rows, :], w2_ref[...]) + row(7)
        for k, i in enumerate(block):
            outs[i] = (gins[i] + total[padded * k : padded * k + length]).astype(BF16)

    def input_back(rows, block):
        grads = against(qkv[rows, :], wq_ref[...])
        for k, i in enumerate(block):
            here = image_rows(i)
            unit, inverse = normalise(xs[here, :].astype(F32))
            back = norm_back(grads[padded * k : padded * k + padded], unit, inverse, row(0))
            gins[i] = (middle[here, :] + back)[:length]

    if linked:
        job3 = grads_pair(3)
        arrive(late_go)
        sums_add(0, 1, late, late_in)
        each_block(contract, 0, 1)
        arrive(job3)
        job3 = grads_plane(3)
        late_go = late_push(1, "plane")
        arrive(tickets["job2"])
        job2 = grads_layer(2)
        arrive(tickets["job0"])
        shares.append(grads_share(0))
        arrive(vec_go)
        sums_add(1, PLANE - 1, vsum, vin)
        vec_go = sums_push(2, "layer")
        each_block(contract, 1, blocks)
        out_copy.start()
        arrive(tickets["job1"])
        shares.append(grads_share(1))
        each_block(input_back, 0, 1)
        arrive(job3)
        job3 = grads_layer(3, both=True)
        arrive(late_go)
        sums_add(1, PLANE - 1, late, late_in)
        late_go = late_push(2, "layer")
        each_block(input_back, 1, blocks)
        gin_copy.start()
        arrive(job2)
        shares.append(grads_share(2))
        arrive(vec_go)
        sums_add(2, layers - 1, vsum, vin)
        arrive(late_go)
        sums_add(2, layers - 1, late, late_in)
        vsum[3, 0:3, 0:128] = late[3, 0:3, :]
        all_sent()
        arrive(job3)
        shares.append(grads_share(3, both=True))
        vsum_ref[...] = vsum[3]
        for copies in shares:
            arrive(copies)
        share_ref[...] = share_in[...]
    else:
        each_block(contract)
        out_copy.start()
        each_block(input_back)
        gin_copy.start()
        column_sums(vsum_ref)
    out_copy.wait()
    gin_copy.wait()


def layer_call(linked, dp, sources, tokens, cotangent, keep, *rest):
    images, length, feat = tokens.shape
    padded = -(-length // 16) * 16
    hidden = 4 * feat
    rows = images * padded
    vmem = pl.BlockSpec(memory_space=pltpu.VMEM)
    anywhere = pl.BlockSpec(memory_space=pl.ANY)
    smem = pl.BlockSpec(memory_space=pltpu.SMEM)
    shape = jax.ShapeDtypeStruct
    outs = [shape((images, length, feat), BF16), shape((images, length, feat), F32)]
    weights, links = [], []
    params = dict(vmem_limit_bytes=64 * 1024 * 1024)
    if linked:
        layers = dp // PLANE
        width = -(-sources // 128) * 128
        in_specs = [anywhere, anywhere, vmem, smem] + [vmem] * 5
        outs += [shape((UNITS, SHARD, feat), F32), shape((SUM_ROWS, feat), F32)]
        along, beside = layers - 1, PLANE - 1
        copies = 4 * (along + beside + 1) + (along + beside) + (along + beside + 1)
        copies += 4 * (1 + beside + along) + 3 + (along + 1) + 2 * (1 + beside + along)
        weights = [
            pltpu.VMEM((feat, PAIRS * feat), BF16),
            pltpu.VMEM((feat, feat), BF16),
            pltpu.VMEM((feat, hidden), BF16),
            pltpu.VMEM((hidden, feat), BF16),
            pltpu.VMEM((16, feat), F32),
        ]
        links = [
            pltpu.VMEM((UNITS, PLANE, layers, SHARD, feat), BF16),
            pltpu.VMEM((PLANE, layers, 16, 128), BF16),
            pltpu.VMEM((32, width), F32),
            pltpu.VMEM((9, 8, width), F32),
            pltpu.VMEM((UNITS // 2, PLANE, layers, SHARD, feat), BF16),
            pltpu.VMEM((beside, UNITS // 2, layers, SHARD, feat), BF16),
            pltpu.VMEM((UNITS // 2, layers, SHARD, feat), BF16),
            pltpu.VMEM((along, UNITS // 2, SHARD, feat), BF16),
            pltpu.VMEM((layers, SHARD, feat), BF16),
            pltpu.VMEM((4, SUM_ROWS, feat), F32),
            pltpu.VMEM((9, SUM_ROWS, feat), F32),
            pltpu.VMEM((4, 8, 128), F32),
            pltpu.VMEM((9, 8, 128), F32),
            pltpu.VMEM((UNITS, SHARD, feat), F32),
            pltpu.SemaphoreType.DMA((copies,)),
            pltpu.SemaphoreType.DMA((copies,)),
        ]
        params.update(collective_id=0, has_side_effects=True)
    else:
        in_specs = [anywhere, anywhere] + [vmem] * 7
        outs += [shape(w.shape, F32) for w in rest[1:5]] + [shape((SUM_ROWS, feat), F32)]
    return pl.pallas_call(
        functools.partial(layer_kernel, linked, dp, sources),
        out_shape=outs,
        in_specs=in_specs,
        out_specs=[anywhere, anywhere] + [vmem] * (len(outs) - 2),
        scratch_shapes=weights
        + links
        + [
            pltpu.VMEM((images, length, feat), BF16),
            pltpu.VMEM((rows, feat), BF16),
            pltpu.VMEM((rows, feat), BF16),
            pltpu.VMEM((rows, PAIRS * feat), BF16),
            pltpu.VMEM((PAIRS, images, 2 * padded, padded), BF16),
            pltpu.VMEM((rows, feat), BF16),
            pltpu.VMEM((rows, feat), F32),
            pltpu.VMEM((rows, feat), BF16),
            pltpu.VMEM((rows, hidden), BF16),
            pltpu.VMEM((rows, hidden), BF16),
            pltpu.VMEM((rows, feat), BF16),
            pltpu.VMEM((rows, feat), BF16),
            pltpu.VMEM((images, 2 * padded, padded), BF16),
            pltpu.VMEM((8, 8, feat), F32),
            pltpu.VMEM((8, hidden), F32),
            pltpu.VMEM((8, hidden), F32),
            pltpu.VMEM((images, length, feat), BF16),
            pltpu.VMEM((images, length, feat), F32),
            pltpu.VMEM((16, 256), F32),
            pltpu.VMEM((16, 256), F32),
            pltpu.SemaphoreType.DMA((4,)),
        ],
        compiler_params=pltpu.CompilerParams(**params),
        name="layer",
    )(tokens, cotangent, keep, *rest)


def adamw(master, first, second, gradient, step_rate, weight_decay):
    first_new = 0.9 * first + 0.1 * gradient
    second_new = 0.999 * second + 0.001 * gradient * gradient
    step_size = first_new / (1.0 - 0.9**STEP) / (jnp.sqrt(second_new / (1.0 - 0.999**STEP)) + 1e-08)
    return (first_new, second_new, master - step_rate * (step_size + weight_decay * master))


def norm_grads(products, weighted, gain, bias):
    return (products - bias * weighted) / gain, weighted


def step_kernel(*refs):
    refs = list(refs)

    def take(count):
        taken = refs[:count]
        del refs[:count]
        return taken

    large_in, small_in, large_out, state_out = take(2), take(17), take(2), take(15)
    large, small, outs = take(2), take(17), take(15)
    came, went, small_came, small_went = take(4)
    share_ref, vsum_ref, *state = small
    feat = share_ref.shape[2]
    images = large[0].shape[0]
    parts = came.shape[1]
    size = images // parts

    def moves(sources, targets, sems):
        return [
            pltpu.make_async_copy(
                sources[n].at[pl.ds(size * i, size)], targets[n].at[pl.ds(size * i, size)], sems.at[n, i]
            )
            for i in range(parts)
            for n in range(2)
        ]

    def copies(sources, targets, sems):
        return [
            pltpu.make_async_copy(src, dst, sems.at[n])
            for n, (src, dst) in enumerate(zip(sources, targets))
        ]

    arrivals, departures = moves(large_in, large, came), moves(large, large_out, went)
    small_arrivals = copies(small_in, small, small_came)
    small_departures = copies(outs, state_out, small_went)

    def fetch(n):
        return [small_arrivals[2 + 5 * k + n] for k in range(3)]

    order = [small_arrivals[0], *fetch(0), *fetch(2), *fetch(3)]
    order += [small_arrivals[1], *fetch(1), *fetch(4)]
    for move in arrivals[:2] + order[:4] + arrivals[2:] + order[4:]:
        move.start()

    def ready(n):
        for move in fetch(n):
            move.wait()

    def store(n):
        for k in range(3):
            small_departures[3 * n + k].start()

    def pass_on(count):
        for _ in range(count):
            arrivals[0].wait()
            departures[0].start()
            del arrivals[0]
            left.append(departures.pop(0))

    left = []

    def update(n, here, gradient):
        new = adamw(
            state[n][here], state[5 + n][here], state[10 + n][here], gradient, step_rates[n], decays[n]
        )
        for k in range(3):
            outs[3 * n + k][here] = new[k]

    def low(values):
        return values.astype(BF16).astype(F32)

    everything = slice(None)
    small_arrivals[0].wait()
    small_arrivals[1].wait()
    first_products = jnp.zeros((SHARD, 128), F32)
    first_weighted = jnp.zeros((SHARD, 128), F32)
    pass_on(2)
    ready(0)
    for u in range(PAIRS):
        for n in range(3):
            first = n * feat + 128 * u
            cols = slice(first, first + 128)
            grad = share_ref[u, :, 128 * n : 128 * n + 128]
            weight = low(state[0][:, cols])
            first_products += grad * weight
            first_weighted += weight * vsum_ref[n : n + 1, 128 * u : 128 * u + 128]
            update(0, (everything, cols), grad)
    store(0)
    pass_on(2)
    second_products = jnp.zeros((SHARD, feat), F32)
    second_weighted = jnp.zeros((SHARD, feat), F32)
    ready(2)
    for j in range(4):
        cols = slice(feat * j, feat * j + feat)
        weight = low(state[2][:, cols])
        second_products += share_ref[4 + j] * weight
        second_weighted += weight * vsum_ref[ROW_FC1 + j : ROW_FC1 + j + 1, :]
        update(2, (everything, cols), share_ref[4 + j])
    store(2)
    pass_on(2)
    ready(3)
    for j in range(4):
        update(3, (slice(SHARD * j, SHARD * j + SHARD), everything), share_ref[8 + j])
    store(3)
    ready(1)
    update(1, (everything, everything), share_ref[3])
    store(1)
    ready(4)
    pass_on(len(arrivals))

    me = lax.axis_index("dp")
    sums = vsum_ref[...]
    lanes = lax.broadcasted_iota(jnp.int32, (SUM_ROWS, 128), 1)
    mine = jnp.zeros((SUM_ROWS, 128), F32)
    for owner in range(16):
        shift = (SHARD * owner) % 128
        block = SHARD * owner // 128
        part = sums[:, 128 * block : 128 * block + 128]
        part = pltpu.roll(part, 128 - shift, 1) if shift else part
        if shift + SHARD > 128:
            rest = pltpu.roll(sums[:, 128 * block + 128 : 128 * block + 256], 128 - shift, 1)
            part = jnp.where(lanes < 128 - shift, part, rest)
        mine = jnp.where(me == owner, part, mine)
    mine = mine[:, 0:SHARD]
    eye = lax.broadcasted_iota(jnp.int32, (SHARD, SHARD), 0) == lax.broadcasted_iota(
        jnp.int32, (SHARD, SHARD), 1
    )

    def as_row(values):
        column = jnp.sum(values, 1, keepdims=True)
        return jnp.sum(jnp.where(eye, column, 0.0), 0, keepdims=True)

    vec = low(state[4][...])
    gain_first, shift_first = norm_grads(
        as_row(first_products), as_row(first_weighted), vec[0:1], vec[1:2]
    )
    gain_second, shift_second = norm_grads(
        as_row(second_products), as_row(second_weighted), vec[5:6], vec[6:7]
    )
    grads = [gain_first, shift_first, mine[0:1], mine[2:3], mine[ROW_PROJ : ROW_PROJ + 1]]
    grads += [gain_second, shift_second, mine[ROW_FC2 : ROW_FC2 + 1]]
    grads += [mine[ROW_FC1 + j : ROW_FC1 + j + 1] for j in range(4)]
    for n, grad in enumerate(grads):
        update(4, (slice(n, n + 1), everything), grad)
    store(4)
    for move in left + small_departures:
        move.wait()


def step_call(layer_out, input_grad, share, vsum, states):
    anywhere = pl.BlockSpec(memory_space=pl.ANY)
    shape = jax.ShapeDtypeStruct
    large = [shape(a.shape, a.dtype) for a in (layer_out, input_grad)]
    new = [shape(states[n].shape, F32) for n in range(5) for _ in range(3)]
    operands = (layer_out, input_grad, share, vsum, *states)
    parts = 3 if layer_out.shape[0] % 3 == 0 else 1
    dma = pltpu.SemaphoreType.DMA
    return pl.pallas_call(
        step_kernel,
        out_shape=large + new,
        in_specs=[anywhere] * len(operands),
        out_specs=[anywhere] * 17,
        scratch_shapes=[pltpu.VMEM(a.shape, a.dtype) for a in (*operands, *new)]
        + [dma((2, parts)), dma((2, parts)), dma((17,)), dma((15,))],
        compiler_params=pltpu.CompilerParams(vmem_limit_bytes=64 * 1024 * 1024),
        name="step",
    )(*operands)


def by_pair(weight):
    rows, cols = weight.shape
    return weight.reshape(rows, 3, PAIRS, 128).transpose(0, 2, 1, 3).reshape(rows, cols)


def from_pairs(grad):
    rows, cols = grad.shape
    return grad.reshape(rows, PAIRS, 3, 128).transpose(0, 2, 1, 3).reshape(rows, cols)


def on_device(tokens, cotangent, keep_mask, source, *states):
    masters = states[:5]
    dp = lax.axis_size("dp")
    images, length, feat = tokens.shape
    sources = images * lax.axis_size("head") * dp // 3
    if dp == 16:
        layer_out, input_grad, share, vsum = layer_call(
            True, dp, sources, tokens, cotangent, keep_mask, source, *masters
        )
        return tuple(step_call(layer_out, input_grad, share, vsum, states))
    gather = functools.partial(lax.all_gather, axis_name="dp", tiled=True)
    low = [master.astype(BF16) for master in masters]
    w_qkv, w_proj, w_fc1, w_fc2 = (gather(w, axis=0) for w in low[:4])
    vectors = gather(low[4], axis=1).astype(F32)
    live_mask = keep_mask.astype(F32)
    kept_rows = jnp.sum(live_mask, 1)
    onehot = (source[:, None] == jnp.arange(sources, dtype=jnp.int32)[None, :]).astype(F32)
    totals = lax.psum(jnp.sum(onehot * kept_rows[:, None], 0), ("dp", "head"))
    image_total = jnp.sum(onehot * totals[None, :], 1)
    token_weight = live_mask * (length / image_total)[:, None]
    layer_out, input_grad, gq, gp, g1, g2, vsum = layer_call(
        False, dp, sources, tokens, cotangent, keep_mask,
        token_weight, by_pair(w_qkv), w_proj, w_fc1, w_fc2, vectors,
    )
    shares = [
        lax.psum_scatter(
            lax.psum(g.astype(BF16), "head").astype(F32), "dp", scatter_dimension=0, tiled=True
        )
        for g in (from_pairs(gq), gp, g1, g2)
    ]
    vsum = lax.psum(vsum, ("dp", "head"))
    low = [w.astype(F32) for w in low]
    own = masters[4].shape[1]
    mine = lax.dynamic_slice_in_dim(vsum, lax.axis_index("dp") * own, own, 1)
    norms = []
    for share, weight, behind, n in (
        (shares[0], low[0], vsum[:3], 0),
        (shares[2], low[2], vsum[ROW_FC1 : ROW_FC1 + 4], 5),
    ):
        products = jnp.sum(share * weight, 1)
        weighted = jnp.sum(weight * behind.reshape(1, -1), 1)
        norms.append(norm_grads(products, weighted, low[4][n], low[4][n + 1]))
    rows = [*norms[0], mine[0], mine[2], mine[ROW_PROJ], *norms[1], mine[ROW_FC2]]
    shares.append(jnp.stack(rows + [mine[ROW_FC1 + j] for j in range(4)]))
    new = []
    for n in range(5):
        new.extend(
            adamw(masters[n], states[5 + n], states[10 + n], shares[n], step_rates[n], decays[n])
        )
    return (layer_out, input_grad, *new)


def solution(mesh):
    split = P(("dp", "head"), None, None)
    rows, cols = P("dp", None), P(None, "dp")
    weights = (rows, rows, rows, rows, cols)
    return jax.shard_map(
        on_device,
        mesh=mesh,
        in_specs=(split, split, P(("dp", "head"), None), P(("dp", "head"))) + weights * 3,
        out_specs=(split, split) + (rows,) * 12 + (cols,) * 3,
        check_vma=False,
    )
```
